32 devices in a mesh: expert: 4 (over y, core), ctx: 4 (over z), dp: 2 (over x).
Axes of the slice: x: 2, y: 2, z: 4, core: 2. Of those that a mesh axis runs over, the one named last changes fastest.
Arguments:
- layer_input: bfloat16 [8, 2048, 768], P(('expert', 'dp'), 'ctx'), may hold values from -6 to 6
- cotangent: bfloat16 [8, 2048, 768], P(('expert', 'dp'), 'ctx'), may hold values from -6 to 6
- norm_gain_one: float32 [768], replicated, may hold values from 0.5 to 1.5
- w_query: bfloat16 [768, 768], replicated, may hold values from -0.21875 to 0.21875
- w_key: bfloat16 [768, 768], replicated, may hold values from -0.21875 to 0.21875
- w_value: bfloat16 [768, 768], replicated, may hold values from -0.21875 to 0.21875
- w_output: bfloat16 [768, 768], replicated, may hold values from -0.875 to 0.875
- rel_table: bfloat16 [12, 32], replicated, may hold values from -4 to 4
- norm_gain_two: float32 [768], replicated, may hold values from 0.5 to 1.5
- w_router: bfloat16 [768, 4], replicated, may hold values from -0.1796875 to 0.1796875
- w_expert_in: bfloat16 [4, 768, 3072], P('expert', ('ctx', 'dp')), may hold values from -0.21875 to 0.21875
- w_expert_out: bfloat16 [4, 3072, 768], P('expert', ('ctx', 'dp')), may hold values from -0.21875 to 0.21875
- segment_ids: int32 [8, 2048], P(('expert', 'dp'), 'ctx'), may hold values from 0 to 8, as said below
- routes: int32 [8, 2048, 2], P(('expert', 'dp'), 'ctx'), may hold values from 0 to 3, all different within a row
- priority: int32 [8, 4, 512], P(('expert', 'dp'), 'ctx'), may hold values from 0 to 511, each once within a row
Outputs:
- layer_output: bfloat16 [8, 2048, 768], P(('expert', 'dp'), 'ctx')
- grad_input: float32 [8, 2048, 768], P(('expert', 'dp'), 'ctx')
- grad_norm_one: float32 [768], replicated
- grad_query: float32 [768, 768], replicated
- grad_key: float32 [768, 768], replicated
- grad_value: float32 [768, 768], replicated
- grad_projection: float32 [768, 768], replicated
- grad_table: float32 [12, 32], replicated
- grad_norm_two: float32 [768], replicated
- grad_router: float32 [768, 4], replicated
- grad_expert_in: float32 [4, 768, 3072], P('expert', ('ctx', 'dp'))
- grad_expert_out: float32 [4, 3072, 768], P('expert', ('ctx', 'dp'))
The draws below stay inside these ranges and needn't reach their ends.
Inputs may be any that keep to these rules, and one draw needn't show every extreme that they name: `segment_ids`: along each sequence the numbers never fall and each sequence ends with the number 8; in one sequence a single document runs from within its first 512 tokens to its end. `routes`: the two experts of a token differ. `priority`: within each block of 512 tokens the priorities are a permutation.
All inputs are finite; a program needn't handle non-finite values.
Results may differ from the reference program's by a relative error of at most 0.014.
Values may be sent and summed in bfloat16 or wider, within the bound.
A program may use at most 192 MiB of HBM per device.

```python
from functools import partial
import jax
import jax.numpy as jnp
from jax import lax

WIDTH = 768
HEADS = 12
HEAD_DIM = 64
HIDDEN_SIZE = 3072
BUCKETS = 32
SHARD_LEN = 512
LENGTH = 2048
SEQUENCES = 8
EXPERTS = 4
CAPACITY = 320
N_CTX = 4


def draw_segment_ids(key, part):
    key = jax.random.fold_in(key, 7)
    key_shift, key_bound, key_pick = jax.random.split(key, 3)
    shifts = jax.random.randint(key_shift, (SEQUENCES, 8), 0, 7)
    bounds = jax.random.randint(key_bound, (SEQUENCES, 8), 1, LENGTH)
    bounds = jnp.right_shift(bounds, shifts)
    picked = jax.random.randint(key_pick, (), 0, SEQUENCES)
    early = bounds % SHARD_LEN
    sequence_rows = jnp.arange(SEQUENCES)[:, None]
    bounds = jnp.where(sequence_rows == picked, early, bounds)
    positions = jnp.arange(LENGTH)
    numbers = jnp.sum((positions[None, :, None] >= bounds[:, None, :]).astype(jnp.int32), axis=2)
    return numbers.astype(jnp.int32)


def levels(own_key, shape, pieces, smallest, high):
    loudness, own = 1.0, jax.random.fold_in(own_key, 6)
    for axis_at, parts in pieces:
        steps = jnp.exp(jax.random.uniform(jax.random.fold_in(own, axis_at), (parts,), jnp.float32, smallest / len(pieces), high / len(pieces)))
        loudness = loudness * jnp.repeat(steps, shape[axis_at] // parts).reshape([-1 if axis == axis_at else 1 for axis in range(len(shape))])
    return loudness


def distinct(own_key, rows, count, top, lift):
    sequence = jax.random.permutation(jax.random.fold_in(own_key, 1), count)
    pull = sequence
    for power in range(3):
        pull = pull * pull // count
    pull = pull * lift // count
    chance = jax.random.randint(jax.random.fold_in(own_key, 2), (rows, count), 0, 4096) + pull
    sure = jax.random.permutation(jax.random.fold_in(own_key, 3), rows)[jnp.arange(count) % rows]
    chance = jnp.where(jnp.arange(rows)[:, None] == sure[None, :], 1 << 14, chance)
    score = chance * count + jnp.arange(count)
    return lax.top_k(score.astype(jnp.int32), top)[1].astype(jnp.int32)


def noise(own_key, dims, spread, most, shards=(), held_as=jnp.bfloat16):
    array = spread * jax.random.normal(own_key, dims, jnp.float32)
    if shards:
        array = array * levels(own_key, dims, shards, -0.22, 0.18)
    return jnp.clip(array, -most, most).astype(held_as)


def setup_inputs(seed: int = 0) -> dict:
    seeds = jax.random.split(jax.random.key(seed), 16)
    layer_input = noise(seeds[0], (SEQUENCES, LENGTH, WIDTH), 1.0, 6.0, ((0, 8), (1, 4)))
    cotangent = noise(seeds[1], (SEQUENCES, LENGTH, WIDTH), 1.0, 6.0, ((0, 8), (1, 4)))
    norm_gain_one = jnp.clip(1.0 + 0.1 * jax.random.normal(seeds[2], (WIDTH,), jnp.float32), 0.5, 1.5)
    w_query = noise(seeds[3], (WIDTH, WIDTH), WIDTH ** -0.5, 0.21875)
    w_key = noise(seeds[4], (WIDTH, WIDTH), WIDTH ** -0.5, 0.21875)
    w_value = noise(seeds[5], (WIDTH, WIDTH), WIDTH ** -0.5, 0.21875)
    w_output = noise(seeds[6], (WIDTH, WIDTH), (WIDTH // 16) ** -0.5, 0.875)
    rel_table = noise(seeds[7], (HEADS, BUCKETS), 1.0, 4.0)
    norm_gain_two = jnp.clip(1.0 + 0.1 * jax.random.normal(seeds[8], (WIDTH,), jnp.float32), 0.5, 1.5)
    w_router = noise(seeds[9], (WIDTH, EXPERTS), 0.03, 0.1796875)
    w_expert_in = noise(seeds[10], (EXPERTS, WIDTH, HIDDEN_SIZE), WIDTH ** -0.5, 0.21875, ((0, 4), (1, 8)))
    w_expert_out = noise(seeds[11], (EXPERTS, HIDDEN_SIZE, WIDTH), (HIDDEN_SIZE // 4) ** -0.5, 0.21875, ((0, 4), (1, 8)))
    segment_ids = draw_segment_ids(jax.random.fold_in(seeds[15], 71), 0)
    routes = distinct(seeds[13], SEQUENCES * LENGTH, EXPERTS, 2, 4096).reshape((SEQUENCES, LENGTH, 2))
    priority = jax.vmap(lambda own: jax.random.permutation(own, SHARD_LEN))(jax.random.split(seeds[14], SEQUENCES * N_CTX)).reshape((SEQUENCES, N_CTX, SHARD_LEN)).astype(jnp.int32)
    return dict(layer_input=layer_input, cotangent=cotangent, norm_gain_one=norm_gain_one, w_query=w_query, w_key=w_key, w_value=w_value, w_output=w_output, rel_table=rel_table, norm_gain_two=norm_gain_two, w_router=w_router, w_expert_in=w_expert_in, w_expert_out=w_expert_out, segment_ids=segment_ids, routes=routes, priority=priority)


HIGH_PRECISION = lax.Precision.HIGHEST
EPSILON = 1e-06
NEGATIVE = -1e+30
THRESHOLDS = (19, 21, 24, 27, 31, 35, 40, 46, 52, 59, 67, 77, 87, 99, 113)

@jax.custom_vjp
def lowered_input(v):
    return lax.optimization_barrier(v.astype(jnp.bfloat16)).astype(jnp.float32)

@jax.custom_vjp
def lowered_backward(v):
    return v

def low_keep(v):
    return (lowered_input(v), None)

def low_pass(kept, grad):
    return (grad,)

def back_keep(v):
    return (v, None)

def back_low(kept, grad):
    return (lowered_input(grad),)
lowered_input.defvjp(low_keep, low_pass)
lowered_backward.defvjp(back_keep, back_low)

def rms_norm(values, gain):
    return values * lax.rsqrt(lax.optimization_barrier(jnp.mean(values * values, axis=-1, keepdims=True)) + EPSILON) * gain

def buckets(distance):
    far = 16 + sum(((distance >= limit).astype(jnp.int32) for limit in THRESHOLDS))
    return jnp.where(distance < 16, jnp.maximum(distance, 0), far).astype(jnp.int32)

def slot_tables(chosen, order, capacity, experts):
    count = chosen.shape[0]
    ranks = jnp.stack([order, order + count], axis=1).reshape(-1)
    flat = chosen.reshape(-1)
    same = flat[:, None] == flat[None, :]
    before = ranks[None, :] < ranks[:, None]
    slots = lax.optimization_barrier(jnp.sum((same & before).astype(jnp.int32), axis=1))
    targets = jnp.where(slots < capacity, flat * capacity + slots, experts * capacity).astype(jnp.int32)
    pair_sources = jnp.full((experts * capacity + 1,), 2 * count, jnp.int32)
    pair_sources = pair_sources.at[targets].set(jnp.arange(2 * count, dtype=jnp.int32))
    return (targets, pair_sources[:experts * capacity])

def attend(queries, keys, values, segments, table):
    length = queries.shape[0]
    block = min(length, 512)
    positions = jnp.arange(length, dtype=jnp.int32)

    def one_block(start):
        rows = lax.dynamic_slice_in_dim(queries, start, block, 0)
        places = start + jnp.arange(block, dtype=jnp.int32)
        row_segments = lax.dynamic_slice_in_dim(segments, start, block, 0)
        raw = jnp.einsum('qhd,khd->hqk', rows, keys, precision=HIGH_PRECISION)
        scores = lowered_backward(raw) * 0.125 + table[:, buckets(places[:, None] - positions[None, :])]
        allowed = (positions[None, :] <= places[:, None]) & (row_segments[:, None] == segments[None, :])
        weights = jax.nn.softmax(jnp.where(allowed[None], scores, NEGATIVE), axis=-1)
        return jnp.einsum('hqk,khd->qhd', lowered_input(weights), values, precision=HIGH_PRECISION)
    starts = jnp.arange(length // block, dtype=jnp.int32) * block
    outcome = lax.map(jax.checkpoint(one_block), starts)
    return outcome.reshape(length, queries.shape[1], queries.shape[2])

def expert_apply(items):
    rows, inner, outer = items
    pre = lowered_backward(jnp.einsum('bcd,df->bcf', rows, inner, precision=HIGH_PRECISION))
    activated = lowered_input(jax.nn.gelu(pre))
    return lowered_backward(lowered_input(jnp.einsum('bcf,fd->bcd', activated, outer, precision=HIGH_PRECISION)))

def reference(layer_input, cotangent, norm_gain_one, w_query, w_key, w_value, w_output, rel_table, norm_gain_two, w_router, w_expert_in, w_expert_out, segment_ids, routes, priority):
    seqs, length, width = layer_input.shape
    block_total = seqs * N_CTX
    route_blocks = routes.reshape(block_total, SHARD_LEN, 2)
    order_blocks = priority.reshape(block_total, SHARD_LEN)
    targets, pair_sources = jax.vmap(partial(slot_tables, capacity=CAPACITY, experts=EXPERTS))(route_blocks, order_blocks)
    token_sources = pair_sources // 2

    def forward(inputs, gain_one, query_w, key_w, value_w, output_weight, table, gain_two, router_weight, inner_w, outer_w):
        normed_input = lowered_input(rms_norm(inputs, gain_one))

        def project(weight_matrix):
            return lowered_backward(lowered_input(jnp.einsum('pkb,bc->pkc', normed_input, weight_matrix, precision=HIGH_PRECISION)))
        queries = project(query_w).reshape(seqs, length, HEADS, HEAD_DIM)
        keys = project(key_w).reshape(seqs, length, HEADS, HEAD_DIM)
        values = project(value_w).reshape(seqs, length, HEADS, HEAD_DIM)
        attended = lax.map(lambda items: attend(items[0], items[1], items[2], items[3], table), (queries, keys, values, segment_ids))
        mixed_output = lowered_backward(lowered_input(attended.reshape(seqs, length, width)))
        branch_output = lowered_backward(jnp.einsum('pkb,bc->pkc', mixed_output, output_weight, precision=HIGH_PRECISION))
        hidden = inputs + branch_output
        second_normed = lowered_input(rms_norm(hidden, gain_two))
        router_logits = jnp.einsum('pkb,bc->pkc', second_normed, router_weight, precision=HIGH_PRECISION)
        chances = jax.nn.softmax(router_logits, axis=-1)
        picked = jnp.take_along_axis(chances, routes, axis=-1)
        gates = picked / lax.optimization_barrier(jnp.sum(picked, axis=-1, keepdims=True))
        token_rows = second_normed.reshape(block_total, SHARD_LEN, width)
        token_rows = jnp.concatenate([token_rows, jnp.zeros((block_total, 1, width), jnp.float32)], axis=1)
        dispatched = jax.vmap(lambda table_rows, index: table_rows[index])(token_rows, token_sources)
        dispatched = lowered_backward(dispatched.reshape(block_total, EXPERTS, CAPACITY, width).transpose(1, 0, 2, 3))
        produced = lax.map(jax.checkpoint(expert_apply), (dispatched, inner_w, outer_w))
        produced = produced.transpose(1, 0, 2, 3).reshape(block_total, EXPERTS * CAPACITY, width)
        produced = jnp.concatenate([produced, jnp.zeros((block_total, 1, width), jnp.float32)], axis=1)
        paired = jax.vmap(lambda table_rows, index: table_rows[index])(produced, targets)
        paired = paired.reshape(seqs, length, 2, width)
        mixture = lax.optimization_barrier(jnp.sum(gates[..., None] * paired, axis=2))
        return hidden + mixture
    primals = (layer_input.astype(jnp.float32), norm_gain_one.astype(jnp.float32), w_query.astype(jnp.float32), w_key.astype(jnp.float32), w_value.astype(jnp.float32), w_output.astype(jnp.float32), rel_table.astype(jnp.float32), norm_gain_two.astype(jnp.float32), w_router.astype(jnp.float32), w_expert_in.astype(jnp.float32), w_expert_out.astype(jnp.float32))
    result, pullback = jax.vjp(forward, *primals)
    grads = pullback(cotangent.astype(jnp.float32))
    return (result.astype(jnp.bfloat16), grads[0], grads[1], grads[2], grads[3], grads[4], grads[5], grads[6], grads[7], grads[8], grads[9], grads[10])
```

```python
import functools
from functools import partial

import jax
import jax.numpy as jnp
from jax import lax
from jax.experimental import pallas as pl
from jax.experimental.pallas import tpu as pltpu
from jax.sharding import PartitionSpec as P

bf16 = jnp.bfloat16
f32 = jnp.float32
HIGH_PRECISION = lax.Precision.HIGHEST
EPSILON = 1e-06
THRESHOLDS = (19, 21, 24, 27, 31, 35, 40, 46, 52, 59, 67, 77, 87, 99, 113)
BUCKETS=32
NEG=-1e30
BLK=256
NT=(((1,),(1,)),((),()))
TN=(((0,),(0,)),((),()))

def dot(a,b,dims=(((1,),(0,)),((),()))):
    return lax.dot_general(a,b,dims,preferred_element_type=f32)

def seg_mask_rows(seg):
    which = lax.broadcasted_iota(jnp.int32, seg.shape, 0).astype(f32)
    same = seg.astype(f32) == which
    return jnp.where(same, 0.0, NEG).astype(bf16), jnp.where(same, 1.0, 0.0).astype(bf16)

def attn_fwd_kernel(heads, n, rows, x_ref, f_ref, o_ref, of_ref, lse_ref, qa, ka, vn, bias, s_ref):
    size = 64
    group = heads*size
    length = n*rows
    def head(h, carry):
        base = pl.multiple_of(h*size, size)
        for s in range(n):
            at = slice(s*rows, (s+1)*rows)
            q = x_ref[s, pl.ds(base, size), :]
            k = x_ref[s, pl.ds(base+group, size), :]
            v = x_ref[s, pl.ds(base+2*group, size), :]
            seg = x_ref[s, 3*group:3*group+16, :]
            mask, hot = seg_mask_rows(seg)
            zeros = jnp.zeros((48, rows), bf16)
            qt = jnp.concatenate([q*jnp.asarray(0.125,bf16), mask, zeros], axis=0)
            qa[at, :] = qt.T
            ka[:, at] = jnp.concatenate([k, hot, zeros], axis=0)
            vn[at, :] = jnp.concatenate([v, jnp.zeros((64,rows),bf16)], axis=0).T
        line = jnp.broadcast_to(f_ref[pl.ds(h,1), :], (BLK, 2*BLK))
        rolled = pltpu.roll(line, 0, 1, stride=1, stride_axis=0)
        r = lax.broadcasted_iota(jnp.int32, (BLK,2*BLK), 0)
        c = lax.broadcasted_iota(jnp.int32, (BLK,2*BLK), 1)
        bias[...] = jnp.where(c - r > BLK, NEG, rolled)
        for t in range(length//BLK):
            qt = qa[t*BLK:(t+1)*BLK, :]
            near0 = max(t-1,0)*BLK
            end = (t+1)*BLK
            chunks = [(near0, end)] + [(a, min(a+2*BLK, near0)) for a in range(0, near0, 2*BLK)]
            top = None
            for (a,b) in chunks:
                s = dot(qt, ka[:, a:b])
                if a == near0:
                    s = s + bias[:, 2*BLK-(b-a):]
                s_ref[:, a:b] = s
                part = s[:, :128]
                for i in range(1,(b-a)//128):
                    part = jnp.maximum(part, s[:, i*128:(i+1)*128])
                top = part if top is None else jnp.maximum(top, part)
            m = jnp.max(top, axis=1, keepdims=True)
            total = None; o = None
            for (a,b) in chunks:
                p = jnp.exp(s_ref[:, a:b] - m)
                part = p[:, :128]
                for i in range(1,(b-a)//128):
                    part = part + p[:, i*128:(i+1)*128]
                total = part if total is None else total + part
                u = dot(p.astype(bf16), vn[a:b, :])
                o = u if o is None else o + u
            l = jnp.sum(total, axis=1, keepdims=True)
            o = o / l
            lane = lax.broadcasted_iota(jnp.int32, (BLK,128), 1)
            o = jnp.where(lane == 64, m + jnp.log(l), o)
            ot = o.T
            src, off = (t*BLK)//rows, (t*BLK)%rows
            o_ref[src, pl.ds(base,size), off:off+BLK] = ot[:size].astype(bf16)
            of_ref[pl.ds(base,size), t*BLK:(t+1)*BLK] = ot[:size]
            lse_ref[pl.ds(h,1), t*BLK:(t+1)*BLK] = ot[size:size+1]
        return carry
    lax.fori_loop(0, heads, head, 0)

def attn_fwd(x, f):
    n, depth, rows = x.shape
    heads = f.shape[0]
    length = n*rows
    return pl.pallas_call(functools.partial(attn_fwd_kernel, heads, n, rows),
        out_shape=[jax.ShapeDtypeStruct((n, heads*64, rows), bf16), jax.ShapeDtypeStruct((heads*64,length), f32), jax.ShapeDtypeStruct((heads,length), f32)],
        in_specs=[pl.BlockSpec(memory_space=pltpu.VMEM)]*2,
        out_specs=[pl.BlockSpec(memory_space=pltpu.VMEM)]*3,
        scratch_shapes=[pltpu.VMEM((length,128),bf16), pltpu.VMEM((128,length),bf16), pltpu.VMEM((length,128),bf16), pltpu.VMEM((BLK,2*BLK),f32), pltpu.VMEM((BLK,length),f32)],
        compiler_params=pltpu.CompilerParams(vmem_limit_bytes=48*1024*1024),
        name="attention_forward",
    )(x, f)

def split3(v):
    hi = v.astype(bf16); rest = v - hi.astype(f32)
    mid = rest.astype(bf16); rest = rest - mid.astype(f32)
    return hi, mid, rest.astype(bf16)

def attn_bwd_kernel(heads, n, rows, x_ref, do_ref, f_ref, of_ref, lse_ref, g_ref, diag_ref, qa, ka, va, da, qn, dn, bias, dq, gsum):
    size = 64
    group = heads*size
    length = n*rows
    def head(h, carry):
        base = pl.multiple_of(h*size, size)
        for s in range(n):
            at = slice(s*rows, (s+1)*rows)
            q = x_ref[s, pl.ds(base, size), :] * jnp.asarray(0.125,bf16)
            k = x_ref[s, pl.ds(base+group, size), :]
            v = x_ref[s, pl.ds(base+2*group, size), :]
            d = do_ref[s, pl.ds(base, size), :]
            seg = x_ref[s, 3*group:3*group+16, :]
            mask, hot = seg_mask_rows(seg)
            which = lax.broadcasted_iota(jnp.int32, (16, rows), 0)
            def rows3(vec):
                hi, mid, lo = split3(jnp.broadcast_to(vec, (16,rows)))
                return jnp.where(which==0, hi, jnp.where(which==1, mid, jnp.where(which==2, lo, jnp.zeros((),bf16))))
            ones = jnp.where(which<3, 1.0, 0.0).astype(bf16)
            zeros = jnp.zeros((32, rows), bf16)
            zeros48 = jnp.zeros((48, rows), bf16)
            lse = lse_ref[pl.ds(h,1), at]
            delta = jnp.sum(of_ref[pl.ds(base,size), at]*d.astype(f32), axis=0, keepdims=True)
            qt = jnp.concatenate([q, mask, rows3(-lse), zeros], axis=0)
            qa[:, at] = qt
            qn[at, :] = qt.T
            ka[at, :] = jnp.concatenate([k, hot, ones, zeros], axis=0).T
            dt = jnp.concatenate([d, rows3(-delta), zeros48], axis=0)
            da[:, at] = dt
            dn[at, :] = dt.T
            va[at, :] = jnp.concatenate([v, ones, zeros48], axis=0).T
        line = jnp.broadcast_to(f_ref[pl.ds(h,1), :], (BLK, 2*BLK))
        rolled = pltpu.roll(line, 0, 1, stride=1, stride_axis=0)
        r = lax.broadcasted_iota(jnp.int32, (BLK,2*BLK), 0)
        c = lax.broadcasted_iota(jnp.int32, (BLK,2*BLK), 1)
        bias[...] = jnp.where(c < r, NEG, rolled)
        gsum[...] = jnp.zeros_like(gsum)
        for j in range(length//BLK):
            a0 = j*BLK
            kj = ka[a0:a0+BLK, :]
            vj = va[a0:a0+BLK, :]
            src, off = a0//rows, a0%rows
            kt = x_ref[src, pl.ds(base+group, size), off:off+BLK]
            dk = dv = None
            for a in range(a0, length, 2*BLK):
                b = min(a+2*BLK, length)
                s = dot(kj, qa[:, a:b])
                if a == a0:
                    s = s + bias[:, :b-a]
                p = jnp.exp(s)
                ds = p * dot(vj, da[:, a:b])
                if a == a0:
                    gsum[:, :b-a] += ds
                pl_, dl = p.astype(bf16), ds.astype(bf16)
                u = dot(pl_, dn[a:b, :]); dv = u if dv is None else dv+u
                u = dot(dl, qn[a:b, :]); dk = u if dk is None else dk+u
                u = dot(kt, dl)
                if j == 0:
                    dq[:, a:b] = u
                else:
                    dq[:, a:b] += u
            g_ref[src, pl.ds(base+group,size), off:off+BLK] = dk.T[:size].astype(bf16)
            g_ref[src, pl.ds(base+2*group,size), off:off+BLK] = dv.T[:size].astype(bf16)
        for s in range(n):
            g_ref[s, pl.ds(base,size), :] = (dq[:, s*rows:(s+1)*rows]*0.125).astype(bf16)
        eight = gsum[0:8, :]
        for i in range(1, BLK//8):
            eight = eight + pltpu.roll(gsum[8*i:8*i+8, :], 2*BLK-8*i, 1)
        line = eight[0:1]
        for i in range(1, 8):
            line = line + pltpu.roll(eight, 2*BLK-i, 1)[i:i+1]
        diag_ref[pl.ds(h,1), :] = line
        return carry
    lax.fori_loop(0, heads, head, 0)

def attn_bwd(x, do, f, of, lse):
    n, depth, rows = x.shape
    heads = f.shape[0]
    length = n*rows
    return pl.pallas_call(functools.partial(attn_bwd_kernel, heads, n, rows),
        out_shape=[jax.ShapeDtypeStruct((n, 3*heads*64, rows), bf16), jax.ShapeDtypeStruct((heads,2*BLK), f32)],
        in_specs=[pl.BlockSpec(memory_space=pltpu.VMEM)]*5,
        out_specs=[pl.BlockSpec(memory_space=pltpu.VMEM)]*2,
        scratch_shapes=[pltpu.VMEM((128,length),bf16), pltpu.VMEM((length,128),bf16), pltpu.VMEM((length,128),bf16), pltpu.VMEM((128,length),bf16), pltpu.VMEM((length,128),bf16), pltpu.VMEM((length,128),bf16),
           pltpu.VMEM((BLK,2*BLK),f32), pltpu.VMEM((64,length),f32), pltpu.VMEM((BLK,2*BLK),f32)],
        compiler_params=pltpu.CompilerParams(vmem_limit_bytes=48*1024*1024),
        name="attention_backward",
    )(x, do, f, of, lse)


def expert_kernel(blocks, rows_ref, cots_ref, inner_ref, outer_ref, made_ref, back_ref, gin_ref, gout_ref, rows_t, cots_t, made, back, act_s, pre_s):
    step = pl.program_id(0)
    total = rows_ref.shape[0]
    piece = total // blocks

    @pl.when(step == 0)
    def _():
        for b in range(blocks):
            at = slice(b * piece, (b + 1) * piece)
            made[at, :] = jnp.zeros((piece, made.shape[1]), f32)
            back[at, :] = jnp.zeros((piece, made.shape[1]), f32)
        for b in range(total // 128):
            at = slice(b * 128, (b + 1) * 128)
            rows_t[:, at] = rows_ref[at, :].T
            cots_t[:, at] = cots_ref[at, :].T

    def part(b, carry):
        at = pl.ds(pl.multiple_of(b * piece, piece), piece)
        pre = dot(rows_ref[at, :], inner_ref[...])
        cot = dot(cots_ref[at, :], outer_ref[...], NT)
        square = pre * pre
        t = jnp.tanh(pre * (ROOT + (ROOT * 0.044715) * square))
        half = 0.5 + 0.5 * t
        act = (pre * half).astype(bf16)
        slope = half + (0.5 * pre) * (1.0 - t * t) * (ROOT + (ROOT * 3 * 0.044715) * square)
        back_pre = (cot * slope).astype(bf16)
        act_s[at, :] = act
        pre_s[at, :] = back_pre
        made[at, :] += dot(act, outer_ref[...])
        back[at, :] += dot(back_pre, inner_ref[...], NT)
        return carry

    lax.fori_loop(0, blocks, part, 0)
    gin_ref[...] = dot(rows_t[...], pre_s[...]).astype(bf16)
    gout_ref[...] = dot(cots_t[...], act_s[...]).astype(bf16).T

    @pl.when(step == pl.num_programs(0) - 1)
    def _():
        for b in range(blocks):
            at = slice(b * piece, (b + 1) * piece)
            made_ref[at, :] = made[at, :].astype(bf16)
            back_ref[at, :] = back[at, :].astype(bf16)


ROOT = 0.7978845608028654


def expert_pass(rows, cots, inner, outer):
    total, width = rows.shape
    hidden = inner.shape[1]
    wide = 384
    whole = pl.BlockSpec((total, width), lambda i: (0, 0))
    return pl.pallas_call(
        partial(expert_kernel, 4),
        grid=(hidden // wide,),
        out_shape=[
            jax.ShapeDtypeStruct((total, width), bf16),
            jax.ShapeDtypeStruct((total, width), bf16),
            jax.ShapeDtypeStruct((width, hidden), bf16),
            jax.ShapeDtypeStruct((hidden, width), bf16),
        ],
        in_specs=[
            whole,
            whole,
            pl.BlockSpec((width, wide), lambda i: (0, i)),
            pl.BlockSpec((wide, width), lambda i: (i, 0)),
        ],
        out_specs=[
            whole,
            whole,
            pl.BlockSpec((width, wide), lambda i: (0, i)),
            pl.BlockSpec((wide, width), lambda i: (i, 0)),
        ],
        scratch_shapes=[
            pltpu.VMEM((width, total), bf16),
            pltpu.VMEM((width, total), bf16),
            pltpu.VMEM((total, width), f32),
            pltpu.VMEM((total, width), f32),
            pltpu.VMEM((total, wide), bf16),
            pltpu.VMEM((total, wide), bf16),
        ],
        compiler_params=pltpu.CompilerParams(vmem_limit_bytes=50 * 1024 * 1024),
        name="expert_pass",
    )(rows, cots, inner, outer)


def rms_norm(values, gain):
    return values * lax.rsqrt(jnp.mean(values * values, axis=-1, keepdims=True) + EPSILON) * gain


def buckets(distance):
    far = 16 + sum(((distance >= limit).astype(jnp.int32) for limit in THRESHOLDS))
    return jnp.where(distance < 16, jnp.maximum(distance, 0), far)


def route_gates(router_logits, chosen):
    chances = jax.nn.softmax(router_logits, axis=-1)
    picks = (
        chosen[:, :, None] == jnp.arange(router_logits.shape[-1], dtype=jnp.int32)[None, None, :]
    ).astype(f32)
    picked = jnp.sum(chances[:, None, :] * picks, axis=2)
    return picked / jnp.sum(picked, axis=1, keepdims=True)


def slot_places(chosen, order, capacity, experts):
    hot = (chosen[:, :, None] == jnp.arange(experts, dtype=jnp.int32)[None, None, :]).astype(bf16)
    before = (order[None, :] < order[:, None]).astype(bf16)
    ahead = dot(before, hot.reshape(chosen.shape[0], 2 * experts)).reshape(hot.shape)
    firsts = jnp.sum(hot[:, 0].astype(f32), axis=0)
    hot = hot.astype(f32)
    slot_first = jnp.sum(ahead[:, 0] * hot[:, 0], axis=1)
    slot_second = jnp.sum((ahead[:, 1] + firsts[None, :]) * hot[:, 1], axis=1)
    slots = jnp.stack([slot_first, slot_second], axis=1).astype(jnp.int32)
    return jnp.where(slots < capacity, chosen * capacity + slots, experts * capacity)


def local(
    layer_input,
    cotangent,
    norm_gain_one,
    w_query,
    w_key,
    w_value,
    w_output,
    rel_table,
    norm_gain_two,
    w_router,
    w_expert_in,
    w_expert_out,
    segment_ids,
    routes,
    priority,
):
    inputs = layer_input[0].astype(f32)
    rows, width = inputs.shape
    heads = rel_table.shape[0]
    head_size = width // heads
    shards = lax.axis_size("ctx")
    experts = lax.axis_size("expert")
    capacity = min(rows, 5 * rows // (2 * experts))
    own_heads = heads // shards
    group = own_heads * head_size

    inner_weight = lax.all_gather(w_expert_in, ("ctx", "dp"), axis=1, tiled=True)[0]
    outer_weight = lax.all_gather(w_expert_out, ("ctx", "dp"), axis=1, tiled=True)[0]

    normed_input, norm_back = jax.vjp(rms_norm, inputs, norm_gain_one)
    normed_low = normed_input.astype(bf16)

    def project(weight):
        made = lax.dot_general(weight, normed_low, (((0,), (1,)), ((), ())), preferred_element_type=f32)
        return made.astype(bf16).reshape(shards, group, rows)

    segment_rows = jnp.broadcast_to(segment_ids.astype(bf16)[None], (shards, 16, rows))
    sent = jnp.concatenate([project(w_query), project(w_key), project(w_value), segment_rows], axis=1)
    held = lax.all_to_all(sent, "ctx", split_axis=0, concat_axis=0, tiled=True)

    table = rel_table.astype(f32)
    table = table - table[:, BUCKETS - 1 :]
    distance = jnp.arange(2 * BLK, dtype=jnp.int32)
    in_bucket = (buckets(distance)[:, None] == jnp.arange(BUCKETS, dtype=jnp.int32)[None, :]) & (
        distance[:, None] < THRESHOLDS[-1]
    )
    in_bucket = in_bucket.astype(f32)
    back_distance = BLK - distance
    in_bucket_front = (
        (buckets(back_distance)[:, None] == jnp.arange(BUCKETS, dtype=jnp.int32)[None, :])
        & (back_distance[:, None] < THRESHOLDS[-1])
        & (back_distance[:, None] >= 0)
    ).astype(f32)
    own_table = lax.dynamic_slice_in_dim(table, lax.axis_index("ctx") * own_heads, own_heads, 0)
    line_front = jnp.sum(own_table[:, None, :] * in_bucket_front[None], axis=2)
    line_back = jnp.sum(own_table[:, None, :] * in_bucket[None], axis=2)
    attended, attended_whole, lse = attn_fwd(held, line_front)
    mixed_t = lax.all_to_all(attended, "ctx", split_axis=0, concat_axis=0, tiled=True).reshape(width, rows)

    hidden = inputs + dot(mixed_t, w_output, TN)
    second_normed, norm_back_two = jax.vjp(rms_norm, hidden, norm_gain_two)
    normed_two_low = second_normed.astype(bf16)
    router_logits = dot(normed_two_low, w_router)
    chosen = routes[0]
    gates, gate_back = jax.vjp(partial(route_gates, chosen=chosen), router_logits)
    places = slot_places(chosen, priority[0, 0], capacity, experts)
    slots = jnp.arange(experts * capacity, dtype=jnp.int32)
    first = (places[:, 0][:, None] == slots[None, :]).astype(bf16)
    second = (places[:, 1][:, None] == slots[None, :]).astype(bf16)
    out_cot = cotangent[0].astype(f32)
    outgoing = dot(first + second, normed_two_low, TN).astype(bf16)
    outgoing_cot = (
        dot(first, (gates[:, 0:1] * out_cot).astype(bf16), TN)
        + dot(second, (gates[:, 1:2] * out_cot).astype(bf16), TN)
    ).astype(bf16)
    outgoing = outgoing.reshape(experts, capacity, width)
    outgoing_cot = outgoing_cot.reshape(experts, capacity, width)
    arrived = lax.all_to_all(outgoing, "expert", split_axis=0, concat_axis=0, tiled=True)
    arrived_cot = lax.all_to_all(outgoing_cot, "expert", split_axis=0, concat_axis=0, tiled=True)
    made, back, inner_grad, outer_grad = expert_pass(
        arrived.reshape(experts * capacity, width),
        arrived_cot.reshape(experts * capacity, width),
        inner_weight,
        outer_weight,
    )
    expert_in_grad = lax.psum_scatter(inner_grad[None], ("ctx", "dp"), scatter_dimension=1, tiled=True)
    expert_out_grad = lax.psum_scatter(outer_grad[None], ("ctx", "dp"), scatter_dimension=1, tiled=True)
    made = lax.all_to_all(
        made.reshape(experts, capacity, width), "expert", split_axis=0, concat_axis=0, tiled=True
    ).reshape(experts * capacity, width)
    back = lax.all_to_all(
        back.reshape(experts, capacity, width), "expert", split_axis=0, concat_axis=0, tiled=True
    ).reshape(experts * capacity, width)
    pair_first = dot(first, made)
    pair_second = dot(second, made)
    layer_output = (hidden + (gates[:, 0:1] * pair_first + gates[:, 1:2] * pair_second)).astype(bf16)
    gate_cot = jnp.stack([jnp.sum(out_cot * pair_first, axis=1), jnp.sum(out_cot * pair_second, axis=1)], axis=1)
    token_cot = dot(first + second, back)
    logit_cot = gate_back(gate_cot)[0]
    normed_two_cot = token_cot + jnp.dot(logit_cot, w_router.astype(f32).T, precision=HIGH_PRECISION)
    router_grad = jnp.dot(normed_two_low.astype(f32).T, logit_cot, precision=HIGH_PRECISION)
    hidden_part, gain_two_grad = norm_back_two(normed_two_cot)
    hidden_cot = out_cot + hidden_part
    hidden_cot_low = hidden_cot.astype(bf16)
    projection_grad = dot(mixed_t, hidden_cot_low)
    mixed_cot = dot(w_output, hidden_cot_low, NT).astype(bf16).reshape(shards, group, rows)
    held_cot = lax.all_to_all(mixed_cot, "ctx", split_axis=0, concat_axis=0, tiled=True)
    grads, diagonals = attn_bwd(held, held_cot, line_back, attended_whole, lse)
    near = jnp.sum(diagonals[:, :, None] * in_bucket[None], axis=1)
    near = jnp.concatenate([near[:, : BUCKETS - 1], -jnp.sum(near, axis=1, keepdims=True)], axis=1)
    table_grad = lax.dynamic_update_slice_in_dim(
        jnp.zeros((heads, BUCKETS), f32), near, lax.axis_index("ctx") * own_heads, 0
    )
    grads = lax.all_to_all(grads, "ctx", split_axis=0, concat_axis=0, tiled=True)
    query_cot = grads[:, :group].reshape(width, rows)
    key_cot = grads[:, group : 2 * group].reshape(width, rows)
    value_cot = grads[:, 2 * group :].reshape(width, rows)

    def turned(weight, cot):
        return lax.dot_general(cot, weight, (((0,), (1,)), ((), ())), preferred_element_type=f32)

    normed_cot = turned(w_query, query_cot) + turned(w_key, key_cot) + turned(w_value, value_cot)

    def weight_grad(cot):
        return lax.dot_general(normed_low, cot, (((0,), (1,)), ((), ())), preferred_element_type=f32).astype(bf16)

    input_part, gain_one_grad = norm_back(normed_cot)
    input_grad = hidden_cot + input_part
    everywhere = ("expert", "ctx", "dp")
    large = lax.psum(
        (weight_grad(query_cot), weight_grad(key_cot), weight_grad(value_cot), projection_grad.astype(bf16)),
        everywhere,
    )
    small = lax.psum((gain_one_grad, table_grad, gain_two_grad, router_grad), everywhere)
    return (
        layer_output[None],
        input_grad[None],
        small[0],
        large[0].astype(f32),
        large[1].astype(f32),
        large[2].astype(f32),
        large[3].astype(f32),
        small[1],
        small[2],
        small[3],
        expert_in_grad.astype(f32),
        expert_out_grad.astype(f32),
    )


def solution(mesh):
    placed = (
        P(("expert", "dp"), "ctx", None),
        P(("expert", "dp"), "ctx", None),
        P(),
        P(),
        P(),
        P(),
        P(),
        P(),
        P(),
        P(),
        P("expert", ("ctx", "dp"), None),
        P("expert", ("ctx", "dp"), None),
        P(("expert", "dp"), "ctx"),
        P(("expert", "dp"), "ctx", None),
        P(("expert", "dp"), "ctx", None),
    )
    return jax.shard_map(
        local,
        mesh=mesh,
        in_specs=placed,
        out_specs=(
            P(("expert", "dp"), "ctx", None),
            P(("expert", "dp"), "ctx", None),
            P(),
            P(),
            P(),
            P(),
            P(),
            P(),
            P(),
            P(),
            P("expert", ("ctx", "dp"), None),
            P("expert", ("ctx", "dp"), None),
        ),
        check_vma=False,
    )
```

```python
import functools
from functools import partial

import jax
import jax.numpy as jnp
from jax import lax
from jax.experimental import pallas as pl
from jax.experimental.pallas import tpu as pltpu
from jax.sharding import PartitionSpec as P

bf16 = jnp.bfloat16
f32 = jnp.float32
HIGH_PRECISION = lax.Precision.HIGHEST
EPSILON = 1e-06
THRESHOLDS = (19, 21, 24, 27, 31, 35, 40, 46, 52, 59, 67, 77, 87, 99, 113)
BUCKETS=32
NEG=-1e30
BLK=256
NT=(((1,),(1,)),((),()))
TN=(((0,),(0,)),((),()))

def dot(a,b,dims=(((1,),(0,)),((),()))):
    return lax.dot_general(a,b,dims,preferred_element_type=f32)

def seg_mask_rows(seg):
    which = lax.broadcasted_iota(jnp.int32, seg.shape, 0).astype(f32)
    same = seg.astype(f32) == which
    return jnp.where(same, 0.0, NEG).astype(bf16), jnp.where(same, 1.0, 0.0).astype(bf16)

def split3(v):
    hi = v.astype(bf16); rest = v - hi.astype(f32)
    mid = rest.astype(bf16); rest = rest - mid.astype(f32)
    return hi, mid, rest.astype(bf16)

ROOT = 0.7978845608028654


def remote(src, dst, send_sem, recv_sem, where):
    return pltpu.make_async_remote_copy(
        src_ref=src,
        dst_ref=dst,
        send_sem=send_sem,
        recv_sem=recv_sem,
        device_id=where,
        device_id_type=pl.DeviceIdType.MESH,
    )


def expert_split():
    experts = lax.axis_size("expert")
    me = lax.axis_index("expert")
    return experts // 2, lax.div(me, 2), lax.rem(me, 2)


def gather_start(piece, whole, near_sems, far_sems, rows=None):
    lanes, lane, core = expert_split()
    me = lane * 2 + core
    view = whole.at[me] if rows is None else whole.at[me, rows]
    copies = [remote(piece, view, near_sems.at[0], near_sems.at[1], {"expert": lane * 2 + 1 - core})]
    for k in range(1, lanes):
        copies.append(
            remote(piece, view, far_sems.at[0, k - 1], far_sems.at[1, k - 1], {"expert": lax.rem(lane + k, lanes) * 2 + core})
        )
    for copy in copies:
        copy.start()
    return copies


def relay(k, whole, sems):
    lanes, lane, core = expert_split()
    source = lax.rem(lane - k + lanes, lanes) * 2 + core
    return remote(whole.at[source], whole.at[source], sems.at[0, k - 1], sems.at[1, k - 1], {"expert": lane * 2 + 1 - core})


def greet(names):
    barrier = pltpu.get_barrier_semaphore()
    total = 0
    for name in names:
        count, at = lax.axis_size(name), lax.axis_index(name)
        for k in range(1, count):
            pl.semaphore_signal(
                barrier, inc=1, device_id={name: lax.rem(at + k, count)}, device_id_type=pl.DeviceIdType.MESH
            )
        total += count - 1
    return barrier, total


def moe_kernel(
    capacity, mixed_t, w_output, x_ref, cot_ref, gain_ref, router_ref, info_ref, cots_hbm, inner_hbm, outer_hbm,
    base_ref, far_ref, hidden_cot_ref, mixed_cot_ref, small_ref, gin_hbm, gout_hbm,
    nt, cots, inner, outer, act_all, pre_all, rows_all, cots_all, made, back, part, pair_in, total,
    core_in, far_in, gate_out, gate_in,
    load_sems, cot_sems, near_sems, far_sems, relay_sems, pair_sems, core_sems, back_sems, gate_sems, stage_sems, free_sem,
):
    experts = lax.axis_size("expert")
    lanes, lane, core = expert_split()
    me = lane * 2 + core
    other = lane * 2 + 1 - core
    rows, width = x_ref.shape
    hidden_size = inner.shape[1]
    wide = width
    hidden = hidden_cot_ref
    pieces = 2
    step_rows = rows // pieces

    loads = [
        pltpu.make_async_copy(inner_hbm, inner, load_sems.at[0]),
        pltpu.make_async_copy(outer_hbm, outer, load_sems.at[1]),
    ]
    for copy in loads:
        copy.start()
    barrier, peers = greet(("expert",))
    sent = []
    for p in range(pieces):
        at = slice(p * step_rows, (p + 1) * step_rows)
        now = x_ref[at, :].astype(f32) + dot(mixed_t[:, at], w_output[...], TN)
        hidden[at, :] = now
        scale = lax.rsqrt(jnp.mean(now * now, axis=1, keepdims=True) + EPSILON)
        nt[me, at, :] = (now * scale * gain_ref[...].reshape(1, width)).astype(bf16)
        if p == 0:
            pl.semaphore_wait(barrier, peers)
        sent.append(gather_start(nt.at[me, at], nt, near_sems.at[p], far_sems.at[p], at))

    def gate_rows(source):
        logits = dot(router_ref[...], nt[source], NT)
        which = lax.broadcasted_iota(jnp.int32, logits.shape, 0)
        info = info_ref[source]
        chosen = (which == info[0:1]) | (which == info[1:2])
        top = jnp.max(jnp.where(chosen, logits, NEG), axis=0, keepdims=True)
        power = jnp.where(chosen, jnp.exp(jnp.minimum(logits - top, 0.0)), 0.0)
        return power / jnp.sum(power, axis=0, keepdims=True)

    order = [me, other] + [
        lax.rem(lane - k + lanes, lanes) * 2 + sc for k in range(1, lanes) for sc in range(2)
    ]

    def fetch(i):
        return pltpu.make_async_copy(cots_hbm.at[order[i]], cots.at[i % 2], cot_sems.at[i % 2])

    fetch(0).start()

    def process(i, target, middle=None):
        source = order[i]
        fetch(i).wait()
        if i + 1 < len(order):
            fetch(i + 1).start()
        block = slice(i * capacity, (i + 1) * capacity)
        info = info_ref[source]
        place = jnp.where(info[0:1] == me, info[2:3], jnp.where(info[1:2] == me, info[3:4], -1))
        slot = lax.broadcasted_iota(jnp.int32, (capacity, rows), 0)
        hot = slot == place
        pick = jnp.where(hot, 1.0, 0.0)
        pick_low = pick.astype(bf16)
        gates = gate_rows(source)
        which = lax.broadcasted_iota(jnp.int32, gates.shape, 0)
        own_gate = jnp.sum(jnp.where(which == me, gates, 0.0), axis=0, keepdims=True)
        slot_gate = jnp.sum(pick * own_gate, axis=1, keepdims=True)
        rows_all[block, :] = dot(pick_low, nt[source]).astype(bf16)
        cots_all[block, :] = (slot_gate * dot(pick_low, cots[i % 2])).astype(bf16)
        made[...] = jnp.zeros_like(made)
        back[...] = jnp.zeros_like(back)

        def part_of(f, carry):
            at = pl.ds(pl.multiple_of(f * wide, wide), wide)
            pre = dot(rows_all[block, :], inner[:, at])
            cot = dot(cots_all[block, :], outer[at, :], NT)
            square = pre * pre
            t = jnp.tanh(pre * (ROOT + (ROOT * 0.044715) * square))
            half = 0.5 + 0.5 * t
            act = (pre * half).astype(bf16)
            slope = half + (0.5 * pre) * (1.0 - t * t) * (ROOT + (ROOT * 3 * 0.044715) * square)
            back_pre = (cot * slope).astype(bf16)
            act_all[block, at] = act
            pre_all[block, at] = back_pre
            made[...] += dot(act, outer[at, :])
            back[...] += dot(back_pre, inner[:, at], NT)
            return carry

        steps = hidden_size // wide
        if middle is None:
            lax.fori_loop(0, steps, part_of, 0)
        else:
            lax.fori_loop(0, steps // 2, part_of, 0)
            middle()
            lax.fori_loop(steps // 2, steps, part_of, 0)
        gated = slot_gate * made[...].astype(bf16).astype(f32)
        picked_cot = dot(pick_low, cots[i % 2])
        slot_cot = jnp.sum(picked_cot * made[...].astype(bf16).astype(f32), axis=1, keepdims=True)
        gate_out[source] = jnp.broadcast_to(jnp.sum(pick * slot_cot, axis=0, keepdims=True), (8, rows))
        column = jnp.broadcast_to(place.astype(f32), (128, rows)).T[:, 0:1]
        lane_at = lax.broadcasted_iota(jnp.int32, (rows, capacity), 1).astype(f32)
        put = jnp.where(lane_at == column, 1.0, 0.0).astype(bf16)
        target[0] = dot(put, back[...].astype(bf16)).astype(bf16)
        target[1] = dot(put, gated.astype(bf16)).astype(bf16)

    for copy in loads:
        copy.wait()
    process(0, total)
    for p in range(pieces):
        sent[p][0].wait_recv()
    process(1, part.at[0])
    core_copies = [
        remote(part.at[0, v], core_in.at[v], core_sems.at[0, v], core_sems.at[1, v], {"expert": other}) for v in range(2)
    ]
    for copy in core_copies:
        copy.start()

    def gate_copy(k):
        to = lax.rem(me + k, experts)
        return remote(gate_out.at[to], gate_in.at[me], gate_sems.at[0, k - 1], gate_sems.at[1, k - 1], {"expert": to})

    relays, pairs, ready = [], [], []
    for k in range(1, lanes):
        for p in range(pieces):
            sent[p][k].wait_recv()
        passed = relay(k, nt, relay_sems)
        passed.start()
        relays.append(passed)
        from_lane = lax.rem(lane - k + lanes, lanes)
        if k == 1:
            for copy in core_copies:
                copy.wait_send()
        for sc in range(2):
            @pl.when(core != sc)
            def _():
                passed.wait_recv()

            process(2 + 2 * (k - 1) + sc, part.at[sc], ready.pop() if ready else None)
            pair = [
                remote(part.at[sc, v], pair_in.at[v], pair_sems.at[0, v, k - 1], pair_sems.at[1, v, k - 1], {"expert": other})
                for v in range(2)
            ]
            home = [
                remote(part.at[sc, 0], far_in.at[k - 1], back_sems.at[0, k - 1], back_sems.at[1, k - 1], {"expert": from_lane * 2 + sc})
            ]

            @pl.when(core != sc)
            def _():
                if k > 1:
                    pl.semaphore_wait(free_sem, 1)
                for copy in pair:
                    copy.start()

            def finish(k=k, sc=sc, pair=pair, home=home):
                @pl.when(core == sc)
                def _():
                    pair[0].wait_recv()
                    part[sc, 0] = (part[sc, 0].astype(f32) + pair_in[0].astype(f32)).astype(bf16)
                    home[0].start()
                    pair[1].wait_recv()
                    far_ref[k - 1] = (part[sc, 1].astype(f32) + pair_in[1].astype(f32)).astype(bf16)
                    if k + 1 < lanes:
                        pl.semaphore_signal(
                            free_sem, inc=1, device_id={"expert": other}, device_id_type=pl.DeviceIdType.MESH
                        )

            ready.append(finish)
            pairs.append((sc, pair, home))
        if k + 1 < lanes:
            ready.pop()()
            for sc, pair, home in pairs[-2:]:
                @pl.when(core != sc)
                def _():
                    for copy in pair:
                        copy.wait_send()

                @pl.when(core == sc)
                def _():
                    for copy in home:
                        copy.wait_send()
    if ready:
        ready.pop()()
    gate_copies = [gate_copy(k) for k in range(1, experts)]
    for copy in gate_copies:
        copy.start()
    count = rows_all.shape[0]
    for b in range(count // 128):
        at = slice(b * 128, (b + 1) * 128)
        inner[:, at] = rows_all[at, :].T
        inner[:, slice(count + b * 128, count + (b + 1) * 128)] = cots_all[at, :].T
    steps = hidden_size // wide

    def store(f, v):
        at = pl.ds(pl.multiple_of(f * wide, wide), wide)
        return pltpu.make_async_copy(outer.at[v * width : (v + 1) * width], gin_hbm.at[:, at] if v == 0 else gout_hbm.at[at, :], stage_sems.at[v])

    def grads(f, carry):
        at = pl.ds(pl.multiple_of(f * wide, wide), wide)

        @pl.when(f > 0)
        def _():
            store(f - 1, 0).wait()

        outer[:width, :] = dot(inner[:, :count], pre_all[:, at]).astype(bf16)
        store(f, 0).start()

        @pl.when(f > 0)
        def _():
            store(f - 1, 1).wait()

        outer[width : 2 * width, :] = dot(inner[:, count : 2 * count], act_all[:, at]).astype(bf16).T
        store(f, 1).start()
        return carry

    lax.fori_loop(0, steps, grads, 0)
    for copy in gate_copies:
        copy.wait()
    core_copies[0].wait_recv()
    token_cot = total[0].astype(f32) + core_in[0].astype(f32)
    for k in range(1, lanes):
        remote(part.at[0, 0], far_in.at[k - 1], back_sems.at[0, k - 1], back_sems.at[1, k - 1], {"expert": other}).wait_recv()
        token_cot = token_cot + far_in[k - 1].astype(f32)
    gates = gate_rows(me)
    pad = gates.shape[0]
    which = lax.broadcasted_iota(jnp.int32, gates.shape, 0)
    gate_cot = jnp.where(which == me, gate_out[me][0:1], 0.0)
    for k in range(1, experts):
        source = lax.rem(me + k, experts)
        gate_cot = gate_cot + jnp.where(which == source, gate_in[source][0:1], 0.0)
    logit_cot = gates * (gate_cot - jnp.sum(gates * gate_cot, axis=0, keepdims=True))
    three = jnp.concatenate(split3(logit_cot), axis=0)
    router_three = jnp.concatenate([router_ref[...]] * 3, axis=0)
    normed_cot = token_cot + dot(three, router_three, TN)
    router_grad = dot(three, nt[me])
    router_grad = router_grad[:pad] + router_grad[pad : 2 * pad] + router_grad[2 * pad :]
    now = hidden[...]
    scale = lax.rsqrt(jnp.mean(now * now, axis=1, keepdims=True) + EPSILON)
    unit = now * scale
    gained = normed_cot * gain_ref[...].reshape(1, width)
    hidden_cot = cot_ref[...].astype(f32) + scale * (gained - unit * jnp.mean(unit * gained, axis=1, keepdims=True))
    hidden_cot_ref[...] = hidden_cot
    mixed_cot_ref[...] = dot(w_output[...], hidden_cot.astype(bf16), NT).astype(bf16)
    small_ref[0:8, :] = jnp.broadcast_to(jnp.sum(unit * normed_cot, axis=0, keepdims=True), (8, width))
    small_ref[8:, :] = router_grad
    core_copies[1].wait_recv()
    base_ref[...] = now + (total[1].astype(f32) + core_in[1].astype(f32))
    store(steps - 1, 0).wait()
    store(steps - 1, 1).wait()
    for sc, pair, home in pairs[-2:]:
        @pl.when(core != sc)
        def _():
            for copy in pair:
                copy.wait_send()

        @pl.when(core == sc)
        def _():
            for copy in home:
                copy.wait_send()
    for copy in relays:
        copy.wait_send()
    for p in range(pieces):
        for copy in sent[p]:
            copy.wait_send()


def moe_pass(capacity, mixed_t, w_output, x, cot, gain, router, info, cots, inner, outer):
    rows, width = x.shape
    experts = cots.shape[0]
    lanes = experts // 2
    hidden_size = inner.shape[1]
    total = experts * capacity
    vmem = pl.BlockSpec(memory_space=pltpu.VMEM)
    hbm = pl.BlockSpec(memory_space=pl.ANY)
    dma = pltpu.SemaphoreType.DMA
    far = max(lanes - 1, 1)
    return pl.pallas_call(
        partial(moe_kernel, capacity),
        out_shape=[
            jax.ShapeDtypeStruct((rows, width), f32),
            jax.ShapeDtypeStruct((far, rows, width), bf16),
            jax.ShapeDtypeStruct((rows, width), f32),
            jax.ShapeDtypeStruct((width, rows), bf16),
            jax.ShapeDtypeStruct((8 + router.shape[0], width), f32),
            jax.ShapeDtypeStruct((width, hidden_size), bf16),
            jax.ShapeDtypeStruct((hidden_size, width), bf16),
        ],
        in_specs=[vmem] * 7 + [hbm] * 3,
        out_specs=[vmem] * 5 + [hbm] * 2,
        scratch_shapes=[
            pltpu.VMEM((experts, rows, width), bf16),
            pltpu.VMEM((2, rows, width), bf16),
            pltpu.VMEM((width, hidden_size), bf16),
            pltpu.VMEM((hidden_size, width), bf16),
            pltpu.VMEM((total, hidden_size), bf16),
            pltpu.VMEM((total, hidden_size), bf16),
            pltpu.VMEM((total, width), bf16),
            pltpu.VMEM((total, width), bf16),
            pltpu.VMEM((capacity, width), f32),
            pltpu.VMEM((capacity, width), f32),
            pltpu.VMEM((2, 2, rows, width), bf16),
            pltpu.VMEM((2, rows, width), bf16),
            pltpu.VMEM((2, rows, width), bf16),
            pltpu.VMEM((2, rows, width), bf16),
            pltpu.VMEM((far, rows, width), bf16),
            pltpu.VMEM((experts, 8, rows), f32),
            pltpu.VMEM((experts, 8, rows), f32),
            dma((2,)),
            dma((2,)),
            dma((2, 2)),
            dma((2, 2, far)),
            dma((2, far)),
            dma((2, 2, far)),
            dma((2, 2)),
            dma((2, far)),
            dma((2, experts - 1)),
            dma((2,)),
            pltpu.SemaphoreType.REGULAR,
        ],
        compiler_params=pltpu.CompilerParams(
            collective_id=1, has_side_effects=True, vmem_limit_bytes=65000 * 1024
        ),
        name="moe_pass",
    )(mixed_t, w_output, x, cot, gain, router, info, cots, inner, outer)


def bias_line(distance, table):
    far = jnp.full(distance.shape, BUCKETS // 2, jnp.int32)
    for limit in THRESHOLDS:
        far = far + jnp.where(distance >= limit, 1, 0)
    bucket = jnp.where(distance < BUCKETS // 2, distance, far)
    own = (distance >= 0) & (distance < THRESHOLDS[-1])
    which = lax.broadcasted_iota(jnp.int32, (BUCKETS, distance.shape[1]), 0)
    hot = jnp.where(own & (which == bucket), 1.0, 0.0).astype(bf16)
    last = table[:, BUCKETS - 1 :].astype(f32)
    return dot(table, hot) - jnp.where(own, last, 0.0)


def column_of(row):
    return jnp.broadcast_to(row, (128, row.shape[1])).T


def front_kernel(
    heads, n, rows, x_ref, gain_ref, wq, wk, wv, table_ref, segment_ref, routes_ref, order_ref, cot_hbm, win_hbm, wout_hbm,
    held, mixed, of_ref, lse_ref, normed_t, infos, cots_hbm, win_all, wout_all,
    made, given, qa, ka, vn, bias, s_ref, lines,
    held_sems, mixed_sems, near_sems, far_sems, relay_sems, info_sems, own_sems, line_sems, side_sems,
):
    size = 64
    group = heads * size
    width = n * group
    length = n * rows
    sides = lax.axis_size("dp")
    me = lax.axis_index("ctx")
    side = lax.axis_index("dp")
    experts = lax.axis_size("expert")
    expert = lax.axis_index("expert")
    barrier = pltpu.get_barrier_semaphore()
    for name, count, at in (("ctx", n, me), ("dp", sides, side), ("expert", experts, expert)):
        for k in range(1, count):
            pl.semaphore_signal(
                barrier, inc=1, device_id={name: lax.rem(at + k, count)}, device_id_type=pl.DeviceIdType.MESH
            )
    owns = [
        pltpu.make_async_copy(cot_hbm, cots_hbm.at[expert], own_sems.at[0]),
        pltpu.make_async_copy(win_hbm, win_all.at[me * sides + side], own_sems.at[1]),
        pltpu.make_async_copy(wout_hbm, wout_all.at[me * sides + side], own_sems.at[2]),
    ]
    for copy in owns:
        copy.start()
    pl.semaphore_wait(barrier, n + sides + experts - 3)
    shard = (win_hbm, wout_hbm)
    whole = (win_all, wout_all)

    def along(way, s, v):
        j = me - s if way == 0 else me + s
        to = me + 1 if way == 0 else me - 1
        at = j * sides + side
        source = shard[v] if s == 0 else whole[v].at[at]
        return remote(source, whole[v].at[at], line_sems.at[0, way, v, s], line_sems.at[1, way, v, s], {"ctx": to})

    def across(way, s, v):
        j = me - s if way == 0 else me + s
        at = j * sides + side
        source = shard[v] if s == 0 else whole[v].at[at]
        return [
            remote(
                source, whole[v].at[at], side_sems.at[0, way, v, k - 1, s], side_sems.at[1, way, v, k - 1, s],
                {"dp": lax.rem(side + k, sides)},
            )
            for k in range(1, sides)
        ]

    def holds(way, s):
        return me - s >= 0 if way == 0 else me + s < n

    def passes(way, s):
        return (me - s >= 0) & (me < n - 1) if way == 0 else (me + s < n) & (me > 0)

    def advance(s, v):
        for way in range(2):
            if s > 0:
                @pl.when(holds(way, s))
                def _():
                    along(way, s - 1, v).wait_recv()

            @pl.when(passes(way, s))
            def _():
                along(way, s, v).start()

            if s > 0:
                @pl.when(holds(way, s))
                def _():
                    for copy in across(way, s, v):
                        copy.start()

    for v in range(2):
        for copy in across(0, 0, v):
            copy.start()
        advance(0, v)
    sent = gather_start(cot_hbm, cots_hbm, near_sems, far_sems)

    x = x_ref[...].astype(f32)
    normed = x * lax.rsqrt(jnp.mean(x * x, axis=1, keepdims=True) + EPSILON) * gain_ref[...].reshape(1, width)
    normed = normed.astype(bf16)
    held_copies = []
    here = pl.ds(pl.multiple_of(me * group, 16), group)
    seg = jnp.broadcast_to(segment_ref[...].astype(f32), (16, rows)).astype(bf16)
    made[3, 0:16, :] = seg
    held[me, 3 * group : 3 * group + 16, :] = seg
    for kind, weight in enumerate((wq, wk, wv)):
        made[kind] = dot(normed, weight[...]).astype(bf16).T
        for k in range(1, n):
            to = lax.rem(me + k, n)
            copy = remote(
                made.at[kind, pl.ds(pl.multiple_of(to * group, 16), group)],
                held.at[me, kind * group : (kind + 1) * group],
                held_sems.at[0, kind, k - 1], held_sems.at[1, kind, k - 1], {"ctx": to},
            )
            copy.start()
            held_copies.append(copy)
        held[me, kind * group : (kind + 1) * group, :] = made[kind, here, :]
    for k in range(1, n):
        copy = remote(
            made.at[3, 0:16], held.at[me, 3 * group : 3 * group + 16], held_sems.at[0, 3, k - 1], held_sems.at[1, 3, k - 1],
            {"ctx": lax.rem(me + k, n)},
        )
        copy.start()
        held_copies.append(copy)
    normed_t[...] = normed.T

    order_row = order_ref[...].astype(f32)
    before = jnp.where(column_of(order_row)[:, 0:1] < order_row, 1.0, 0.0).astype(bf16)
    kinds = 16
    which = lax.broadcasted_iota(jnp.int32, (kinds, rows), 0)
    chosen = [routes_ref[c : c + 1, :] for c in range(2)]
    hot = [jnp.where(which == c, 1.0, 0.0) for c in chosen]
    ahead = [dot(h.astype(bf16), before) for h in hot]
    firsts = jnp.sum(hot[0], axis=1, keepdims=True)
    slots = [jnp.sum(hot[0] * ahead[0], axis=0, keepdims=True), jnp.sum(hot[1] * (ahead[1] + firsts), axis=0, keepdims=True)]
    infos[expert] = jnp.concatenate(chosen + [s.astype(jnp.int32) for s in slots] + [jnp.zeros((4, rows), jnp.int32)], axis=0)
    info_copies = [
        remote(infos.at[expert], infos.at[expert], info_sems.at[0, k - 1], info_sems.at[1, k - 1], {"expert": lax.rem(expert + k, experts)})
        for k in range(1, experts)
    ]
    for copy in info_copies:
        copy.start()
    lines[...] = bias_line(BLK - lax.broadcasted_iota(jnp.int32, (1, 2 * BLK), 1), table_ref[...])

    advance(1, 0)
    advance(1, 1)
    for copy in held_copies:
        copy.wait_recv()

    def mixed_copy(h, k):
        to = lax.rem(me + k, n)
        base = pl.multiple_of(h * size, size)
        return remote(
            given.at[to, pl.ds(base, size)], mixed.at[pl.ds(pl.multiple_of(me * group + base, 16), size)],
            mixed_sems.at[0, h, k - 1], mixed_sems.at[1, h, k - 1], {"ctx": to},
        )

    def head(h, carry):
        base = pl.multiple_of(h * size, size)
        for s in range(n):
            at = slice(s * rows, (s + 1) * rows)
            q = held[s, pl.ds(base, size), :]
            k = held[s, pl.ds(base + group, size), :]
            v = held[s, pl.ds(base + 2 * group, size), :]
            mask, hot = seg_mask_rows(held[s, 3 * group : 3 * group + 16, :])
            zeros = jnp.zeros((48, rows), bf16)
            qa[at, :] = jnp.concatenate([q * jnp.asarray(0.125, bf16), mask, zeros], axis=0).T
            ka[:, at] = jnp.concatenate([k, hot, zeros], axis=0)
            vn[at, :] = jnp.concatenate([v, jnp.zeros((64, rows), bf16)], axis=0).T
        line = jnp.broadcast_to(lines[pl.ds(me * heads + h, 1), :], (BLK, 2 * BLK))
        rolled = pltpu.roll(line, 0, 1, stride=1, stride_axis=0)
        r = lax.broadcasted_iota(jnp.int32, (BLK, 2 * BLK), 0)
        c = lax.broadcasted_iota(jnp.int32, (BLK, 2 * BLK), 1)
        bias[...] = jnp.where(c - r > BLK, NEG, rolled)
        for t in range(length // BLK):
            qt = qa[t * BLK : (t + 1) * BLK, :]
            near0 = max(t - 1, 0) * BLK
            end = (t + 1) * BLK
            chunks = [(near0, end)] + [(a, min(a + 2 * BLK, near0)) for a in range(0, near0, 2 * BLK)]
            top = None
            for a, b in chunks:
                s = dot(qt, ka[:, a:b])
                if a == near0:
                    s = s + bias[:, 2 * BLK - (b - a) :]
                s_ref[:, a:b] = s
                part = s[:, :128]
                for i in range(1, (b - a) // 128):
                    part = jnp.maximum(part, s[:, i * 128 : (i + 1) * 128])
                top = part if top is None else jnp.maximum(top, part)
            m = jnp.max(top, axis=1, keepdims=True)
            total = None
            o = None
            for a, b in chunks:
                p = jnp.exp(s_ref[:, a:b] - m)
                part = p[:, :128]
                for i in range(1, (b - a) // 128):
                    part = part + p[:, i * 128 : (i + 1) * 128]
                total = part if total is None else total + part
                u = dot(p.astype(bf16), vn[a:b, :])
                o = u if o is None else o + u
            l = jnp.sum(total, axis=1, keepdims=True)
            o = o / l
            lane = lax.broadcasted_iota(jnp.int32, (BLK, 128), 1)
            o = jnp.where(lane == 64, m + jnp.log(l), o)
            ot = o.T
            src, off = (t * BLK) // rows, (t * BLK) % rows
            given[src, pl.ds(base, size), off : off + BLK] = ot[:size].astype(bf16)
            of_ref[pl.ds(base, size), t * BLK : (t + 1) * BLK] = ot[:size]
            lse_ref[pl.ds(h, 1), t * BLK : (t + 1) * BLK] = ot[size : size + 1]
        for k in range(1, n):
            mixed_copy(h, k).start()
        mixed[pl.ds(pl.multiple_of(me * group + base, 16), size), :] = given[me, pl.ds(base, size), :]

        @pl.when(h == 0)
        def _():
            advance(2, 0)

        @pl.when(h == 1)
        def _():
            advance(2, 1)

        return carry

    lax.fori_loop(0, heads, head, 0)
    for s in range(3, n):
        for v in range(2):
            advance(s, v)
    relays = []
    for k in range(1, experts // 2):
        sent[k].wait_recv()
        passed = relay(k, cots_hbm, relay_sems)
        passed.start()
        relays.append(passed)
    sent[0].wait_recv()
    for h in range(heads):
        for k in range(1, n):
            mixed_copy(h, k).wait()
    for copy in held_copies + sent:
        copy.wait_send()
    for copy in relays + info_copies + owns:
        copy.wait()
    for v in range(2):
        for s in range(n):
            for way in range(2):
                @pl.when(passes(way, s))
                def _():
                    along(way, s, v).wait_send()

                if s > 0 or way == 0:
                    @pl.when(holds(way, s))
                    def _():
                        for copy in across(way, s, v):
                            copy.wait()


def front_pass(x, gain, wq, wk, wv, table, segments, routes, order, cot, win, wout):
    rows, width = x.shape
    n = lax.axis_size("ctx")
    sides = lax.axis_size("dp")
    experts = lax.axis_size("expert")
    heads = table.shape[0] // n
    group = heads * 64
    length = n * rows
    blocks = n * sides
    vmem = pl.BlockSpec(memory_space=pltpu.VMEM)
    hbm = pl.BlockSpec(memory_space=pl.ANY)
    dma = pltpu.SemaphoreType.DMA
    far = max(experts // 2 - 1, 1)
    some = max(sides - 1, 1)
    return pl.pallas_call(
        partial(front_kernel, heads, n, rows),
        out_shape=[
            jax.ShapeDtypeStruct((n, 3 * group + 16, rows), bf16),
            jax.ShapeDtypeStruct((width, rows), bf16),
            jax.ShapeDtypeStruct((group, length), f32),
            jax.ShapeDtypeStruct((heads, length), f32),
            jax.ShapeDtypeStruct((width, rows), bf16),
            jax.ShapeDtypeStruct((experts, 8, rows), jnp.int32),
            jax.ShapeDtypeStruct((experts, rows, width), bf16),
            jax.ShapeDtypeStruct((blocks,) + win.shape, bf16),
            jax.ShapeDtypeStruct((blocks,) + wout.shape, bf16),
        ],
        in_specs=[vmem] * 9 + [hbm] * 3,
        out_specs=[vmem] * 6 + [hbm] * 3,
        scratch_shapes=[
            pltpu.VMEM((4, width, rows), bf16),
            pltpu.VMEM((n, group, rows), bf16),
            pltpu.VMEM((length, 128), bf16),
            pltpu.VMEM((128, length), bf16),
            pltpu.VMEM((length, 128), bf16),
            pltpu.VMEM((BLK, 2 * BLK), f32),
            pltpu.VMEM((BLK, length), f32),
            pltpu.VMEM((table.shape[0], 2 * BLK), f32),
            dma((2, 4, n - 1)),
            dma((2, heads, n - 1)),
            dma((2,)),
            dma((2, far)),
            dma((2, far)),
            dma((2, experts - 1)),
            dma((3,)),
            dma((2, 2, 2, n)),
            dma((2, 2, 2, some, n)),
        ],
        compiler_params=pltpu.CompilerParams(
            collective_id=2, has_side_effects=True, vmem_limit_bytes=60 * 1024 * 1024
        ),
        name="front_pass",
    )(x, gain, wq, wk, wv, table, segments, routes, order, cot, win, wout)


def line_order(n):
    order = []
    for i in range((n + 1) // 2):
        order.append(n - 1 - i)
        if i != n - 1 - i:
            order.append(i)
    return order


def line_scatter(n, own, right, left, right_sems, left_sems, ready):
    me = lax.axis_index("ctx")
    items = {}
    for j in line_order(n):
        for r in range(j):
            items.setdefault(ready[j] + r, []).append((0, r, j))
        for r in range(n - 1, j, -1):
            items.setdefault(ready[j] + n - 1 - r, []).append((1, r, j))
    steps = max(items) + 1

    def pass_on(way, r, j):
        taken, sems = (right, right_sems) if way == 0 else (left, left_sems)
        first = 0 if way == 0 else n - 1
        return remote(
            own.at[j] if r == first else taken.at[j], taken.at[j], sems.at[0, j], sems.at[1, j],
            {"ctx": r + 1 if way == 0 else r - 1},
        )

    def advance(step):
        for way, r, j in items.get(step, []):
            @pl.when(me == r)
            def _():
                copy = pass_on(way, r, j)
                if r != (0 if way == 0 else n - 1):
                    taken = right if way == 0 else left
                    copy.wait_recv()
                    taken[j] = (taken[j].astype(f32) + own[j].astype(f32)).astype(bf16)
                copy.start()

    def finish(out):
        for j in range(n):
            @pl.when(me == j)
            def _():
                total = own[j].astype(f32)
                if j > 0:
                    pass_on(0, j - 1, j).wait_recv()
                    total = total + right[j].astype(f32)
                if j < n - 1:
                    pass_on(1, j + 1, j).wait_recv()
                    total = total + left[j].astype(f32)
                out[...] = total.astype(bf16)

    def drain():
        for step in range(steps):
            for way, r, j in items.get(step, []):
                @pl.when(me == r)
                def _():
                    pass_on(way, r, j).wait_send()

    return advance, finish, drain, steps


def back_kernel(
    heads, n, rows, x_ref, do_ref, table_ref, of_ref, lse_ref, base_ref, far_ref, gin_hbm, gout_hbm,
    cots_ref, diag_ref, ein_ref, own_b, out_ref,
    do_in, g_ref, qa, ka, va, da, qn, dn, bias, dq, gsum,
    own_a, side_a, side_b, right_a, left_a,
    do_sems, out_sems, own_sems, side_sems, right_sems, left_sems, lines, far_in, far_sems,
):
    size = 64
    group = heads * size
    length = n * rows
    sides = lax.axis_size("dp")
    me = lax.axis_index("ctx")
    side = lax.axis_index("dp")
    barrier, peers = greet(("ctx", "dp", "expert"))
    order = line_order(n)
    advance, finish, drain, steps = line_scatter(
        n, own_a, right_a, left_a, right_sems, left_sems, {j: i for i, j in enumerate(order)}
    )
    loads = {}
    for j in order:
        at = j * sides + side
        loads[j] = [
            pltpu.make_async_copy(gin_hbm.at[at], own_a.at[j], own_sems.at[0, j]),
            pltpu.make_async_copy(gout_hbm.at[at], own_b.at[j], own_sems.at[1, j]),
        ]
        for copy in loads[j]:
            copy.start()
    pl.semaphore_wait(barrier, peers)
    lanes, lane, core = expert_split()
    homes = [
        remote(
            far_ref.at[k - 1], far_in.at[k - 1], far_sems.at[0, k - 1], far_sems.at[1, k - 1],
            {"expert": lax.rem(lane - k + lanes, lanes) * 2 + core},
        )
        for k in range(1, lanes)
    ]
    for copy in homes:
        copy.start()
    lines[...] = bias_line(lax.broadcasted_iota(jnp.int32, (1, 2 * BLK), 1), table_ref[...])
    arriving = []
    for k in range(1, n):
        to = lax.rem(me + k, n)
        copy = remote(
            do_ref.at[pl.ds(pl.multiple_of(to * group, 16), group)], do_in.at[me], do_sems.at[0, k - 1], do_sems.at[1, k - 1], {"ctx": to}
        )
        copy.start()
        arriving.append(copy)
    beside = {}
    for v, gone, taken in ((0, gin_hbm, side_a), (1, gout_hbm, side_b)):
        for j in order:
            beside[v, j] = []
            for k in range(1, sides):
                to = lax.rem(side + k, sides)
                beside[v, j].append(
                    remote(
                        gone.at[j * sides + to], taken.at[k - 1, j],
                        side_sems.at[0, v, k - 1, j], side_sems.at[1, v, k - 1, j], {"dp": to},
                    )
                )
                beside[v, j][-1].start()

    def sum_sides(v, j):
        own, taken = ((own_a, side_a), (own_b, side_b))[v]
        loads[j][v].wait()
        total = own[j].astype(f32)
        for k in range(1, sides):
            beside[v, j][k - 1].wait_recv()
            total = total + taken[k - 1, j].astype(f32)
        own[j] = total.astype(bf16)

    do_in[me] = do_ref[pl.ds(pl.multiple_of(me * group, 16), group), :]

    for copy in arriving:
        copy.wait_recv()

    def out_copy(h, kind, k):
        to = lax.rem(me + k, n)
        base = pl.multiple_of(h * size, size)
        return remote(
            g_ref.at[to, pl.ds(kind * group + base, size)],
            cots_ref.at[pl.ds(pl.multiple_of(kind * n * group + me * group + base, 16), size)],
            out_sems.at[0, h, kind, k - 1],
            out_sems.at[1, h, kind, k - 1],
            {"ctx": to},
        )

    def head(h, carry):
        base = pl.multiple_of(h * size, size)
        for s in range(n):
            at = slice(s * rows, (s + 1) * rows)
            q = x_ref[s, pl.ds(base, size), :] * jnp.asarray(0.125, bf16)
            k = x_ref[s, pl.ds(base + group, size), :]
            v = x_ref[s, pl.ds(base + 2 * group, size), :]
            d = do_in[s, pl.ds(base, size), :]
            seg = x_ref[s, 3 * group : 3 * group + 16, :]
            mask, hot = seg_mask_rows(seg)
            which = lax.broadcasted_iota(jnp.int32, (16, rows), 0)

            def rows3(vec):
                hi, mid, lo = split3(jnp.broadcast_to(vec, (16, rows)))
                return jnp.where(which == 0, hi, jnp.where(which == 1, mid, jnp.where(which == 2, lo, jnp.zeros((), bf16))))

            ones = jnp.where(which < 3, 1.0, 0.0).astype(bf16)
            zeros = jnp.zeros((32, rows), bf16)
            zeros48 = jnp.zeros((48, rows), bf16)
            lse = lse_ref[pl.ds(h, 1), at]
            delta = jnp.sum(of_ref[pl.ds(base, size), at] * d.astype(f32), axis=0, keepdims=True)
            qt = jnp.concatenate([q, mask, rows3(-lse), zeros], axis=0)
            qa[:, at] = qt
            qn[at, :] = qt.T
            ka[at, :] = jnp.concatenate([k, hot, ones, zeros], axis=0).T
            dt = jnp.concatenate([d, rows3(-delta), zeros48], axis=0)
            da[:, at] = dt
            dn[at, :] = dt.T
            va[at, :] = jnp.concatenate([v, ones, zeros48], axis=0).T
        line = jnp.broadcast_to(lines[pl.ds(me * heads + h, 1), :], (BLK, 2 * BLK))
        rolled = pltpu.roll(line, 0, 1, stride=1, stride_axis=0)
        r = lax.broadcasted_iota(jnp.int32, (BLK, 2 * BLK), 0)
        c = lax.broadcasted_iota(jnp.int32, (BLK, 2 * BLK), 1)
        bias[...] = jnp.where(c < r, NEG, rolled)
        gsum[...] = jnp.zeros_like(gsum)
        for j in range(length // BLK):
            a0 = j * BLK
            kj = ka[a0 : a0 + BLK, :]
            vj = va[a0 : a0 + BLK, :]
            src, off = a0 // rows, a0 % rows
            kt = x_ref[src, pl.ds(base + group, size), off : off + BLK]
            dk = dv = None
            for a in range(a0, length, 2 * BLK):
                b = min(a + 2 * BLK, length)
                s = dot(kj, qa[:, a:b])
                if a == a0:
                    s = s + bias[:, : b - a]
                p = jnp.exp(s)
                ds = p * dot(vj, da[:, a:b])
                if a == a0:
                    gsum[:, : b - a] += ds
                p_low, ds_low = p.astype(bf16), ds.astype(bf16)
                u = dot(p_low, dn[a:b, :])
                dv = u if dv is None else dv + u
                u = dot(ds_low, qn[a:b, :])
                dk = u if dk is None else dk + u
                u = dot(kt, ds_low)
                if j == 0:
                    dq[:, a:b] = u
                else:
                    dq[:, a:b] += u
            g_ref[src, pl.ds(base + group, size), off : off + BLK] = dk.T[:size].astype(bf16)
            g_ref[src, pl.ds(base + 2 * group, size), off : off + BLK] = dv.T[:size].astype(bf16)
        for s in range(n):
            g_ref[s, pl.ds(base, size), :] = (dq[:, s * rows : (s + 1) * rows] * 0.125).astype(bf16)
        for kind in range(3):
            for k in range(1, n):
                out_copy(h, kind, k).start()
            cots_ref[pl.ds(pl.multiple_of(kind * n * group + me * group + base, 16), size), :] = g_ref[
                me, pl.ds(kind * group + base, size), :
            ]
        eight = gsum[0:8, :]
        for i in range(1, BLK // 8):
            eight = eight + pltpu.roll(gsum[8 * i : 8 * i + 8, :], 2 * BLK - 8 * i, 1)
        line = eight[0:1]
        for i in range(1, 8):
            line = line + pltpu.roll(eight, 2 * BLK - i, 1)[i : i + 1]
        diag_ref[pl.ds(h, 1), :] = line
        return carry

    lax.fori_loop(0, 1, head, 0)
    sum_sides(0, order[0])
    advance(0)
    lax.fori_loop(1, heads, head, 0)
    for step in range(1, steps):
        if step < n:
            sum_sides(0, order[step])
        advance(step)
        if step >= n and step - n < n:
            sum_sides(1, order[step - n])
    for i in range(max(steps - n, 0), n):
        sum_sides(1, order[i])
    mixture = base_ref[...]
    for k in range(1, lanes):
        homes[k - 1].wait()
        mixture = mixture + far_in[k - 1].astype(f32)
    out_ref[...] = mixture.astype(bf16)
    finish(ein_ref)
    for h in range(heads):
        for kind in range(3):
            for k in range(1, n):
                out_copy(h, kind, k).wait()
    for copy in arriving:
        copy.wait_send()
    for copies in beside.values():
        for copy in copies:
            copy.wait_send()
    drain()


def back_pass(x, do, table, of, lse, base, far, gin, gout):
    n, depth, rows = x.shape
    heads = table.shape[0] // n
    group = heads * 64
    length = n * rows
    sides = lax.axis_size("dp")
    _, high_a, wide_a = gin.shape
    _, high_b, wide_b = gout.shape
    vmem = pl.BlockSpec(memory_space=pltpu.VMEM)
    hbm = pl.BlockSpec(memory_space=pl.ANY)
    dma = pltpu.SemaphoreType.DMA
    some = max(sides - 1, 1)
    return pl.pallas_call(
        partial(back_kernel, heads, n, rows),
        out_shape=[
            jax.ShapeDtypeStruct((3 * n * group, rows), bf16),
            jax.ShapeDtypeStruct((heads, 2 * BLK), f32),
            jax.ShapeDtypeStruct((high_a, wide_a), bf16),
            jax.ShapeDtypeStruct((n, high_b, wide_b), bf16),
            jax.ShapeDtypeStruct(base.shape, bf16),
        ],
        in_specs=[vmem] * 7 + [hbm] * 2,
        out_specs=[vmem] * 5,
        scratch_shapes=[
            pltpu.VMEM((n, group, rows), bf16),
            pltpu.VMEM((n, 3 * group, rows), bf16),
            pltpu.VMEM((128, length), bf16),
            pltpu.VMEM((length, 128), bf16),
            pltpu.VMEM((length, 128), bf16),
            pltpu.VMEM((128, length), bf16),
            pltpu.VMEM((length, 128), bf16),
            pltpu.VMEM((length, 128), bf16),
            pltpu.VMEM((BLK, 2 * BLK), f32),
            pltpu.VMEM((64, length), f32),
            pltpu.VMEM((BLK, 2 * BLK), f32),
            pltpu.VMEM((n, high_a, wide_a), bf16),
            pltpu.VMEM((some, n, high_a, wide_a), bf16),
            pltpu.VMEM((some, n, high_b, wide_b), bf16),
            pltpu.VMEM((n, high_a, wide_a), bf16),
            pltpu.VMEM((n, high_a, wide_a), bf16),
            dma((2, n - 1)),
            dma((2, heads, 3, n - 1)),
            dma((2, n)),
            dma((2, 2, some, n)),
            dma((2, n)),
            dma((2, n)),
            pltpu.VMEM((table.shape[0], 2 * BLK), f32),
            pltpu.VMEM(far.shape, bf16),
            dma((2, far.shape[0])),
        ],
        compiler_params=pltpu.CompilerParams(
            collective_id=3, has_side_effects=True, vmem_limit_bytes=60 * 1024 * 1024
        ),
        name="back_pass",
    )(x, do, table, of, lse, base, far, gin, gout)


def add_all(parts):
    return functools.reduce(lambda a, b: a + b, parts)


def axis_stages():
    experts = lax.axis_size("expert")
    me = lax.axis_index("expert")
    core, lane = lax.rem(me, 2), lax.div(me, 2)
    return {
        "core": (2, core, lambda j: {"expert": lane * 2 + j}),
        "lane": (experts // 2, lane, lambda j: {"expert": j * 2 + core}),
        "dp": (lax.axis_size("dp"), lax.axis_index("dp"), lambda j: {"dp": j}),
        "ctx": (lax.axis_size("ctx"), lax.axis_index("ctx"), lambda j: {"ctx": j}),
    }


ORDERS = (("core", "lane", "dp", "ctx"), ("core", "dp", "lane", "ctx"))
SLICES = 2


def sum_plan(sizes, rows):
    plans = []
    for order in ORDERS:
        length, plan = rows // 2, []
        for name in order:
            count = sizes[name]
            split = length % count == 0 and (length // count) % 16 == 0
            plan.append((name, count, length, split))
            if split:
                length = length // count
        plans.append(plan)
    return plans


def received_rows(plans):
    return [
        [(count - 1) * (length // count if split else length) for (_, count, length, split) in plan]
        for plan in plans
    ]


def sizes_of():
    return {
        "core": 2,
        "lane": lax.axis_size("expert") // 2,
        "dp": lax.axis_size("dp"),
        "ctx": lax.axis_size("ctx"),
    }


def tail_kernel(
    plans, normed_t, cots, mixed_t, wq, wk, wv, x_ref, gain_ref, hidden_cot_ref, moe_small_ref, diag_ref, sums_ref,
    grads_ref, input_grad_ref, small_out_ref, eout_ref,
    acc, whole, taken_a, taken_b, small, small_taken, send, recv, back_send, back_recv, small_send, small_recv,
    right, left, right_sems, left_sems,
):
    stages = axis_stages()
    width = wq.shape[0]
    rows = x_ref.shape[0]
    barrier = pltpu.get_barrier_semaphore()
    peers = 0
    for name, (count, me, at) in stages.items():
        for k in range(1, count):
            pl.semaphore_signal(barrier, inc=1, device_id=at(lax.rem(me + k, count)), device_id_type=pl.DeviceIdType.MESH)
            peers += 1

    def make(k):
        if k < 3:
            acc[k * width : (k + 1) * width, :] = dot(
                normed_t[...], cots[k * width : (k + 1) * width, :], NT
            ).astype(bf16)
        else:
            acc[3 * width :, :] = dot(mixed_t[...], hidden_cot_ref[...].astype(bf16)).astype(bf16)

    taken = (taken_a, taken_b)
    half = 2 * width
    piece = width // SLICES
    parts = [(h, c) for c in range(SLICES) for h in range(2)]
    spans = {}
    for part in parts:
        spans[part] = [part[0] * half]

    def columns(part):
        return pl.ds(part[1] * piece, piece)

    def rows_at(start, size):
        return pl.ds(pl.multiple_of(start, 16), size)

    flying = {}

    def send_stage(part, step):
        h, c = part
        name, count, length, split = plans[h][step]
        _, me, at = stages[name]
        start = spans[part][-1]
        size = length // count if split else length
        base = sum(received[h][:step])
        copies = []
        for k in range(1, count):
            peer = lax.rem(me + k, count)
            copies.append(
                pltpu.make_async_remote_copy(
                    src_ref=acc.at[rows_at(start + peer * size if split else start, size), columns(part)],
                    dst_ref=taken[h].at[pl.ds(base + (k - 1) * size, size), columns(part)],
                    send_sem=send.at[h * SLICES + c, step, k - 1],
                    recv_sem=recv.at[h * SLICES + c, step, k - 1],
                    device_id=at(peer),
                    device_id_type=pl.DeviceIdType.MESH,
                )
            )
        for copy in copies:
            copy.start()
        flying[part] = copies

    def add_stage(part, step):
        h, c = part
        name, count, length, split = plans[h][step]
        _, me, at = stages[name]
        size = length // count if split else length
        start = spans[part][-1] + me * size if split else spans[part][-1]
        base = sum(received[h][:step])
        for copy in flying[part]:
            copy.wait()
        total = acc[rows_at(start, size), columns(part)].astype(f32)
        for k in range(1, count):
            total = total + taken[h][base + (k - 1) * size : base + k * size, columns(part)].astype(f32)
        if step == len(plans[h]) - 1:
            whole[rows_at(start, size), columns(part)] = total.astype(bf16)
        else:
            acc[rows_at(start, size), columns(part)] = total.astype(bf16)
        spans[part].append(start)

    def give_stage(part, step):
        h, c = part
        name, count, length, split = plans[h][step]
        if not split:
            flying[part] = []
            return
        _, me, at = stages[name]
        size = length // count
        start = spans[part][step + 1]
        copies = []
        for k in range(1, count):
            peer = lax.rem(me + k, count)
            copies.append(
                pltpu.make_async_remote_copy(
                    src_ref=whole.at[rows_at(start, size), columns(part)],
                    dst_ref=whole.at[rows_at(start, size), columns(part)],
                    send_sem=back_send.at[h * SLICES + c, step, k - 1],
                    recv_sem=back_recv.at[h * SLICES + c, step, k - 1],
                    device_id=at(peer),
                    device_id_type=pl.DeviceIdType.MESH,
                )
            )
        for copy in copies:
            copy.start()
        flying[part] = copies

    n = sums_ref.shape[0]
    advance, finish, drain, line_steps = line_scatter(n, sums_ref, right, left, right_sems, left_sems, [0] * n)
    received = received_rows(plans)
    make(2)
    make(3)
    pl.semaphore_wait(barrier, peers)
    for c in range(SLICES):
        send_stage((1, c), 0)
    advance(0)
    make(0)
    make(1)
    for c in range(SLICES):
        send_stage((0, c), 0)
    parts = [(1, 0), (0, 0), (1, 1), (0, 1)]

    turned = dot(wq[...], cots[:width, :]) + dot(wk[...], cots[width : 2 * width, :]) + dot(wv[...], cots[2 * width :, :])
    cot = turned.T
    x = x_ref[...].astype(f32)
    gain = gain_ref[...].reshape(1, width)
    scale = lax.rsqrt(jnp.mean(x * x, axis=1, keepdims=True) + EPSILON)
    unit = x * scale
    gained = cot * gain
    input_grad_ref[...] = hidden_cot_ref[...] + scale * (gained - unit * jnp.mean(unit * gained, axis=1, keepdims=True))
    gain_grad = jnp.sum(unit * cot, axis=0, keepdims=True)
    which = lax.broadcasted_iota(jnp.int32, (8, width), 0)
    low = jnp.where(which == 0, gain_grad, jnp.where(which == 1, moe_small_ref[0:8, :], 0.0))
    distance = lax.broadcasted_iota(jnp.int32, (2 * BLK, width), 0)
    lane = lax.broadcasted_iota(jnp.int32, (2 * BLK, width), 1)
    far = jnp.full(distance.shape, BUCKETS // 2, jnp.int32)
    for limit in THRESHOLDS:
        far = far + jnp.where(distance >= limit, 1, 0)
    bucket = jnp.where(distance < BUCKETS // 2, distance, far)
    own = distance < THRESHOLDS[-1]
    which = lax.broadcasted_iota(jnp.int32, (8, width), 0)
    lane_row = lax.broadcasted_iota(jnp.int32, (8, width), 1)
    heads = diag_ref.shape[0]
    for h in range(heads):
        at = lax.axis_index("ctx") * heads + h
        start = lax.div(at, 6) * 128
        hot = jnp.where(own & (bucket + start == lane), 1.0, 0.0).astype(bf16)
        three = split3(jnp.broadcast_to(diag_ref[h : h + 1, :], (16, 2 * BLK)))
        near = (dot(three[0], hot) + dot(three[1], hot) + dot(three[2], hot))[0:1]
        near = jnp.where(lane_row[0:1] == start + BUCKETS - 1, -jnp.sum(near, axis=1, keepdims=True), near)
        low = low + jnp.where(which == 2 + lax.rem(at, 6), near, 0.0)
    small[0:8, :] = low
    small[8:16, :] = moe_small_ref[8:16, :]

    def send_small(step):
        name = ORDERS[0][step]
        count, me, at = stages[name]
        base = sum(stages[n][0] - 1 for n in ORDERS[0][:step])
        copies = [
            pltpu.make_async_remote_copy(
                src_ref=small,
                dst_ref=small_taken.at[base + k - 1],
                send_sem=small_send.at[base + k - 1],
                recv_sem=small_recv.at[base + k - 1],
                device_id=at(lax.rem(me + k, count)),
                device_id_type=pl.DeviceIdType.MESH,
            )
            for k in range(1, count)
        ]
        for copy in copies:
            copy.start()
        flying["small"] = copies

    def add_small(step):
        base = sum(stages[n][0] - 1 for n in ORDERS[0][:step])
        for copy in flying["small"]:
            copy.wait()
        total = small[...]
        for k in range(len(flying["small"])):
            total = total + small_taken[base + k]
        small[...] = total

    last = len(ORDERS[0])
    send_small(0)
    for step in range(last):
        for part in parts:
            add_stage(part, step)
            if step + 1 < last:
                send_stage(part, step + 1)
            else:
                give_stage(part, step)
        add_small(step)
        if step + 1 < last:
            send_small(step + 1)
        advance(step + 1)
    small_out_ref[...] = small[...]
    for step in range(last - 1, -1, -1):
        for part in parts:
            for copy in flying[part]:
                copy.wait()
            if step > 0:
                give_stage(part, step - 1)
    for step in range(last + 1, line_steps):
        advance(step)
    finish(eout_ref)
    drain()
    grads_ref[...] = whole[...]


def tail_pass(normed_t, cots, mixed_t, wq, wk, wv, x, gain, hidden_cot, moe_small, diag, sums):
    rows, width = x.shape
    sizes = sizes_of()
    plans = sum_plan(sizes, 4 * width)
    received = [sum(r) for r in received_rows(plans)]
    most = max(sizes.values()) - 1
    few = sum(n - 1 for n in sizes.values())
    small = jax.ShapeDtypeStruct((16, width), f32)
    return pl.pallas_call(
        partial(tail_kernel, plans),
        out_shape=[
            jax.ShapeDtypeStruct((4 * width, width), bf16),
            jax.ShapeDtypeStruct((rows, width), f32),
            jax.ShapeDtypeStruct(small.shape, f32),
            jax.ShapeDtypeStruct(sums.shape[1:], bf16),
        ],
        in_specs=[pl.BlockSpec(memory_space=pltpu.VMEM)] * 12,
        out_specs=[pl.BlockSpec(memory_space=pltpu.VMEM)] * 4,
        scratch_shapes=[
            pltpu.VMEM((4 * width, width), bf16),
            pltpu.VMEM((4 * width, width), bf16),
            pltpu.VMEM((received[0], width), bf16),
            pltpu.VMEM((received[1], width), bf16),
            pltpu.VMEM(small.shape, f32),
            pltpu.VMEM((few,) + small.shape, f32),
            pltpu.SemaphoreType.DMA((2 * SLICES, 4, most)),
            pltpu.SemaphoreType.DMA((2 * SLICES, 4, most)),
            pltpu.SemaphoreType.DMA((2 * SLICES, 4, most)),
            pltpu.SemaphoreType.DMA((2 * SLICES, 4, most)),
            pltpu.SemaphoreType.DMA((few,)),
            pltpu.SemaphoreType.DMA((few,)),
            pltpu.VMEM(sums.shape, bf16),
            pltpu.VMEM(sums.shape, bf16),
            pltpu.SemaphoreType.DMA((2, sums.shape[0])),
            pltpu.SemaphoreType.DMA((2, sums.shape[0])),
        ],
        compiler_params=pltpu.CompilerParams(
            collective_id=0, has_side_effects=True, vmem_limit_bytes=56 * 1024 * 1024
        ),
        name="tail_pass",
    )(normed_t, cots, mixed_t, wq, wk, wv, x, gain, hidden_cot, moe_small, diag, sums)


def local(
    layer_input,
    cotangent,
    norm_gain_one,
    w_query,
    w_key,
    w_value,
    w_output,
    rel_table,
    norm_gain_two,
    w_router,
    w_expert_in,
    w_expert_out,
    segment_ids,
    routes,
    priority,
):
    rows, width = layer_input.shape[1:]
    heads = rel_table.shape[0]
    shards = lax.axis_size("ctx")
    experts = lax.axis_size("expert")
    capacity = min(rows, 5 * rows // (2 * experts))
    blocks = shards * lax.axis_size("dp")

    def padded(array):
        return jnp.pad(array, ((0, 0), (0, -array.shape[1] % 16), (0, 0)))

    held, mixed_t, attended_whole, lse, normed_t, info_all, cots_all, inner_weight, outer_weight = front_pass(
        layer_input[0], norm_gain_one, w_query, w_key, w_value, rel_table, segment_ids, routes[0].T, priority[0],
        cotangent[0], padded(w_expert_in)[0], padded(w_expert_out)[0],
    )
    inner_weight = inner_weight[:, : w_expert_in.shape[1]].reshape(width, -1)
    outer_weight = outer_weight[:, : w_expert_out.shape[1]].reshape(-1, width)
    router_t = jnp.pad(w_router.T, ((0, 16 - experts), (0, 0)))
    base, far, hidden_cot, mixed_cot, moe_small, inner_grad, outer_grad = moe_pass(
        capacity, mixed_t, w_output, layer_input[0], cotangent[0], norm_gain_two, router_t, info_all, cots_all, inner_weight, outer_weight
    )

    def cut(array):
        return padded(array.reshape(blocks, array.shape[0] // blocks, array.shape[1]))

    cots, diagonals, expert_in_grad, expert_out_sums, layer_output = back_pass(
        held, mixed_cot, rel_table, attended_whole, lse, base, far, cut(inner_grad), cut(outer_grad)
    )
    expert_in_grad = expert_in_grad[None, : w_expert_in.shape[1]]
    large, input_grad, small, expert_out_grad = tail_pass(
        normed_t, cots, mixed_t, w_query, w_key, w_value, layer_input[0], norm_gain_one, hidden_cot, moe_small, diagonals, expert_out_sums
    )
    expert_out_grad = expert_out_grad[None, : w_expert_out.shape[1]]
    large = large.reshape(4, width, width)
    return (
        layer_output[None],
        input_grad[None],
        small[0],
        large[0].astype(f32),
        large[1].astype(f32),
        large[2].astype(f32),
        large[3].astype(f32),
        jnp.concatenate([small[2:8, a : a + BUCKETS] for a in range(0, heads * 128 // 6, 128)], axis=0),
        small[1],
        small[8 : 8 + experts].T,
        expert_in_grad.astype(f32),
        expert_out_grad.astype(f32),
    )


def solution(mesh):
    placed = (
        P(("expert", "dp"), "ctx", None),
        P(("expert", "dp"), "ctx", None),
        P(),
        P(),
        P(),
        P(),
        P(),
        P(),
        P(),
        P(),
        P("expert", ("ctx", "dp"), None),
        P("expert", ("ctx", "dp"), None),
        P(("expert", "dp"), "ctx"),
        P(("expert", "dp"), "ctx", None),
        P(("expert", "dp"), "ctx", None),
    )
    return jax.shard_map(
        local,
        mesh=mesh,
        in_specs=placed,
        out_specs=(
            P(("expert", "dp"), "ctx", None),
            P(("expert", "dp"), "ctx", None),
            P(),
            P(),
            P(),
            P(),
            P(),
            P(),
            P(),
            P(),
            P("expert", ("ctx", "dp"), None),
            P("expert", ("ctx", "dp"), None),
        ),
        check_vma=False,
    )
```

```python
import functools
from functools import partial

import jax
import jax.numpy as jnp
from jax import lax
from jax.experimental import pallas as pl
from jax.experimental.pallas import tpu as pltpu
from jax.sharding import PartitionSpec as P

bf16 = jnp.bfloat16
f32 = jnp.float32
HIGH_PRECISION = lax.Precision.HIGHEST
EPSILON = 1e-06
THRESHOLDS = (19, 21, 24, 27, 31, 35, 40, 46, 52, 59, 67, 77, 87, 99, 113)
BUCKETS=32
NEG=-1e30
BLK=256
NT=(((1,),(1,)),((),()))
TN=(((0,),(0,)),((),()))

def dot(a,b,dims=(((1,),(0,)),((),()))):
    return lax.dot_general(a,b,dims,preferred_element_type=f32)

def seg_mask_rows(seg):
    which = lax.broadcasted_iota(jnp.int32, seg.shape, 0).astype(f32)
    same = seg.astype(f32) == which
    return jnp.where(same, 0.0, NEG).astype(bf16), jnp.where(same, 1.0, 0.0).astype(bf16)

def split3(v):
    hi = v.astype(bf16); rest = v - hi.astype(f32)
    mid = rest.astype(bf16); rest = rest - mid.astype(f32)
    return hi, mid, rest.astype(bf16)

ROOT = 0.7978845608028654


def remote(src, dst, send_sem, recv_sem, where):
    return pltpu.make_async_remote_copy(
        src_ref=src,
        dst_ref=dst,
        send_sem=send_sem,
        recv_sem=recv_sem,
        device_id=where,
        device_id_type=pl.DeviceIdType.MESH,
    )


def expert_split():
    experts = lax.axis_size("expert")
    me = lax.axis_index("expert")
    return experts // 2, lax.div(me, 2), lax.rem(me, 2)


def gather_start(piece, whole, near_sems, far_sems, rows=None):
    lanes, lane, core = expert_split()
    me = lane * 2 + core
    view = whole.at[me] if rows is None else whole.at[me, rows]
    copies = [remote(piece, view, near_sems.at[0], near_sems.at[1], {"expert": lane * 2 + 1 - core})]
    for k in range(1, lanes):
        copies.append(
            remote(piece, view, far_sems.at[0, k - 1], far_sems.at[1, k - 1], {"expert": lax.rem(lane + k, lanes) * 2 + core})
        )
    for copy in copies:
        copy.start()
    return copies


def relay(k, whole, sems):
    lanes, lane, core = expert_split()
    source = lax.rem(lane - k + lanes, lanes) * 2 + core
    return remote(whole.at[source], whole.at[source], sems.at[0, k - 1], sems.at[1, k - 1], {"expert": lane * 2 + 1 - core})


def greet(names):
    barrier = pltpu.get_barrier_semaphore()
    total = 0
    for name in names:
        count, at = lax.axis_size(name), lax.axis_index(name)
        for k in range(1, count):
            pl.semaphore_signal(
                barrier, inc=1, device_id={name: lax.rem(at + k, count)}, device_id_type=pl.DeviceIdType.MESH
            )
        total += count - 1
    return barrier, total


def moe_kernel(
    capacity, mixed_t, w_output, x_ref, cot_ref, gain_ref, router_ref, info_ref, cots_hbm, inner_hbm, outer_hbm,
    base_ref, far_ref, hidden_cot_ref, mixed_cot_ref, small_ref, gin_hbm, gout_hbm,
    nt, cots, inner, outer, act_all, pre_all, rows_all, cots_all, made, back, part, pair_in, total,
    core_in, far_in, gate_out, gate_in,
    load_sems, cot_sems, near_sems, far_sems, relay_sems, pair_sems, core_sems, back_sems, gate_sems, stage_sems, free_sem, late_sems,
):
    experts = lax.axis_size("expert")
    lanes, lane, core = expert_split()
    me = lane * 2 + core
    other = lane * 2 + 1 - core
    rows, width = cot_ref.shape
    hidden = hidden_cot_ref
    pieces = 2
    step_rows = rows // pieces
    hidden_size = inner.shape[1]
    n = lax.axis_size("ctx")
    place_z = lax.axis_index("ctx")
    wide = hidden_size // n

    first = pltpu.make_async_copy(inner_hbm, inner, load_sems.at[n])
    first.start()

    def chunk_rows(j):
        return pl.ds(pl.multiple_of(j * wide, wide), wide)

    def chunk_at(f):
        return jnp.where(place_z == n - 1, n - 1 - f, f)

    def has(f):
        return (f < n - 1) | ((place_z > 0) & (place_z < n - 1))

    def load(f):
        at = chunk_rows(chunk_at(f))
        return pltpu.make_async_copy(outer_hbm.at[at], outer.at[at], load_sems.at[f])

    for f in range(n):
        @pl.when(has(f))
        def _():
            load(f).start()

    def late(up):
        at = chunk_rows(0 if up else n - 1)
        return remote(
            outer_hbm.at[at], outer.at[at], late_sems.at[0, int(up)], late_sems.at[1, int(up)],
            {"ctx": n - 1 if up else 0},
        )

    barrier, peers = greet(("expert", "ctx"))
    pl.semaphore_wait(barrier, peers)

    @pl.when(place_z == n - 2)
    def _():
        late(True).start()

    @pl.when(place_z == 1)
    def _():
        late(False).start()

    sent = []
    for p in range(pieces):
        at = slice(p * step_rows, (p + 1) * step_rows)
        now = x_ref[at, :].astype(f32) + dot(mixed_t[:, at], w_output[...], TN)
        hidden[at, :] = now
        scale = lax.rsqrt(jnp.mean(now * now, axis=1, keepdims=True) + EPSILON)
        nt[me, at, :] = (now * scale * gain_ref[...].reshape(1, width)).astype(bf16)
        sent.append(gather_start(nt.at[me, at], nt, near_sems.at[p], far_sems.at[p], at))

    def gate_rows(source):
        logits = dot(router_ref[...], nt[source], NT)
        which = lax.broadcasted_iota(jnp.int32, logits.shape, 0)
        info = info_ref[source]
        chosen = (which == info[0:1]) | (which == info[1:2])
        top = jnp.max(jnp.where(chosen, logits, NEG), axis=0, keepdims=True)
        power = jnp.where(chosen, jnp.exp(jnp.minimum(logits - top, 0.0)), 0.0)
        return power / jnp.sum(power, axis=0, keepdims=True)

    def pair_of(k):
        return [lax.rem(lane - k + lanes, lanes) * 2 + sc for sc in range(2)]

    order = pair_of(1) + [me, other]
    for k in range(2, lanes):
        order += pair_of(k)
    first_group = 4

    def fetch(i):
        return pltpu.make_async_copy(cots_hbm.at[order[i]], cots.at[i % first_group], cot_sems.at[i % first_group])

    for i in range(first_group):
        fetch(i).start()

    def place_of(i):
        info = info_ref[order[i]]
        place = jnp.where(info[0:1] == me, info[2:3], jnp.where(info[1:2] == me, info[3:4], -1))
        slot = lax.broadcasted_iota(jnp.int32, (capacity, rows), 0)
        pick = jnp.where(slot == place, 1.0, 0.0)
        gates = gate_rows(order[i])
        which = lax.broadcasted_iota(jnp.int32, gates.shape, 0)
        own_gate = jnp.sum(jnp.where(which == me, gates, 0.0), axis=0, keepdims=True)
        return place, pick, jnp.sum(pick * own_gate, axis=1, keepdims=True)

    def dispatch(i):
        fetch(i).wait()
        _, pick, slot_gate = place_of(i)
        block = slice(i * capacity, (i + 1) * capacity)
        rows_all[block, :] = dot(pick.astype(bf16), nt[order[i]]).astype(bf16)
        cots_all[block, :] = (slot_gate * dot(pick.astype(bf16), cots[i % first_group])).astype(bf16)
        made[i % first_group] = jnp.zeros((capacity, width), f32)
        back[i % first_group] = jnp.zeros((capacity, width), f32)

    def part_of(i, f):
        block = pl.ds(i * capacity if isinstance(i, int) else pl.multiple_of(i * capacity, 16), capacity)
        at = chunk_rows(chunk_at(f))
        turn = i % first_group if isinstance(i, int) else i
        pre = dot(rows_all[block, :], inner[:, at])
        cot = dot(cots_all[block, :], outer[at, :], NT)
        square = pre * pre
        t = jnp.tanh(pre * (ROOT + (ROOT * 0.044715) * square))
        half = 0.5 + 0.5 * t
        act = (pre * half).astype(bf16)
        slope = half + (0.5 * pre) * (1.0 - t * t) * (ROOT + (ROOT * 3 * 0.044715) * square)
        back_pre = (cot * slope).astype(bf16)
        act_all[block, at] = act
        pre_all[block, at] = back_pre
        made[turn] += dot(act, outer[at, :])
        back[turn] += dot(back_pre, inner[:, at], NT)

    def finish_source(i, target):
        place, pick, slot_gate = place_of(i)
        outcome = made[i % first_group].astype(bf16).astype(f32)
        slot_cot = jnp.sum(dot(pick.astype(bf16), cots[i % first_group]) * outcome, axis=1, keepdims=True)
        gate_out[order[i]] = jnp.broadcast_to(jnp.sum(pick * slot_cot, axis=0, keepdims=True), (8, rows))
        column = jnp.broadcast_to(place.astype(f32), (128, rows)).T[:, 0:1]
        lane_at = lax.broadcasted_iota(jnp.int32, (rows, capacity), 1).astype(f32)
        put = jnp.where(lane_at == column, 1.0, 0.0).astype(bf16)
        target[0] = dot(put, back[i % first_group].astype(bf16)).astype(bf16)
        target[1] = dot(put, (slot_gate * outcome).astype(bf16)).astype(bf16)
        if i + first_group < len(order):
            fetch(i + first_group).start()

    def process(i, target):
        dispatch(i)

        def step(f, carry):
            part_of(i, f)
            return carry

        lax.fori_loop(0, n, step, 0)
        finish_source(i, target)

    def pair_copies(k, sc):
        return [
            remote(part.at[sc, v], pair_in.at[v], pair_sems.at[0, v, k - 1], pair_sems.at[1, v, k - 1], {"expert": other})
            for v in range(2)
        ]

    def home_copy(k, sc):
        to = lax.rem(lane - k + lanes, lanes) * 2 + sc
        return remote(part.at[sc, 0], far_in.at[k - 1], back_sems.at[0, k - 1], back_sems.at[1, k - 1], {"expert": to})

    def begin_pair(k, sc):
        @pl.when(core != sc)
        def _():
            if k > 1:
                pl.semaphore_wait(free_sem, 1)
            for copy in pair_copies(k, sc):
                copy.start()

    def end_pair(k, sc):
        @pl.when(core == sc)
        def _():
            pair = pair_copies(k, sc)
            pair[0].wait_recv()
            part[sc, 0] = (part[sc, 0].astype(f32) + pair_in[0].astype(f32)).astype(bf16)
            home_copy(k, sc).start()
            pair[1].wait_recv()
            far_ref[k - 1] = (part[sc, 1].astype(f32) + pair_in[1].astype(f32)).astype(bf16)
            if k + 1 < lanes:
                pl.semaphore_signal(
                    free_sem, inc=1, device_id={"expert": other}, device_id_type=pl.DeviceIdType.MESH
                )

    def pair_sent(k):
        for sc in range(2):
            @pl.when(core != sc)
            def _():
                for copy in pair_copies(k, sc):
                    copy.wait_send()

    def home_sent(k):
        for sc in range(2):
            @pl.when(core == sc)
            def _():
                home_copy(k, sc).wait_send()

    dispatch(2)
    for p in range(pieces):
        sent[p][0].wait_recv()
    dispatch(3)
    first.wait()
    for f in range(n - 1):
        load(f).wait()

    def steps_of(start):
        def step(at, carry):
            part_of(start + lax.rem(at, 2), lax.div(at, 2))
            return carry

        return step

    lax.fori_loop(0, 2 * (n - 1), steps_of(2), 0)
    passed_on = []
    for k in range(1, lanes):
        for p in range(pieces):
            sent[p][k].wait_recv()
        passed = relay(k, nt, relay_sems)
        passed.start()
        passed_on.append(passed)

    def relayed(k, sc):
        @pl.when(core != sc)
        def _():
            passed_on[k - 1].wait_recv()

    for sc in range(2):
        relayed(1, sc)
        dispatch(sc)
    lax.fori_loop(0, 2 * (n - 1), steps_of(0), 0)

    @pl.when(has(n - 1))
    def _():
        load(n - 1).wait()

    @pl.when(place_z == n - 1)
    def _():
        late(True).wait_recv()

    @pl.when(place_z == 0)
    def _():
        late(False).wait_recv()

    lax.fori_loop(2 * (n - 1), 2 * n, steps_of(0), 0)
    finish_source(0, part.at[0])
    begin_pair(1, 0)
    finish_source(1, part.at[1])
    begin_pair(1, 1)
    end_pair(1, 0)
    lax.fori_loop(2 * (n - 1), 2 * n, steps_of(2), 0)
    end_pair(1, 1)
    pair_sent(1)
    finish_source(3, part.at[1 - core])
    core_copies = [
        remote(part.at[1 - core, v], core_in.at[v], core_sems.at[0, v], core_sems.at[1, v], {"expert": other}) for v in range(2)
    ]
    for copy in core_copies:
        copy.start()
    finish_source(2, total)

    def gate_copy(k):
        to = lax.rem(me + k, experts)
        return remote(gate_out.at[to], gate_in.at[me], gate_sems.at[0, k - 1], gate_sems.at[1, k - 1], {"expert": to})

    for k in range(2, lanes):
        if k == 2:
            for copy in core_copies:
                copy.wait_send()
        home_sent(k - 1)
        for sc in range(2):
            relayed(k, sc)
            process(2 * k + sc, part.at[sc])
            begin_pair(k, sc)
        for sc in range(2):
            end_pair(k, sc)
        pair_sent(k)
    gate_copies = [gate_copy(k) for k in range(1, experts)]
    for copy in gate_copies:
        copy.start()
    count = rows_all.shape[0]
    for b in range(count // 128):
        at = slice(b * 128, (b + 1) * 128)
        inner[:, at] = rows_all[at, :].T
        inner[:, slice(count + b * 128, count + (b + 1) * 128)] = cots_all[at, :].T
    wide = width
    steps = hidden_size // wide

    def store(f, v):
        at = pl.ds(pl.multiple_of(f * wide, wide), wide)
        return pltpu.make_async_copy(outer.at[v * width : (v + 1) * width], gin_hbm.at[:, at] if v == 0 else gout_hbm.at[at, :], stage_sems.at[v])

    def grads(f, carry):
        at = pl.ds(pl.multiple_of(f * wide, wide), wide)

        @pl.when(f > 0)
        def _():
            store(f - 1, 0).wait()

        outer[:width, :] = dot(inner[:, :count], pre_all[:, at]).astype(bf16)
        store(f, 0).start()

        @pl.when(f > 0)
        def _():
            store(f - 1, 1).wait()

        outer[width : 2 * width, :] = dot(inner[:, count : 2 * count], act_all[:, at]).astype(bf16).T
        store(f, 1).start()
        return carry

    lax.fori_loop(0, steps, grads, 0)
    for copy in gate_copies:
        copy.wait()
    gates = gate_rows(me)
    pad = gates.shape[0]
    which = lax.broadcasted_iota(jnp.int32, gates.shape, 0)
    gate_cot = jnp.where(which == me, gate_out[me][0:1], 0.0)
    for k in range(1, experts):
        source = lax.rem(me + k, experts)
        gate_cot = gate_cot + jnp.where(which == source, gate_in[source][0:1], 0.0)
    logit_cot = gates * (gate_cot - jnp.sum(gates * gate_cot, axis=0, keepdims=True))
    three = jnp.concatenate(split3(logit_cot), axis=0)
    router_three = jnp.concatenate([router_ref[...]] * 3, axis=0)
    router_grad = dot(three, nt[me])
    small_ref[8:, :] = router_grad[:pad] + router_grad[pad : 2 * pad] + router_grad[2 * pad :]
    for copy in core_copies:
        copy.wait_recv()
    for k in range(1, lanes):
        remote(part.at[0, 0], far_in.at[k - 1], back_sems.at[0, k - 1], back_sems.at[1, k - 1], {"expert": other}).wait_recv()
    gain = gain_ref[...].reshape(1, width)
    gain_grad = jnp.zeros((1, width), f32)
    for start in range(0, rows, 128):
        at = slice(start, start + 128)
        normed_cot = total[0, at, :].astype(f32) + core_in[0, at, :].astype(f32)
        for k in range(1, lanes):
            normed_cot = normed_cot + far_in[k - 1, at, :].astype(f32)
        normed_cot = normed_cot + dot(three[:, at], router_three, TN)
        now = hidden[at, :]
        scale = lax.rsqrt(jnp.mean(now * now, axis=1, keepdims=True) + EPSILON)
        unit = now * scale
        gained = normed_cot * gain
        hidden_cot = cot_ref[at, :].astype(f32) + scale * (gained - unit * jnp.mean(unit * gained, axis=1, keepdims=True))
        hidden_cot_ref[at, :] = hidden_cot
        mixed_cot_ref[:, at] = dot(w_output[...], hidden_cot.astype(bf16), NT).astype(bf16)
        gain_grad = gain_grad + jnp.sum(unit * normed_cot, axis=0, keepdims=True)
        base_ref[at, :] = now + (total[1, at, :].astype(f32) + core_in[1, at, :].astype(f32))
    small_ref[0:8, :] = jnp.broadcast_to(gain_grad, (8, width))
    store(steps - 1, 0).wait()
    store(steps - 1, 1).wait()
    home_sent(lanes - 1)
    if lanes == 2:
        for copy in core_copies:
            copy.wait_send()
    for copy in passed_on:
        copy.wait_send()
    for p in range(pieces):
        for copy in sent[p]:
            copy.wait_send()

    @pl.when(place_z == n - 2)
    def _():
        late(True).wait_send()

    @pl.when(place_z == 1)
    def _():
        late(False).wait_send()


def moe_pass(capacity, mixed_t, w_output, x, cot, gain, router, info, cots, inner, outer):
    rows, width = cot.shape
    experts = cots.shape[0]
    lanes = experts // 2
    hidden_size = inner.shape[1]
    total = experts * capacity
    vmem = pl.BlockSpec(memory_space=pltpu.VMEM)
    hbm = pl.BlockSpec(memory_space=pl.ANY)
    dma = pltpu.SemaphoreType.DMA
    far = max(lanes - 1, 1)
    return pl.pallas_call(
        partial(moe_kernel, capacity),
        out_shape=[
            jax.ShapeDtypeStruct((rows, width), f32),
            jax.ShapeDtypeStruct((far, rows, width), bf16),
            jax.ShapeDtypeStruct((rows, width), f32),
            jax.ShapeDtypeStruct((width, rows), bf16),
            jax.ShapeDtypeStruct((8 + router.shape[0], width), f32),
            jax.ShapeDtypeStruct((width, hidden_size), bf16),
            jax.ShapeDtypeStruct((hidden_size, width), bf16),
        ],
        in_specs=[vmem] * 7 + [hbm] * 3,
        out_specs=[vmem] * 5 + [hbm] * 2,
        scratch_shapes=[
            pltpu.VMEM((experts, rows, width), bf16),
            pltpu.VMEM((4, rows, width), bf16),
            pltpu.VMEM((width, hidden_size), bf16),
            pltpu.VMEM((hidden_size, width), bf16),
            pltpu.VMEM((total, hidden_size), bf16),
            pltpu.VMEM((total, hidden_size), bf16),
            pltpu.VMEM((total, width), bf16),
            pltpu.VMEM((total, width), bf16),
            pltpu.VMEM((4, capacity, width), f32),
            pltpu.VMEM((4, capacity, width), f32),
            pltpu.VMEM((2, 2, rows, width), bf16),
            pltpu.VMEM((2, rows, width), bf16),
            pltpu.VMEM((2, rows, width), bf16),
            pltpu.VMEM((2, rows, width), bf16),
            pltpu.VMEM((far, rows, width), bf16),
            pltpu.VMEM((experts, 8, rows), f32),
            pltpu.VMEM((experts, 8, rows), f32),
            dma((lax.axis_size("ctx") + 1,)),
            dma((4,)),
            dma((2, 2)),
            dma((2, 2, far)),
            dma((2, far)),
            dma((2, 2, far)),
            dma((2, 2)),
            dma((2, far)),
            dma((2, experts - 1)),
            dma((2,)),
            pltpu.SemaphoreType.REGULAR,
            dma((2, 2)),
        ],
        compiler_params=pltpu.CompilerParams(
            collective_id=1, has_side_effects=True, vmem_limit_bytes=65000 * 1024
        ),
        name="moe_pass",
    )(mixed_t, w_output, x, cot, gain, router, info, cots, inner, outer)


def bias_line(distance, table):
    far = jnp.full(distance.shape, BUCKETS // 2, jnp.int32)
    for limit in THRESHOLDS:
        far = far + jnp.where(distance >= limit, 1, 0)
    bucket = jnp.where(distance < BUCKETS // 2, distance, far)
    own = (distance >= 0) & (distance < THRESHOLDS[-1])
    which = lax.broadcasted_iota(jnp.int32, (BUCKETS, distance.shape[1]), 0)
    hot = jnp.where(own & (which == bucket), 1.0, 0.0).astype(bf16)
    last = table[:, BUCKETS - 1 :].astype(f32)
    return dot(table, hot) - jnp.where(own, last, 0.0)


def column_of(row):
    return jnp.broadcast_to(row, (128, row.shape[1])).T


def front_kernel(
    heads, n, rows, x_ref, gain_ref, wq, wk, wv, table_ref, segment_ref, routes_ref, order_ref, cot_hbm, win_hbm, wout_hbm,
    held, mixed, of_ref, lse_ref, normed_t, infos, cots_hbm, win_all, wout_all,
    made, given, qa, ka, vn, bias, s_ref, lines,
    held_sems, mixed_sems, near_sems, far_sems, relay_sems, info_sems, own_sems, line_sems, side_sems,
):
    size = 64
    group = heads * size
    width = n * group
    length = n * rows
    sides = lax.axis_size("dp")
    me = lax.axis_index("ctx")
    side = lax.axis_index("dp")
    experts = lax.axis_size("expert")
    expert = lax.axis_index("expert")
    barrier = pltpu.get_barrier_semaphore()
    for name, count, at in (("ctx", n, me), ("dp", sides, side), ("expert", experts, expert)):
        for k in range(1, count):
            pl.semaphore_signal(
                barrier, inc=1, device_id={name: lax.rem(at + k, count)}, device_id_type=pl.DeviceIdType.MESH
            )
    owns = [
        pltpu.make_async_copy(cot_hbm, cots_hbm.at[expert], own_sems.at[0]),
        pltpu.make_async_copy(win_hbm, win_all.at[me * sides + side], own_sems.at[1]),
        pltpu.make_async_copy(wout_hbm, wout_all.at[me * sides + side], own_sems.at[2]),
    ]
    for copy in owns:
        copy.start()
    pl.semaphore_wait(barrier, n + sides + experts - 3)
    shard = (win_hbm, wout_hbm)
    whole = (win_all, wout_all)

    def along(way, s, v):
        j = me - s if way == 0 else me + s
        to = me + 1 if way == 0 else me - 1
        at = j * sides + side
        source = shard[v] if s == 0 else whole[v].at[at]
        return remote(source, whole[v].at[at], line_sems.at[0, way, v, s], line_sems.at[1, way, v, s], {"ctx": to})

    def across(way, s, v):
        j = me - s if way == 0 else me + s
        at = j * sides + side
        source = shard[v] if s == 0 else whole[v].at[at]
        return [
            remote(
                source, whole[v].at[at], side_sems.at[0, way, v, k - 1, s], side_sems.at[1, way, v, k - 1, s],
                {"dp": lax.rem(side + k, sides)},
            )
            for k in range(1, sides)
        ]

    def holds(way, s):
        return me - s >= 0 if way == 0 else me + s < n

    def passes(way, s, v):
        if v == 1 and s == n - 2:
            return None
        return (me - s >= 0) & (me < n - 1) if way == 0 else (me + s < n) & (me > 0)

    def advance(s, v):
        for way in range(2):
            if s > 0:
                @pl.when(holds(way, s))
                def _():
                    along(way, s - 1, v).wait_recv()

            if passes(way, s, v) is not None:
                @pl.when(passes(way, s, v))
                def _():
                    along(way, s, v).start()

            if s > 0:
                @pl.when(holds(way, s))
                def _():
                    for copy in across(way, s, v):
                        copy.start()

    for v in range(2):
        for copy in across(0, 0, v):
            copy.start()
        advance(0, v)
    sent = gather_start(cot_hbm, cots_hbm, near_sems, far_sems)

    x = x_ref[...].astype(f32)
    normed = x * lax.rsqrt(jnp.mean(x * x, axis=1, keepdims=True) + EPSILON) * gain_ref[...].reshape(1, width)
    normed = normed.astype(bf16)
    held_copies = []
    here = pl.ds(pl.multiple_of(me * group, 16), group)
    seg = jnp.broadcast_to(segment_ref[...].astype(f32), (16, rows)).astype(bf16)
    made[3, 0:16, :] = seg
    held[me, 3 * group : 3 * group + 16, :] = seg
    for kind, weight in enumerate((wq, wk, wv)):
        made[kind] = dot(normed, weight[...]).astype(bf16).T
        for k in range(1, n):
            to = lax.rem(me + k, n)
            copy = remote(
                made.at[kind, pl.ds(pl.multiple_of(to * group, 16), group)],
                held.at[me, kind * group : (kind + 1) * group],
                held_sems.at[0, kind, k - 1], held_sems.at[1, kind, k - 1], {"ctx": to},
            )
            copy.start()
            held_copies.append(copy)
        held[me, kind * group : (kind + 1) * group, :] = made[kind, here, :]
    for k in range(1, n):
        copy = remote(
            made.at[3, 0:16], held.at[me, 3 * group : 3 * group + 16], held_sems.at[0, 3, k - 1], held_sems.at[1, 3, k - 1],
            {"ctx": lax.rem(me + k, n)},
        )
        copy.start()
        held_copies.append(copy)
    normed_t[...] = normed.T

    order_row = order_ref[...].astype(f32)
    before = jnp.where(column_of(order_row)[:, 0:1] < order_row, 1.0, 0.0).astype(bf16)
    kinds = 16
    which = lax.broadcasted_iota(jnp.int32, (kinds, rows), 0)
    chosen = [routes_ref[c : c + 1, :] for c in range(2)]
    hot = [jnp.where(which == c, 1.0, 0.0) for c in chosen]
    ahead = [dot(h.astype(bf16), before) for h in hot]
    firsts = jnp.sum(hot[0], axis=1, keepdims=True)
    slots = [jnp.sum(hot[0] * ahead[0], axis=0, keepdims=True), jnp.sum(hot[1] * (ahead[1] + firsts), axis=0, keepdims=True)]
    infos[expert] = jnp.concatenate(chosen + [s.astype(jnp.int32) for s in slots] + [jnp.zeros((4, rows), jnp.int32)], axis=0)
    info_copies = [
        remote(infos.at[expert], infos.at[expert], info_sems.at[0, k - 1], info_sems.at[1, k - 1], {"expert": lax.rem(expert + k, experts)})
        for k in range(1, experts)
    ]
    for copy in info_copies:
        copy.start()
    lines[...] = bias_line(BLK - lax.broadcasted_iota(jnp.int32, (1, 2 * BLK), 1), table_ref[...])

    advance(1, 0)
    advance(1, 1)
    advance(2, 0)
    for copy in held_copies:
        copy.wait_recv()

    def mixed_copy(h, k):
        to = lax.rem(me + k, n)
        base = pl.multiple_of(h * size, size)
        return remote(
            given.at[to, pl.ds(base, size)], mixed.at[pl.ds(pl.multiple_of(me * group + base, 16), size)],
            mixed_sems.at[0, h, k - 1], mixed_sems.at[1, h, k - 1], {"ctx": to},
        )

    def head(h, carry):
        base = pl.multiple_of(h * size, size)
        for s in range(n):
            at = slice(s * rows, (s + 1) * rows)
            q = held[s, pl.ds(base, size), :]
            k = held[s, pl.ds(base + group, size), :]
            v = held[s, pl.ds(base + 2 * group, size), :]
            mask, hot = seg_mask_rows(held[s, 3 * group : 3 * group + 16, :])
            zeros = jnp.zeros((48, rows), bf16)
            qa[at, :] = jnp.concatenate([q * jnp.asarray(0.125, bf16), mask, zeros], axis=0).T
            ka[:, at] = jnp.concatenate([k, hot, zeros], axis=0)
            vn[at, :] = jnp.concatenate([v, jnp.zeros((64, rows), bf16)], axis=0).T
        line = jnp.broadcast_to(lines[pl.ds(me * heads + h, 1), :], (BLK, 2 * BLK))
        rolled = pltpu.roll(line, 0, 1, stride=1, stride_axis=0)
        r = lax.broadcasted_iota(jnp.int32, (BLK, 2 * BLK), 0)
        c = lax.broadcasted_iota(jnp.int32, (BLK, 2 * BLK), 1)
        bias[...] = jnp.where(c - r > BLK, NEG, rolled)
        for t in range(length // BLK):
            qt = qa[t * BLK : (t + 1) * BLK, :]
            near0 = max(t - 1, 0) * BLK
            end = (t + 1) * BLK
            chunks = [(near0, end)] + [(a, min(a + 2 * BLK, near0)) for a in range(0, near0, 2 * BLK)]
            top = None
            for a, b in chunks:
                s = dot(qt, ka[:, a:b])
                if a == near0:
                    s = s + bias[:, 2 * BLK - (b - a) :]
                s_ref[:, a:b] = s
                part = s[:, :128]
                for i in range(1, (b - a) // 128):
                    part = jnp.maximum(part, s[:, i * 128 : (i + 1) * 128])
                top = part if top is None else jnp.maximum(top, part)
            m = jnp.max(top, axis=1, keepdims=True)
            total = None
            o = None
            for a, b in chunks:
                p = jnp.exp(s_ref[:, a:b] - m)
                part = p[:, :128]
                for i in range(1, (b - a) // 128):
                    part = part + p[:, i * 128 : (i + 1) * 128]
                total = part if total is None else total + part
                u = dot(p.astype(bf16), vn[a:b, :])
                o = u if o is None else o + u
            l = jnp.sum(total, axis=1, keepdims=True)
            o = o / l
            lane = lax.broadcasted_iota(jnp.int32, (BLK, 128), 1)
            o = jnp.where(lane == 64, m + jnp.log(l), o)
            ot = o.T
            src, off = (t * BLK) // rows, (t * BLK) % rows
            given[src, pl.ds(base, size), off : off + BLK] = ot[:size].astype(bf16)
            of_ref[pl.ds(base, size), t * BLK : (t + 1) * BLK] = ot[:size]
            lse_ref[pl.ds(h, 1), t * BLK : (t + 1) * BLK] = ot[size : size + 1]
        for k in range(1, n):
            mixed_copy(h, k).start()
        mixed[pl.ds(pl.multiple_of(me * group + base, 16), size), :] = given[me, pl.ds(base, size), :]

        @pl.when(h == 0)
        def _():
            advance(2, 1)

        @pl.when(h == 1)
        def _():
            for s in range(3, n):
                advance(s, 0)

        return carry

    lax.fori_loop(0, heads, head, 0)
    relays = []
    for k in range(1, experts // 2):
        sent[k].wait_recv()
        passed = relay(k, cots_hbm, relay_sems)
        passed.start()
        relays.append(passed)
    sent[0].wait_recv()
    for h in range(heads):
        for k in range(1, n):
            mixed_copy(h, k).wait()
    for copy in held_copies + sent:
        copy.wait_send()
    for copy in relays + info_copies + owns:
        copy.wait()
    for v in range(2):
        for s in range(n):
            for way in range(2):
                if v == 1 and s == n - 1:
                    continue
                if passes(way, s, v) is not None:
                    @pl.when(passes(way, s, v))
                    def _():
                        along(way, s, v).wait_send()

                if s > 0 or way == 0:
                    @pl.when(holds(way, s))
                    def _():
                        for copy in across(way, s, v):
                            copy.wait()


def front_pass(x, gain, wq, wk, wv, table, segments, routes, order, cot, win, wout):
    rows, width = x.shape
    n = lax.axis_size("ctx")
    sides = lax.axis_size("dp")
    experts = lax.axis_size("expert")
    heads = table.shape[0] // n
    group = heads * 64
    length = n * rows
    blocks = n * sides
    vmem = pl.BlockSpec(memory_space=pltpu.VMEM)
    hbm = pl.BlockSpec(memory_space=pl.ANY)
    dma = pltpu.SemaphoreType.DMA
    far = max(experts // 2 - 1, 1)
    some = max(sides - 1, 1)
    return pl.pallas_call(
        partial(front_kernel, heads, n, rows),
        out_shape=[
            jax.ShapeDtypeStruct((n, 3 * group + 16, rows), bf16),
            jax.ShapeDtypeStruct((width, rows), bf16),
            jax.ShapeDtypeStruct((group, length), f32),
            jax.ShapeDtypeStruct((heads, length), f32),
            jax.ShapeDtypeStruct((width, rows), bf16),
            jax.ShapeDtypeStruct((experts, 8, rows), jnp.int32),
            jax.ShapeDtypeStruct((experts, rows, width), bf16),
            jax.ShapeDtypeStruct((blocks,) + win.shape, bf16),
            jax.ShapeDtypeStruct((blocks,) + wout.shape, bf16),
        ],
        in_specs=[vmem] * 9 + [hbm] * 3,
        out_specs=[vmem] * 6 + [hbm] * 3,
        scratch_shapes=[
            pltpu.VMEM((4, width, rows), bf16),
            pltpu.VMEM((n, group, rows), bf16),
            pltpu.VMEM((length, 128), bf16),
            pltpu.VMEM((128, length), bf16),
            pltpu.VMEM((length, 128), bf16),
            pltpu.VMEM((BLK, 2 * BLK), f32),
            pltpu.VMEM((BLK, length), f32),
            pltpu.VMEM((table.shape[0], 2 * BLK), f32),
            dma((2, 4, n - 1)),
            dma((2, heads, n - 1)),
            dma((2,)),
            dma((2, far)),
            dma((2, far)),
            dma((2, experts - 1)),
            dma((3,)),
            dma((2, 2, 2, n)),
            dma((2, 2, 2, some, n)),
        ],
        compiler_params=pltpu.CompilerParams(
            collective_id=2, has_side_effects=True, vmem_limit_bytes=60 * 1024 * 1024
        ),
        name="front_pass",
    )(x, gain, wq, wk, wv, table, segments, routes, order, cot, win, wout)


def line_order(n):
    order = []
    for i in range((n + 1) // 2):
        order.append(n - 1 - i)
        if i != n - 1 - i:
            order.append(i)
    return order


def line_scatter(n, own, right, left, right_sems, left_sems, ready):
    me = lax.axis_index("ctx")
    items = {}
    for j in line_order(n):
        for r in range(j):
            items.setdefault(ready[j] + r, []).append((0, r, j))
        for r in range(n - 1, j, -1):
            items.setdefault(ready[j] + n - 1 - r, []).append((1, r, j))
    steps = max(items) + 1

    def pass_on(way, r, j):
        taken, sems = (right, right_sems) if way == 0 else (left, left_sems)
        first = 0 if way == 0 else n - 1
        return remote(
            own.at[j] if r == first else taken.at[j], taken.at[j], sems.at[0, j], sems.at[1, j],
            {"ctx": r + 1 if way == 0 else r - 1},
        )

    def advance(step):
        for way, r, j in items.get(step, []):
            @pl.when(me == r)
            def _():
                copy = pass_on(way, r, j)
                if r != (0 if way == 0 else n - 1):
                    taken = right if way == 0 else left
                    copy.wait_recv()
                    taken[j] = (taken[j].astype(f32) + own[j].astype(f32)).astype(bf16)
                copy.start()

    def finish(out):
        for j in range(n):
            @pl.when(me == j)
            def _():
                total = own[j].astype(f32)
                if j > 0:
                    pass_on(0, j - 1, j).wait_recv()
                    total = total + right[j].astype(f32)
                if j < n - 1:
                    pass_on(1, j + 1, j).wait_recv()
                    total = total + left[j].astype(f32)
                out[...] = total.astype(bf16)

    def drain():
        for step in range(steps):
            for way, r, j in items.get(step, []):
                @pl.when(me == r)
                def _():
                    pass_on(way, r, j).wait_send()

    return advance, finish, drain, steps


def back_kernel(
    heads, n, rows, x_ref, do_ref, table_ref, of_ref, lse_ref, base_ref, far_ref, gin_hbm, gout_hbm,
    cots_ref, diag_ref, ein_ref, own_b, out_ref,
    do_in, g_ref, qa, ka, va, da, qn, dn, bias, dq, gsum,
    own_a, side_a, side_b, right_a, left_a,
    do_sems, out_sems, own_sems, side_sems, right_sems, left_sems, lines, far_in, far_sems,
):
    size = 64
    group = heads * size
    length = n * rows
    sides = lax.axis_size("dp")
    me = lax.axis_index("ctx")
    side = lax.axis_index("dp")
    barrier, peers = greet(("ctx", "dp", "expert"))
    order = line_order(n)
    advance, finish, drain, steps = line_scatter(
        n, own_a, right_a, left_a, right_sems, left_sems, {j: i for i, j in enumerate(order)}
    )
    loads = {}
    for j in order:
        at = j * sides + side
        loads[j] = [
            pltpu.make_async_copy(gin_hbm.at[at], own_a.at[j], own_sems.at[0, j]),
            pltpu.make_async_copy(gout_hbm.at[at], own_b.at[j], own_sems.at[1, j]),
        ]
        for copy in loads[j]:
            copy.start()
    pl.semaphore_wait(barrier, peers)
    lanes, lane, core = expert_split()
    homes = [
        remote(
            far_ref.at[k - 1], far_in.at[k - 1], far_sems.at[0, k - 1], far_sems.at[1, k - 1],
            {"expert": lax.rem(lane - k + lanes, lanes) * 2 + core},
        )
        for k in range(1, lanes)
    ]
    for copy in homes:
        copy.start()
    lines[...] = bias_line(lax.broadcasted_iota(jnp.int32, (1, 2 * BLK), 1), table_ref[...])
    arriving = []
    for k in range(1, n):
        to = lax.rem(me + k, n)
        copy = remote(
            do_ref.at[pl.ds(pl.multiple_of(to * group, 16), group)], do_in.at[me], do_sems.at[0, k - 1], do_sems.at[1, k - 1], {"ctx": to}
        )
        copy.start()
        arriving.append(copy)
    beside = {}
    for v, gone, taken in ((0, gin_hbm, side_a), (1, gout_hbm, side_b)):
        for j in order:
            beside[v, j] = []
            for k in range(1, sides):
                to = lax.rem(side + k, sides)
                beside[v, j].append(
                    remote(
                        gone.at[j * sides + to], taken.at[k - 1, j],
                        side_sems.at[0, v, k - 1, j], side_sems.at[1, v, k - 1, j], {"dp": to},
                    )
                )
                beside[v, j][-1].start()

    def sum_sides(v, j):
        own, taken = ((own_a, side_a), (own_b, side_b))[v]
        loads[j][v].wait()
        total = own[j].astype(f32)
        for k in range(1, sides):
            beside[v, j][k - 1].wait_recv()
            total = total + taken[k - 1, j].astype(f32)
        own[j] = total.astype(bf16)

    do_in[me] = do_ref[pl.ds(pl.multiple_of(me * group, 16), group), :]

    sum_sides(0, order[0])
    advance(0)
    for copy in arriving:
        copy.wait_recv()

    def out_copy(h, kind, k):
        to = lax.rem(me + k, n)
        base = pl.multiple_of(h * size, size)
        return remote(
            g_ref.at[to, pl.ds(kind * group + base, size)],
            cots_ref.at[pl.ds(pl.multiple_of(kind * n * group + me * group + base, 16), size)],
            out_sems.at[0, h, kind, k - 1],
            out_sems.at[1, h, kind, k - 1],
            {"ctx": to},
        )

    def head(h, carry):
        base = pl.multiple_of(h * size, size)
        for s in range(n):
            at = slice(s * rows, (s + 1) * rows)
            q = x_ref[s, pl.ds(base, size), :] * jnp.asarray(0.125, bf16)
            k = x_ref[s, pl.ds(base + group, size), :]
            v = x_ref[s, pl.ds(base + 2 * group, size), :]
            d = do_in[s, pl.ds(base, size), :]
            seg = x_ref[s, 3 * group : 3 * group + 16, :]
            mask, hot = seg_mask_rows(seg)
            which = lax.broadcasted_iota(jnp.int32, (16, rows), 0)

            def rows3(vec):
                hi, mid, lo = split3(jnp.broadcast_to(vec, (16, rows)))
                return jnp.where(which == 0, hi, jnp.where(which == 1, mid, jnp.where(which == 2, lo, jnp.zeros((), bf16))))

            ones = jnp.where(which < 3, 1.0, 0.0).astype(bf16)
            zeros = jnp.zeros((32, rows), bf16)
            zeros48 = jnp.zeros((48, rows), bf16)
            lse = lse_ref[pl.ds(h, 1), at]
            delta = jnp.sum(of_ref[pl.ds(base, size), at] * d.astype(f32), axis=0, keepdims=True)
            qt = jnp.concatenate([q, mask, rows3(-lse), zeros], axis=0)
            qa[:, at] = qt
            qn[at, :] = qt.T
            ka[at, :] = jnp.concatenate([k, hot, ones, zeros], axis=0).T
            dt = jnp.concatenate([d, rows3(-delta), zeros48], axis=0)
            da[:, at] = dt
            dn[at, :] = dt.T
            va[at, :] = jnp.concatenate([v, ones, zeros48], axis=0).T
        line = jnp.broadcast_to(lines[pl.ds(me * heads + h, 1), :], (BLK, 2 * BLK))
        rolled = pltpu.roll(line, 0, 1, stride=1, stride_axis=0)
        r = lax.broadcasted_iota(jnp.int32, (BLK, 2 * BLK), 0)
        c = lax.broadcasted_iota(jnp.int32, (BLK, 2 * BLK), 1)
        bias[...] = jnp.where(c < r, NEG, rolled)
        gsum[...] = jnp.zeros_like(gsum)
        for j in range(length // BLK):
            a0 = j * BLK
            kj = ka[a0 : a0 + BLK, :]
            vj = va[a0 : a0 + BLK, :]
            src, off = a0 // rows, a0 % rows
            kt = x_ref[src, pl.ds(base + group, size), off : off + BLK]
            dk = dv = None
            for a in range(a0, length, 2 * BLK):
                b = min(a + 2 * BLK, length)
                s = dot(kj, qa[:, a:b])
                if a == a0:
                    s = s + bias[:, : b - a]
                p = jnp.exp(s)
                ds = p * dot(vj, da[:, a:b])
                if a == a0:
                    gsum[:, : b - a] += ds
                p_low, ds_low = p.astype(bf16), ds.astype(bf16)
                u = dot(p_low, dn[a:b, :])
                dv = u if dv is None else dv + u
                u = dot(ds_low, qn[a:b, :])
                dk = u if dk is None else dk + u
                u = dot(kt, ds_low)
                if j == 0:
                    dq[:, a:b] = u
                else:
                    dq[:, a:b] += u
            g_ref[src, pl.ds(base + group, size), off : off + BLK] = dk.T[:size].astype(bf16)
            g_ref[src, pl.ds(base + 2 * group, size), off : off + BLK] = dv.T[:size].astype(bf16)
        for s in range(n):
            g_ref[s, pl.ds(base, size), :] = (dq[:, s * rows : (s + 1) * rows] * 0.125).astype(bf16)
        for kind in range(3):
            for k in range(1, n):
                out_copy(h, kind, k).start()
            cots_ref[pl.ds(pl.multiple_of(kind * n * group + me * group + base, 16), size), :] = g_ref[
                me, pl.ds(kind * group + base, size), :
            ]
        eight = gsum[0:8, :]
        for i in range(1, BLK // 8):
            eight = eight + pltpu.roll(gsum[8 * i : 8 * i + 8, :], 2 * BLK - 8 * i, 1)
        line = eight[0:1]
        for i in range(1, 8):
            line = line + pltpu.roll(eight, 2 * BLK - i, 1)[i : i + 1]
        diag_ref[pl.ds(h, 1), :] = line
        for step in range(1, heads):
            @pl.when(h == step - 1)
            def _():
                if step < n:
                    sum_sides(0, order[step])
                advance(step)

        return carry

    lax.fori_loop(0, heads, head, 0)
    for step in range(heads, steps):
        if step < n:
            sum_sides(0, order[step])
        advance(step)
        if step >= n and step - n < n:
            sum_sides(1, order[step - n])
    for i in range(max(steps - n, 0), n):
        sum_sides(1, order[i])
    mixture = base_ref[...]
    for k in range(1, lanes):
        homes[k - 1].wait()
        mixture = mixture + far_in[k - 1].astype(f32)
    out_ref[...] = mixture.astype(bf16)
    finish(ein_ref)
    for h in range(heads):
        for kind in range(3):
            for k in range(1, n):
                out_copy(h, kind, k).wait()
    for copy in arriving:
        copy.wait_send()
    for copies in beside.values():
        for copy in copies:
            copy.wait_send()
    drain()


def back_pass(x, do, table, of, lse, base, far, gin, gout):
    n, depth, rows = x.shape
    heads = table.shape[0] // n
    group = heads * 64
    length = n * rows
    sides = lax.axis_size("dp")
    _, high_a, wide_a = gin.shape
    _, high_b, wide_b = gout.shape
    vmem = pl.BlockSpec(memory_space=pltpu.VMEM)
    hbm = pl.BlockSpec(memory_space=pl.ANY)
    dma = pltpu.SemaphoreType.DMA
    some = max(sides - 1, 1)
    return pl.pallas_call(
        partial(back_kernel, heads, n, rows),
        out_shape=[
            jax.ShapeDtypeStruct((3 * n * group, rows), bf16),
            jax.ShapeDtypeStruct((heads, 2 * BLK), f32),
            jax.ShapeDtypeStruct((high_a, wide_a), bf16),
            jax.ShapeDtypeStruct((n, high_b, wide_b), bf16),
            jax.ShapeDtypeStruct(base.shape, bf16),
        ],
        in_specs=[vmem] * 7 + [hbm] * 2,
        out_specs=[vmem] * 5,
        scratch_shapes=[
            pltpu.VMEM((n, group, rows), bf16),
            pltpu.VMEM((n, 3 * group, rows), bf16),
            pltpu.VMEM((128, length), bf16),
            pltpu.VMEM((length, 128), bf16),
            pltpu.VMEM((length, 128), bf16),
            pltpu.VMEM((128, length), bf16),
            pltpu.VMEM((length, 128), bf16),
            pltpu.VMEM((length, 128), bf16),
            pltpu.VMEM((BLK, 2 * BLK), f32),
            pltpu.VMEM((64, length), f32),
            pltpu.VMEM((BLK, 2 * BLK), f32),
            pltpu.VMEM((n, high_a, wide_a), bf16),
            pltpu.VMEM((some, n, high_a, wide_a), bf16),
            pltpu.VMEM((some, n, high_b, wide_b), bf16),
            pltpu.VMEM((n, high_a, wide_a), bf16),
            pltpu.VMEM((n, high_a, wide_a), bf16),
            dma((2, n - 1)),
            dma((2, heads, 3, n - 1)),
            dma((2, n)),
            dma((2, 2, some, n)),
            dma((2, n)),
            dma((2, n)),
            pltpu.VMEM((table.shape[0], 2 * BLK), f32),
            pltpu.VMEM(far.shape, bf16),
            dma((2, far.shape[0])),
        ],
        compiler_params=pltpu.CompilerParams(
            collective_id=3, has_side_effects=True, vmem_limit_bytes=60 * 1024 * 1024
        ),
        name="back_pass",
    )(x, do, table, of, lse, base, far, gin, gout)


def add_all(parts):
    return functools.reduce(lambda a, b: a + b, parts)


def axis_stages():
    experts = lax.axis_size("expert")
    me = lax.axis_index("expert")
    core, lane = lax.rem(me, 2), lax.div(me, 2)
    return {
        "core": (2, core, lambda j: {"expert": lane * 2 + j}),
        "lane": (experts // 2, lane, lambda j: {"expert": j * 2 + core}),
        "dp": (lax.axis_size("dp"), lax.axis_index("dp"), lambda j: {"dp": j}),
        "ctx": (lax.axis_size("ctx"), lax.axis_index("ctx"), lambda j: {"ctx": j}),
    }


ORDERS = (("core", "lane", "dp", "ctx"), ("core", "dp", "lane", "ctx"))
SLICES = 2


def sum_plan(sizes, rows):
    plans = []
    for order in ORDERS:
        length, plan = rows // 2, []
        for name in order:
            count = sizes[name]
            split = length % count == 0 and (length // count) % 16 == 0
            plan.append((name, count, length, split))
            if split:
                length = length // count
        plans.append(plan)
    return plans


def received_rows(plans):
    return [
        [(count - 1) * (length // count if split else length) for (_, count, length, split) in plan]
        for plan in plans
    ]


def sizes_of():
    return {
        "core": 2,
        "lane": lax.axis_size("expert") // 2,
        "dp": lax.axis_size("dp"),
        "ctx": lax.axis_size("ctx"),
    }


def tail_kernel(
    plans, normed_t, cots, mixed_t, wq, wk, wv, x_ref, gain_ref, hidden_cot_ref, moe_small_ref, diag_ref, sums_ref,
    grads_ref, input_grad_ref, small_out_ref, eout_ref,
    acc, whole, taken_a, taken_b, small, small_taken, send, recv, back_send, back_recv, small_send, small_recv,
    right, left, right_sems, left_sems,
):
    stages = axis_stages()
    width = wq.shape[0]
    rows = x_ref.shape[0]
    barrier = pltpu.get_barrier_semaphore()
    peers = 0
    for name, (count, me, at) in stages.items():
        for k in range(1, count):
            pl.semaphore_signal(barrier, inc=1, device_id=at(lax.rem(me + k, count)), device_id_type=pl.DeviceIdType.MESH)
            peers += 1

    def make(k):
        if k < 3:
            acc[k * width : (k + 1) * width, :] = dot(
                normed_t[...], cots[k * width : (k + 1) * width, :], NT
            ).astype(bf16)
        else:
            acc[3 * width :, :] = dot(mixed_t[...], hidden_cot_ref[...].astype(bf16)).astype(bf16)

    taken = (taken_a, taken_b)
    half = 2 * width
    piece = width // SLICES
    parts = [(h, c) for c in range(SLICES) for h in range(2)]
    spans = {}
    for part in parts:
        spans[part] = [part[0] * half]

    def columns(part):
        return pl.ds(part[1] * piece, piece)

    def rows_at(start, size):
        return pl.ds(pl.multiple_of(start, 16), size)

    flying = {}

    def send_stage(part, step):
        h, c = part
        name, count, length, split = plans[h][step]
        _, me, at = stages[name]
        start = spans[part][-1]
        size = length // count if split else length
        base = sum(received[h][:step])
        copies = []
        for k in range(1, count):
            peer = lax.rem(me + k, count)
            copies.append(
                pltpu.make_async_remote_copy(
                    src_ref=acc.at[rows_at(start + peer * size if split else start, size), columns(part)],
                    dst_ref=taken[h].at[pl.ds(base + (k - 1) * size, size), columns(part)],
                    send_sem=send.at[h * SLICES + c, step, k - 1],
                    recv_sem=recv.at[h * SLICES + c, step, k - 1],
                    device_id=at(peer),
                    device_id_type=pl.DeviceIdType.MESH,
                )
            )
        for copy in copies:
            copy.start()
        flying[part] = copies

    def add_stage(part, step):
        h, c = part
        name, count, length, split = plans[h][step]
        _, me, at = stages[name]
        size = length // count if split else length
        start = spans[part][-1] + me * size if split else spans[part][-1]
        base = sum(received[h][:step])
        for copy in flying[part]:
            copy.wait()
        total = acc[rows_at(start, size), columns(part)].astype(f32)
        for k in range(1, count):
            total = total + taken[h][base + (k - 1) * size : base + k * size, columns(part)].astype(f32)
        if step == len(plans[h]) - 1:
            whole[rows_at(start, size), columns(part)] = total.astype(bf16)
        else:
            acc[rows_at(start, size), columns(part)] = total.astype(bf16)
        spans[part].append(start)

    def give_stage(part, step):
        h, c = part
        name, count, length, split = plans[h][step]
        if not split:
            flying[part] = []
            return
        _, me, at = stages[name]
        size = length // count
        start = spans[part][step + 1]
        copies = []
        for k in range(1, count):
            peer = lax.rem(me + k, count)
            copies.append(
                pltpu.make_async_remote_copy(
                    src_ref=whole.at[rows_at(start, size), columns(part)],
                    dst_ref=whole.at[rows_at(start, size), columns(part)],
                    send_sem=back_send.at[h * SLICES + c, step, k - 1],
                    recv_sem=back_recv.at[h * SLICES + c, step, k - 1],
                    device_id=at(peer),
                    device_id_type=pl.DeviceIdType.MESH,
                )
            )
        for copy in copies:
            copy.start()
        flying[part] = copies

    n = sums_ref.shape[0]
    advance, finish, drain, line_steps = line_scatter(n, sums_ref, right, left, right_sems, left_sems, [0] * n)
    received = received_rows(plans)
    make(2)
    make(3)
    pl.semaphore_wait(barrier, peers)
    for c in range(SLICES):
        send_stage((1, c), 0)
    advance(0)
    make(0)
    make(1)
    for c in range(SLICES):
        send_stage((0, c), 0)
    parts = [(1, 0), (0, 0), (1, 1), (0, 1)]

    turned = dot(wq[...], cots[:width, :]) + dot(wk[...], cots[width : 2 * width, :]) + dot(wv[...], cots[2 * width :, :])
    cot = turned.T
    x = x_ref[...].astype(f32)
    gain = gain_ref[...].reshape(1, width)
    scale = lax.rsqrt(jnp.mean(x * x, axis=1, keepdims=True) + EPSILON)
    unit = x * scale
    gained = cot * gain
    input_grad_ref[...] = hidden_cot_ref[...] + scale * (gained - unit * jnp.mean(unit * gained, axis=1, keepdims=True))
    gain_grad = jnp.sum(unit * cot, axis=0, keepdims=True)
    which = lax.broadcasted_iota(jnp.int32, (8, width), 0)
    low = jnp.where(which == 0, gain_grad, jnp.where(which == 1, moe_small_ref[0:8, :], 0.0))
    distance = lax.broadcasted_iota(jnp.int32, (2 * BLK, width), 0)
    lane = lax.broadcasted_iota(jnp.int32, (2 * BLK, width), 1)
    far = jnp.full(distance.shape, BUCKETS // 2, jnp.int32)
    for limit in THRESHOLDS:
        far = far + jnp.where(distance >= limit, 1, 0)
    bucket = jnp.where(distance < BUCKETS // 2, distance, far)
    own = distance < THRESHOLDS[-1]
    which = lax.broadcasted_iota(jnp.int32, (8, width), 0)
    lane_row = lax.broadcasted_iota(jnp.int32, (8, width), 1)
    heads = diag_ref.shape[0]
    for h in range(heads):
        at = lax.axis_index("ctx") * heads + h
        start = lax.div(at, 6) * 128
        hot = jnp.where(own & (bucket + start == lane), 1.0, 0.0).astype(bf16)
        three = split3(jnp.broadcast_to(diag_ref[h : h + 1, :], (16, 2 * BLK)))
        near = (dot(three[0], hot) + dot(three[1], hot) + dot(three[2], hot))[0:1]
        near = jnp.where(lane_row[0:1] == start + BUCKETS - 1, -jnp.sum(near, axis=1, keepdims=True), near)
        low = low + jnp.where(which == 2 + lax.rem(at, 6), near, 0.0)
    small[0:8, :] = low
    small[8:16, :] = moe_small_ref[8:16, :]

    def send_small(step):
        name = ORDERS[0][step]
        count, me, at = stages[name]
        base = sum(stages[n][0] - 1 for n in ORDERS[0][:step])
        copies = [
            pltpu.make_async_remote_copy(
                src_ref=small,
                dst_ref=small_taken.at[base + k - 1],
                send_sem=small_send.at[base + k - 1],
                recv_sem=small_recv.at[base + k - 1],
                device_id=at(lax.rem(me + k, count)),
                device_id_type=pl.DeviceIdType.MESH,
            )
            for k in range(1, count)
        ]
        for copy in copies:
            copy.start()
        flying["small"] = copies

    def add_small(step):
        base = sum(stages[n][0] - 1 for n in ORDERS[0][:step])
        for copy in flying["small"]:
            copy.wait()
        total = small[...]
        for k in range(len(flying["small"])):
            total = total + small_taken[base + k]
        small[...] = total

    last = len(ORDERS[0])
    send_small(0)
    for step in range(last):
        for part in parts:
            add_stage(part, step)
            if step + 1 < last:
                send_stage(part, step + 1)
            else:
                give_stage(part, step)
        add_small(step)
        if step + 1 < last:
            send_small(step + 1)
        advance(step + 1)
    small_out_ref[...] = small[...]
    for step in range(last - 1, -1, -1):
        for part in parts:
            for copy in flying[part]:
                copy.wait()
            if step > 0:
                give_stage(part, step - 1)
    for step in range(last + 1, line_steps):
        advance(step)
    finish(eout_ref)
    drain()
    grads_ref[...] = whole[...]


def tail_pass(normed_t, cots, mixed_t, wq, wk, wv, x, gain, hidden_cot, moe_small, diag, sums):
    rows, width = x.shape
    sizes = sizes_of()
    plans = sum_plan(sizes, 4 * width)
    received = [sum(r) for r in received_rows(plans)]
    most = max(sizes.values()) - 1
    few = sum(n - 1 for n in sizes.values())
    small = jax.ShapeDtypeStruct((16, width), f32)
    return pl.pallas_call(
        partial(tail_kernel, plans),
        out_shape=[
            jax.ShapeDtypeStruct((4 * width, width), bf16),
            jax.ShapeDtypeStruct((rows, width), f32),
            jax.ShapeDtypeStruct(small.shape, f32),
            jax.ShapeDtypeStruct(sums.shape[1:], bf16),
        ],
        in_specs=[pl.BlockSpec(memory_space=pltpu.VMEM)] * 12,
        out_specs=[pl.BlockSpec(memory_space=pltpu.VMEM)] * 4,
        scratch_shapes=[
            pltpu.VMEM((4 * width, width), bf16),
            pltpu.VMEM((4 * width, width), bf16),
            pltpu.VMEM((received[0], width), bf16),
            pltpu.VMEM((received[1], width), bf16),
            pltpu.VMEM(small.shape, f32),
            pltpu.VMEM((few,) + small.shape, f32),
            pltpu.SemaphoreType.DMA((2 * SLICES, 4, most)),
            pltpu.SemaphoreType.DMA((2 * SLICES, 4, most)),
            pltpu.SemaphoreType.DMA((2 * SLICES, 4, most)),
            pltpu.SemaphoreType.DMA((2 * SLICES, 4, most)),
            pltpu.SemaphoreType.DMA((few,)),
            pltpu.SemaphoreType.DMA((few,)),
            pltpu.VMEM(sums.shape, bf16),
            pltpu.VMEM(sums.shape, bf16),
            pltpu.SemaphoreType.DMA((2, sums.shape[0])),
            pltpu.SemaphoreType.DMA((2, sums.shape[0])),
        ],
        compiler_params=pltpu.CompilerParams(
            collective_id=0, has_side_effects=True, vmem_limit_bytes=56 * 1024 * 1024
        ),
        name="tail_pass",
    )(normed_t, cots, mixed_t, wq, wk, wv, x, gain, hidden_cot, moe_small, diag, sums)


def local(
    layer_input,
    cotangent,
    norm_gain_one,
    w_query,
    w_key,
    w_value,
    w_output,
    rel_table,
    norm_gain_two,
    w_router,
    w_expert_in,
    w_expert_out,
    segment_ids,
    routes,
    priority,
):
    rows, width = layer_input.shape[1:]
    heads = rel_table.shape[0]
    shards = lax.axis_size("ctx")
    experts = lax.axis_size("expert")
    capacity = min(rows, 5 * rows // (2 * experts))
    blocks = shards * lax.axis_size("dp")

    def padded(array):
        return jnp.pad(array, ((0, 0), (0, -array.shape[1] % 16), (0, 0)))

    held, mixed_t, attended_whole, lse, normed_t, info_all, cots_all, inner_weight, outer_weight = front_pass(
        layer_input[0], norm_gain_one, w_query, w_key, w_value, rel_table, segment_ids, routes[0].T, priority[0],
        cotangent[0], padded(w_expert_in)[0], padded(w_expert_out)[0],
    )
    inner_weight = inner_weight[:, : w_expert_in.shape[1]].reshape(width, -1)
    outer_weight = outer_weight[:, : w_expert_out.shape[1]].reshape(-1, width)
    router_t = jnp.pad(w_router.T, ((0, 16 - experts), (0, 0)))
    base, far, hidden_cot, mixed_cot, moe_small, inner_grad, outer_grad = moe_pass(
        capacity, mixed_t, w_output, layer_input[0], cotangent[0], norm_gain_two, router_t, info_all, cots_all, inner_weight, outer_weight
    )

    def cut(array):
        return padded(array.reshape(blocks, array.shape[0] // blocks, array.shape[1]))

    cots, diagonals, expert_in_grad, expert_out_sums, layer_output = back_pass(
        held, mixed_cot, rel_table, attended_whole, lse, base, far, cut(inner_grad), cut(outer_grad)
    )
    expert_in_grad = expert_in_grad[None, : w_expert_in.shape[1]]
    large, input_grad, small, expert_out_grad = tail_pass(
        normed_t, cots, mixed_t, w_query, w_key, w_value, layer_input[0], norm_gain_one, hidden_cot, moe_small, diagonals, expert_out_sums
    )
    expert_out_grad = expert_out_grad[None, : w_expert_out.shape[1]]
    large = large.reshape(4, width, width)
    return (
        layer_output[None],
        input_grad[None],
        small[0],
        large[0].astype(f32),
        large[1].astype(f32),
        large[2].astype(f32),
        large[3].astype(f32),
        jnp.concatenate([small[2:8, a : a + BUCKETS] for a in range(0, heads * 128 // 6, 128)], axis=0),
        small[1],
        small[8 : 8 + experts].T,
        expert_in_grad.astype(f32),
        expert_out_grad.astype(f32),
    )


def solution(mesh):
    placed = (
        P(("expert", "dp"), "ctx", None),
        P(("expert", "dp"), "ctx", None),
        P(),
        P(),
        P(),
        P(),
        P(),
        P(),
        P(),
        P(),
        P("expert", ("ctx", "dp"), None),
        P("expert", ("ctx", "dp"), None),
        P(("expert", "dp"), "ctx"),
        P(("expert", "dp"), "ctx", None),
        P(("expert", "dp"), "ctx", None),
    )
    return jax.shard_map(
        local,
        mesh=mesh,
        in_specs=placed,
        out_specs=(
            P(("expert", "dp"), "ctx", None),
            P(("expert", "dp"), "ctx", None),
            P(),
            P(),
            P(),
            P(),
            P(),
            P(),
            P(),
            P(),
            P("expert", ("ctx", "dp"), None),
            P("expert", ("ctx", "dp"), None),
        ),
        check_vma=False,
    )
```

```python
import functools
from functools import partial

import jax
import jax.numpy as jnp
from jax import lax
from jax.experimental import pallas as pl
from jax.experimental.pallas import tpu as pltpu
from jax.sharding import PartitionSpec as P

bf16 = jnp.bfloat16
f32 = jnp.float32
HIGH_PRECISION = lax.Precision.HIGHEST
EPSILON = 1e-06
THRESHOLDS = (19, 21, 24, 27, 31, 35, 40, 46, 52, 59, 67, 77, 87, 99, 113)
BUCKETS=32
NEG=-1e30
BLK=256
NT=(((1,),(1,)),((),()))
TN=(((0,),(0,)),((),()))

def dot(a,b,dims=(((1,),(0,)),((),()))):
    return lax.dot_general(a,b,dims,preferred_element_type=f32)

def seg_mask_rows(seg):
    which = lax.broadcasted_iota(jnp.int32, seg.shape, 0).astype(f32)
    same = seg.astype(f32) == which
    return jnp.where(same, 0.0, NEG).astype(bf16), jnp.where(same, 1.0, 0.0).astype(bf16)

def split3(v):
    hi = v.astype(bf16); rest = v - hi.astype(f32)
    mid = rest.astype(bf16); rest = rest - mid.astype(f32)
    return hi, mid, rest.astype(bf16)

ROOT = 0.7978845608028654


def remote(src, dst, send_sem, recv_sem, where):
    return pltpu.make_async_remote_copy(
        src_ref=src,
        dst_ref=dst,
        send_sem=send_sem,
        recv_sem=recv_sem,
        device_id=where,
        device_id_type=pl.DeviceIdType.MESH,
    )


def expert_split():
    experts = lax.axis_size("expert")
    me = lax.axis_index("expert")
    return experts // 2, lax.div(me, 2), lax.rem(me, 2)


def gather_start(piece, whole, near_sems, far_sems, rows=None):
    lanes, lane, core = expert_split()
    me = lane * 2 + core
    view = whole.at[me] if rows is None else whole.at[me, rows]
    copies = [remote(piece, view, near_sems.at[0], near_sems.at[1], {"expert": lane * 2 + 1 - core})]
    for k in range(1, lanes):
        copies.append(
            remote(piece, view, far_sems.at[0, k - 1], far_sems.at[1, k - 1], {"expert": lax.rem(lane + k, lanes) * 2 + core})
        )
    for copy in copies:
        copy.start()
    return copies


def relay(k, whole, sems):
    lanes, lane, core = expert_split()
    source = lax.rem(lane - k + lanes, lanes) * 2 + core
    return remote(whole.at[source], whole.at[source], sems.at[0, k - 1], sems.at[1, k - 1], {"expert": lane * 2 + 1 - core})


def greet(names):
    barrier = pltpu.get_barrier_semaphore()
    total = 0
    for name in names:
        count, at = lax.axis_size(name), lax.axis_index(name)
        for k in range(1, count):
            pl.semaphore_signal(
                barrier, inc=1, device_id={name: lax.rem(at + k, count)}, device_id_type=pl.DeviceIdType.MESH
            )
        total += count - 1
    return barrier, total


def moe_kernel(
    capacity, mixed_t, w_output, x_ref, cot_ref, gain_ref, router_ref, info_ref, cots_hbm, inner_hbm, outer_hbm,
    base_ref, far_ref, hidden_cot_ref, mixed_cot_ref, small_ref, gin_hbm, gout_hbm,
    nt, cots, inner, outer, act_all, pre_all, rows_all, cots_all, made, back, part, pair_in, total,
    core_in, far_in, gate_out, gate_in,
    load_sems, cot_sems, near_sems, far_sems, relay_sems, pair_sems, core_sems, back_sems, gate_sems, stage_sems, free_sem, late_sems,
):
    experts = lax.axis_size("expert")
    lanes, lane, core = expert_split()
    me = lane * 2 + core
    other = lane * 2 + 1 - core
    rows, width = cot_ref.shape
    hidden = hidden_cot_ref
    pieces = 2
    step_rows = rows // pieces
    hidden_size = inner.shape[1]
    n = lax.axis_size("ctx")
    place_z = lax.axis_index("ctx")
    wide = hidden_size // n

    first = pltpu.make_async_copy(inner_hbm, inner, load_sems.at[n])
    first.start()

    def chunk_rows(j):
        return pl.ds(pl.multiple_of(j * wide, wide), wide)

    def chunk_at(f):
        return jnp.where(place_z == n - 1, n - 1 - f, f)

    def has(f):
        return (f < n - 1) | ((place_z > 0) & (place_z < n - 1))

    def load(f):
        at = chunk_rows(chunk_at(f))
        return pltpu.make_async_copy(outer_hbm.at[at], outer.at[at], load_sems.at[f])

    for f in range(n):
        @pl.when(has(f))
        def _():
            load(f).start()

    def late(up):
        at = chunk_rows(0 if up else n - 1)
        return remote(
            outer_hbm.at[at], outer.at[at], late_sems.at[0, int(up)], late_sems.at[1, int(up)],
            {"ctx": n - 1 if up else 0},
        )

    barrier, peers = greet(("expert", "ctx"))
    pl.semaphore_wait(barrier, peers)

    @pl.when(place_z == n - 2)
    def _():
        late(True).start()

    @pl.when(place_z == 1)
    def _():
        late(False).start()

    sent = []
    for p in range(pieces):
        at = slice(p * step_rows, (p + 1) * step_rows)
        now = x_ref[at, :].astype(f32) + dot(mixed_t[:, at], w_output[...], TN)
        hidden[at, :] = now
        scale = lax.rsqrt(jnp.mean(now * now, axis=1, keepdims=True) + EPSILON)
        nt[me, at, :] = (now * scale * gain_ref[...].reshape(1, width)).astype(bf16)
        sent.append(gather_start(nt.at[me, at], nt, near_sems.at[p], far_sems.at[p], at))

    def gate_rows(source):
        logits = dot(router_ref[...], nt[source], NT)
        which = lax.broadcasted_iota(jnp.int32, logits.shape, 0)
        info = info_ref[source]
        chosen = (which == info[0:1]) | (which == info[1:2])
        top = jnp.max(jnp.where(chosen, logits, NEG), axis=0, keepdims=True)
        power = jnp.where(chosen, jnp.exp(jnp.minimum(logits - top, 0.0)), 0.0)
        return power / jnp.sum(power, axis=0, keepdims=True)

    def pair_of(k):
        return [lax.rem(lane - k + lanes, lanes) * 2 + sc for sc in range(2)]

    order = pair_of(1) + [me, other]
    for k in range(2, lanes):
        order += pair_of(k)
    first_group = 4

    def fetch(i):
        return pltpu.make_async_copy(cots_hbm.at[order[i]], cots.at[i % first_group], cot_sems.at[i % first_group])

    for i in range(first_group):
        fetch(i).start()

    def place_of(i):
        info = info_ref[order[i]]
        place = jnp.where(info[0:1] == me, info[2:3], jnp.where(info[1:2] == me, info[3:4], -1))
        slot = lax.broadcasted_iota(jnp.int32, (capacity, rows), 0)
        pick = jnp.where(slot == place, 1.0, 0.0)
        gates = gate_rows(order[i])
        which = lax.broadcasted_iota(jnp.int32, gates.shape, 0)
        own_gate = jnp.sum(jnp.where(which == me, gates, 0.0), axis=0, keepdims=True)
        return place, pick, jnp.sum(pick * own_gate, axis=1, keepdims=True)

    def dispatch(i):
        fetch(i).wait()
        _, pick, slot_gate = place_of(i)
        block = slice(i * capacity, (i + 1) * capacity)
        rows_all[block, :] = dot(pick.astype(bf16), nt[order[i]]).astype(bf16)
        cots_all[block, :] = (slot_gate * dot(pick.astype(bf16), cots[i % first_group])).astype(bf16)
        made[i % first_group] = jnp.zeros((capacity, width), f32)
        back[i % first_group] = jnp.zeros((capacity, width), f32)

    def part_of(i, f):
        block = pl.ds(i * capacity if isinstance(i, int) else pl.multiple_of(i * capacity, 16), capacity)
        at = chunk_rows(chunk_at(f))
        turn = i % first_group if isinstance(i, int) else i
        pre = dot(rows_all[block, :], inner[:, at])
        cot = dot(cots_all[block, :], outer[at, :], NT)
        square = pre * pre
        t = jnp.tanh(pre * (ROOT + (ROOT * 0.044715) * square))
        half = 0.5 + 0.5 * t
        act = (pre * half).astype(bf16)
        slope = half + (0.5 * pre) * (1.0 - t * t) * (ROOT + (ROOT * 3 * 0.044715) * square)
        back_pre = (cot * slope).astype(bf16)
        act_all[block, at] = act
        pre_all[block, at] = back_pre
        made[turn] += dot(act, outer[at, :])
        back[turn] += dot(back_pre, inner[:, at], NT)

    def finish_source(i, target):
        place, pick, slot_gate = place_of(i)
        outcome = made[i % first_group].astype(bf16).astype(f32)
        slot_cot = jnp.sum(dot(pick.astype(bf16), cots[i % first_group]) * outcome, axis=1, keepdims=True)
        gate_out[order[i]] = jnp.broadcast_to(jnp.sum(pick * slot_cot, axis=0, keepdims=True), (8, rows))
        column = jnp.broadcast_to(place.astype(f32), (128, rows)).T[:, 0:1]
        lane_at = lax.broadcasted_iota(jnp.int32, (rows, capacity), 1).astype(f32)
        put = jnp.where(lane_at == column, 1.0, 0.0).astype(bf16)
        target[0] = dot(put, back[i % first_group].astype(bf16)).astype(bf16)
        target[1] = dot(put, (slot_gate * outcome).astype(bf16)).astype(bf16)
        if i + first_group < len(order):
            fetch(i + first_group).start()

    def process(i, target):
        dispatch(i)

        def step(f, carry):
            part_of(i, f)
            return carry

        lax.fori_loop(0, n, step, 0)
        finish_source(i, target)

    def pair_copies(k, sc):
        return [
            remote(part.at[sc, v], pair_in.at[v], pair_sems.at[0, v, k - 1], pair_sems.at[1, v, k - 1], {"expert": other})
            for v in range(2)
        ]

    def home_copy(k, sc):
        to = lax.rem(lane - k + lanes, lanes) * 2 + sc
        return remote(part.at[sc, 0], far_in.at[k - 1], back_sems.at[0, k - 1], back_sems.at[1, k - 1], {"expert": to})

    def begin_pair(k, sc):
        @pl.when(core != sc)
        def _():
            if k > 1:
                pl.semaphore_wait(free_sem, 1)
            for copy in pair_copies(k, sc):
                copy.start()

    def end_pair(k, sc):
        @pl.when(core == sc)
        def _():
            pair = pair_copies(k, sc)
            pair[0].wait_recv()
            part[sc, 0] = (part[sc, 0].astype(f32) + pair_in[0].astype(f32)).astype(bf16)
            home_copy(k, sc).start()
            pair[1].wait_recv()
            far_ref[k - 1] = (part[sc, 1].astype(f32) + pair_in[1].astype(f32)).astype(bf16)
            if k + 1 < lanes:
                pl.semaphore_signal(
                    free_sem, inc=1, device_id={"expert": other}, device_id_type=pl.DeviceIdType.MESH
                )

    def pair_sent(k):
        for sc in range(2):
            @pl.when(core != sc)
            def _():
                for copy in pair_copies(k, sc):
                    copy.wait_send()

    def home_sent(k):
        for sc in range(2):
            @pl.when(core == sc)
            def _():
                home_copy(k, sc).wait_send()

    dispatch(2)
    for p in range(pieces):
        sent[p][0].wait_recv()
    dispatch(3)
    first.wait()
    for f in range(n - 1):
        load(f).wait()

    def steps_of(start):
        def step(at, carry):
            part_of(start + lax.rem(at, 2), lax.div(at, 2))
            return carry

        return step

    lax.fori_loop(0, 2 * (n - 1), steps_of(2), 0)
    passed_on = []
    for k in range(1, lanes):
        for p in range(pieces):
            sent[p][k].wait_recv()
        passed = relay(k, nt, relay_sems)
        passed.start()
        passed_on.append(passed)

    def relayed(k, sc):
        @pl.when(core != sc)
        def _():
            passed_on[k - 1].wait_recv()

    for sc in range(2):
        relayed(1, sc)
        dispatch(sc)
    lax.fori_loop(0, 2 * (n - 1), steps_of(0), 0)

    @pl.when(has(n - 1))
    def _():
        load(n - 1).wait()

    @pl.when(place_z == n - 1)
    def _():
        late(True).wait_recv()

    @pl.when(place_z == 0)
    def _():
        late(False).wait_recv()

    lax.fori_loop(2 * (n - 1), 2 * n, steps_of(0), 0)
    finish_source(0, part.at[0])
    begin_pair(1, 0)
    finish_source(1, part.at[1])
    begin_pair(1, 1)
    end_pair(1, 0)
    lax.fori_loop(2 * (n - 1), 2 * n, steps_of(2), 0)
    end_pair(1, 1)
    pair_sent(1)
    finish_source(3, part.at[1 - core])
    core_copies = [
        remote(part.at[1 - core, v], core_in.at[v], core_sems.at[0, v], core_sems.at[1, v], {"expert": other}) for v in range(2)
    ]
    for copy in core_copies:
        copy.start()
    finish_source(2, total)

    def gate_copy(k):
        to = lax.rem(me + k, experts)
        return remote(gate_out.at[to], gate_in.at[me], gate_sems.at[0, k - 1], gate_sems.at[1, k - 1], {"expert": to})

    for k in range(2, lanes):
        if k == 2:
            for copy in core_copies:
                copy.wait_send()
        home_sent(k - 1)
        for sc in range(2):
            relayed(k, sc)
            process(2 * k + sc, part.at[sc])
            begin_pair(k, sc)
        for sc in range(2):
            end_pair(k, sc)
        pair_sent(k)
    gate_copies = [gate_copy(k) for k in range(1, experts)]
    for copy in gate_copies:
        copy.start()
    count = rows_all.shape[0]
    for b in range(count // 128):
        at = slice(b * 128, (b + 1) * 128)
        inner[:, at] = rows_all[at, :].T
        inner[:, slice(count + b * 128, count + (b + 1) * 128)] = cots_all[at, :].T
    wide = width
    steps = hidden_size // wide

    def store(f, v):
        at = pl.ds(pl.multiple_of(f * wide, wide), wide)
        return pltpu.make_async_copy(outer.at[v * width : (v + 1) * width], gin_hbm.at[:, at] if v == 0 else gout_hbm.at[at, :], stage_sems.at[v])

    def grads(f, carry):
        at = pl.ds(pl.multiple_of(f * wide, wide), wide)

        @pl.when(f > 0)
        def _():
            store(f - 1, 0).wait()

        outer[:width, :] = dot(inner[:, :count], pre_all[:, at]).astype(bf16)
        store(f, 0).start()

        @pl.when(f > 0)
        def _():
            store(f - 1, 1).wait()

        outer[width : 2 * width, :] = dot(inner[:, count : 2 * count], act_all[:, at]).astype(bf16).T
        store(f, 1).start()
        return carry

    lax.fori_loop(0, steps, grads, 0)
    for copy in gate_copies:
        copy.wait()
    gates = gate_rows(me)
    pad = gates.shape[0]
    which = lax.broadcasted_iota(jnp.int32, gates.shape, 0)
    gate_cot = jnp.where(which == me, gate_out[me][0:1], 0.0)
    for k in range(1, experts):
        source = lax.rem(me + k, experts)
        gate_cot = gate_cot + jnp.where(which == source, gate_in[source][0:1], 0.0)
    logit_cot = gates * (gate_cot - jnp.sum(gates * gate_cot, axis=0, keepdims=True))
    three = jnp.concatenate(split3(logit_cot), axis=0)
    router_three = jnp.concatenate([router_ref[...]] * 3, axis=0)
    router_grad = dot(three, nt[me])
    small_ref[8:, :] = router_grad[:pad] + router_grad[pad : 2 * pad] + router_grad[2 * pad :]
    for copy in core_copies:
        copy.wait_recv()
    for k in range(1, lanes):
        remote(part.at[0, 0], far_in.at[k - 1], back_sems.at[0, k - 1], back_sems.at[1, k - 1], {"expert": other}).wait_recv()
    gain = gain_ref[...].reshape(1, width)
    gain_grad = jnp.zeros((1, width), f32)
    for start in range(0, rows, 128):
        at = slice(start, start + 128)
        normed_cot = total[0, at, :].astype(f32) + core_in[0, at, :].astype(f32)
        for k in range(1, lanes):
            normed_cot = normed_cot + far_in[k - 1, at, :].astype(f32)
        normed_cot = normed_cot + dot(three[:, at], router_three, TN)
        now = hidden[at, :]
        scale = lax.rsqrt(jnp.mean(now * now, axis=1, keepdims=True) + EPSILON)
        unit = now * scale
        gained = normed_cot * gain
        hidden_cot = cot_ref[at, :].astype(f32) + scale * (gained - unit * jnp.mean(unit * gained, axis=1, keepdims=True))
        hidden_cot_ref[at, :] = hidden_cot
        mixed_cot_ref[:, at] = dot(w_output[...], hidden_cot.astype(bf16), NT).astype(bf16)
        gain_grad = gain_grad + jnp.sum(unit * normed_cot, axis=0, keepdims=True)
        base_ref[at, :] = now + (total[1, at, :].astype(f32) + core_in[1, at, :].astype(f32))
    small_ref[0:8, :] = jnp.broadcast_to(gain_grad, (8, width))
    store(steps - 1, 0).wait()
    store(steps - 1, 1).wait()
    home_sent(lanes - 1)
    if lanes == 2:
        for copy in core_copies:
            copy.wait_send()
    for copy in passed_on:
        copy.wait_send()
    for p in range(pieces):
        for copy in sent[p]:
            copy.wait_send()

    @pl.when(place_z == n - 2)
    def _():
        late(True).wait_send()

    @pl.when(place_z == 1)
    def _():
        late(False).wait_send()


def moe_pass(capacity, mixed_t, w_output, x, cot, gain, router, info, cots, inner, outer):
    rows, width = cot.shape
    experts = cots.shape[0]
    lanes = experts // 2
    hidden_size = inner.shape[1]
    total = experts * capacity
    vmem = pl.BlockSpec(memory_space=pltpu.VMEM)
    hbm = pl.BlockSpec(memory_space=pl.ANY)
    dma = pltpu.SemaphoreType.DMA
    far = max(lanes - 1, 1)
    return pl.pallas_call(
        partial(moe_kernel, capacity),
        out_shape=[
            jax.ShapeDtypeStruct((rows, width), f32),
            jax.ShapeDtypeStruct((far, rows, width), bf16),
            jax.ShapeDtypeStruct((rows, width), f32),
            jax.ShapeDtypeStruct((width, rows), bf16),
            jax.ShapeDtypeStruct((8 + router.shape[0], width), f32),
            jax.ShapeDtypeStruct((width, hidden_size), bf16),
            jax.ShapeDtypeStruct((hidden_size, width), bf16),
        ],
        in_specs=[vmem] * 7 + [hbm] * 3,
        out_specs=[vmem] * 5 + [hbm] * 2,
        scratch_shapes=[
            pltpu.VMEM((experts, rows, width), bf16),
            pltpu.VMEM((4, rows, width), bf16),
            pltpu.VMEM((width, hidden_size), bf16),
            pltpu.VMEM((hidden_size, width), bf16),
            pltpu.VMEM((total, hidden_size), bf16),
            pltpu.VMEM((total, hidden_size), bf16),
            pltpu.VMEM((total, width), bf16),
            pltpu.VMEM((total, width), bf16),
            pltpu.VMEM((4, capacity, width), f32),
            pltpu.VMEM((4, capacity, width), f32),
            pltpu.VMEM((2, 2, rows, width), bf16),
            pltpu.VMEM((2, rows, width), bf16),
            pltpu.VMEM((2, rows, width), bf16),
            pltpu.VMEM((2, rows, width), bf16),
            pltpu.VMEM((far, rows, width), bf16),
            pltpu.VMEM((experts, 8, rows), f32),
            pltpu.VMEM((experts, 8, rows), f32),
            dma((lax.axis_size("ctx") + 1,)),
            dma((4,)),
            dma((2, 2)),
            dma((2, 2, far)),
            dma((2, far)),
            dma((2, 2, far)),
            dma((2, 2)),
            dma((2, far)),
            dma((2, experts - 1)),
            dma((2,)),
            pltpu.SemaphoreType.REGULAR,
            dma((2, 2)),
        ],
        compiler_params=pltpu.CompilerParams(
            collective_id=1, has_side_effects=True, vmem_limit_bytes=65000 * 1024
        ),
        name="moe_pass",
    )(mixed_t, w_output, x, cot, gain, router, info, cots, inner, outer)


def bias_line(distance, table):
    far = jnp.full(distance.shape, BUCKETS // 2, jnp.int32)
    for limit in THRESHOLDS:
        far = far + jnp.where(distance >= limit, 1, 0)
    bucket = jnp.where(distance < BUCKETS // 2, distance, far)
    own = (distance >= 0) & (distance < THRESHOLDS[-1])
    which = lax.broadcasted_iota(jnp.int32, (BUCKETS, distance.shape[1]), 0)
    hot = jnp.where(own & (which == bucket), 1.0, 0.0).astype(bf16)
    last = table[:, BUCKETS - 1 :].astype(f32)
    return dot(table, hot) - jnp.where(own, last, 0.0)


def column_of(row):
    return jnp.broadcast_to(row, (128, row.shape[1])).T


def front_kernel(
    heads, n, rows, x_ref, gain_ref, wq, wk, wv, table_ref, segment_ref, routes_ref, order_ref, cot_hbm, win_hbm, wout_hbm,
    held, mixed, of_ref, lse_ref, normed_t, infos, cots_hbm, win_all, wout_all,
    made, given, qa, ka, vn, bias, s_ref, lines,
    held_sems, mixed_sems, near_sems, far_sems, relay_sems, info_sems, own_sems, line_sems, side_sems,
):
    size = 64
    group = heads * size
    width = n * group
    length = n * rows
    sides = lax.axis_size("dp")
    me = lax.axis_index("ctx")
    side = lax.axis_index("dp")
    experts = lax.axis_size("expert")
    expert = lax.axis_index("expert")
    barrier = pltpu.get_barrier_semaphore()
    for name, count, at in (("ctx", n, me), ("dp", sides, side), ("expert", experts, expert)):
        for k in range(1, count):
            pl.semaphore_signal(
                barrier, inc=1, device_id={name: lax.rem(at + k, count)}, device_id_type=pl.DeviceIdType.MESH
            )
    owns = [
        pltpu.make_async_copy(cot_hbm, cots_hbm.at[expert], own_sems.at[0]),
        pltpu.make_async_copy(win_hbm, win_all.at[me * sides + side], own_sems.at[1]),
        pltpu.make_async_copy(wout_hbm, wout_all.at[me * sides + side], own_sems.at[2]),
    ]
    for copy in owns:
        copy.start()
    pl.semaphore_wait(barrier, n + sides + experts - 3)
    shard = (win_hbm, wout_hbm)
    whole = (win_all, wout_all)

    def along(way, s, v):
        j = me - s if way == 0 else me + s
        to = me + 1 if way == 0 else me - 1
        at = j * sides + side
        source = shard[v] if s == 0 else whole[v].at[at]
        return remote(source, whole[v].at[at], line_sems.at[0, way, v, s], line_sems.at[1, way, v, s], {"ctx": to})

    def across(way, s, v):
        j = me - s if way == 0 else me + s
        at = j * sides + side
        source = shard[v] if s == 0 else whole[v].at[at]
        return [
            remote(
                source, whole[v].at[at], side_sems.at[0, way, v, k - 1, s], side_sems.at[1, way, v, k - 1, s],
                {"dp": lax.rem(side + k, sides)},
            )
            for k in range(1, sides)
        ]

    def holds(way, s):
        return me - s >= 0 if way == 0 else me + s < n

    def passes(way, s, v):
        if v == 1 and s == n - 2:
            return None
        return (me - s >= 0) & (me < n - 1) if way == 0 else (me + s < n) & (me > 0)

    def advance(s, v):
        for way in range(2):
            if s > 0:
                @pl.when(holds(way, s))
                def _():
                    along(way, s - 1, v).wait_recv()

            if passes(way, s, v) is not None:
                @pl.when(passes(way, s, v))
                def _():
                    along(way, s, v).start()

            if s > 0:
                @pl.when(holds(way, s))
                def _():
                    for copy in across(way, s, v):
                        copy.start()

    for v in range(2):
        for copy in across(0, 0, v):
            copy.start()
        advance(0, v)
    sent = gather_start(cot_hbm, cots_hbm, near_sems, far_sems)

    x = x_ref[...].astype(f32)
    normed = x * lax.rsqrt(jnp.mean(x * x, axis=1, keepdims=True) + EPSILON) * gain_ref[...].reshape(1, width)
    normed = normed.astype(bf16)
    held_copies = []
    here = pl.ds(pl.multiple_of(me * group, 16), group)
    seg = jnp.broadcast_to(segment_ref[...].astype(f32), (16, rows)).astype(bf16)
    made[3, 0:16, :] = seg
    held[me, 3 * group : 3 * group + 16, :] = seg
    for kind, weight in enumerate((wq, wk, wv)):
        made[kind] = dot(normed, weight[...]).astype(bf16).T
        for k in range(1, n):
            to = lax.rem(me + k, n)
            copy = remote(
                made.at[kind, pl.ds(pl.multiple_of(to * group, 16), group)],
                held.at[me, kind * group : (kind + 1) * group],
                held_sems.at[0, kind, k - 1], held_sems.at[1, kind, k - 1], {"ctx": to},
            )
            copy.start()
            held_copies.append(copy)
        held[me, kind * group : (kind + 1) * group, :] = made[kind, here, :]
    for k in range(1, n):
        copy = remote(
            made.at[3, 0:16], held.at[me, 3 * group : 3 * group + 16], held_sems.at[0, 3, k - 1], held_sems.at[1, 3, k - 1],
            {"ctx": lax.rem(me + k, n)},
        )
        copy.start()
        held_copies.append(copy)
    normed_t[...] = normed.T

    order_row = order_ref[...].astype(f32)
    before = jnp.where(column_of(order_row)[:, 0:1] < order_row, 1.0, 0.0).astype(bf16)
    kinds = 16
    which = lax.broadcasted_iota(jnp.int32, (kinds, rows), 0)
    chosen = [routes_ref[c : c + 1, :] for c in range(2)]
    hot = [jnp.where(which == c, 1.0, 0.0) for c in chosen]
    ahead = [dot(h.astype(bf16), before) for h in hot]
    firsts = jnp.sum(hot[0], axis=1, keepdims=True)
    slots = [jnp.sum(hot[0] * ahead[0], axis=0, keepdims=True), jnp.sum(hot[1] * (ahead[1] + firsts), axis=0, keepdims=True)]
    infos[expert] = jnp.concatenate(chosen + [s.astype(jnp.int32) for s in slots] + [jnp.zeros((4, rows), jnp.int32)], axis=0)
    info_copies = [
        remote(infos.at[expert], infos.at[expert], info_sems.at[0, k - 1], info_sems.at[1, k - 1], {"expert": lax.rem(expert + k, experts)})
        for k in range(1, experts)
    ]
    for copy in info_copies:
        copy.start()
    lines[...] = bias_line(BLK - lax.broadcasted_iota(jnp.int32, (1, 2 * BLK), 1), table_ref[...])

    advance(1, 0)
    advance(1, 1)
    advance(2, 0)
    for copy in held_copies:
        copy.wait_recv()

    def mixed_copy(h, k):
        to = lax.rem(me + k, n)
        base = pl.multiple_of(h * size, size)
        return remote(
            given.at[to, pl.ds(base, size)], mixed.at[pl.ds(pl.multiple_of(me * group + base, 16), size)],
            mixed_sems.at[0, h, k - 1], mixed_sems.at[1, h, k - 1], {"ctx": to},
        )

    def head(h, carry):
        base = pl.multiple_of(h * size, size)
        for s in range(n):
            at = slice(s * rows, (s + 1) * rows)
            q = held[s, pl.ds(base, size), :]
            k = held[s, pl.ds(base + group, size), :]
            v = held[s, pl.ds(base + 2 * group, size), :]
            mask, hot = seg_mask_rows(held[s, 3 * group : 3 * group + 16, :])
            zeros = jnp.zeros((48, rows), bf16)
            qa[at, :] = jnp.concatenate([q * jnp.asarray(0.125, bf16), mask, zeros], axis=0).T
            ka[:, at] = jnp.concatenate([k, hot, zeros], axis=0)
            vn[at, :] = jnp.concatenate([v, jnp.zeros((64, rows), bf16)], axis=0).T
        line = jnp.broadcast_to(lines[pl.ds(me * heads + h, 1), :], (BLK, 2 * BLK))
        rolled = pltpu.roll(line, 0, 1, stride=1, stride_axis=0)
        r = lax.broadcasted_iota(jnp.int32, (BLK, 2 * BLK), 0)
        c = lax.broadcasted_iota(jnp.int32, (BLK, 2 * BLK), 1)
        bias[...] = jnp.where(c - r > BLK, NEG, rolled)
        for t in range(length // BLK):
            qt = qa[t * BLK : (t + 1) * BLK, :]
            near0 = max(t - 1, 0) * BLK
            end = (t + 1) * BLK
            chunks = [(near0, end)] + [(a, min(a + 2 * BLK, near0)) for a in range(0, near0, 2 * BLK)]
            top = None
            for a, b in chunks:
                s = dot(qt, ka[:, a:b])
                if a == near0:
                    s = s + bias[:, 2 * BLK - (b - a) :]
                s_ref[:, a:b] = s
                part = s[:, :128]
                for i in range(1, (b - a) // 128):
                    part = jnp.maximum(part, s[:, i * 128 : (i + 1) * 128])
                top = part if top is None else jnp.maximum(top, part)
            m = jnp.max(top, axis=1, keepdims=True)
            total = None
            o = None
            for a, b in chunks:
                p = jnp.exp(s_ref[:, a:b] - m)
                part = p[:, :128]
                for i in range(1, (b - a) // 128):
                    part = part + p[:, i * 128 : (i + 1) * 128]
                total = part if total is None else total + part
                u = dot(p.astype(bf16), vn[a:b, :])
                o = u if o is None else o + u
            l = jnp.sum(total, axis=1, keepdims=True)
            o = o / l
            lane = lax.broadcasted_iota(jnp.int32, (BLK, 128), 1)
            o = jnp.where(lane == 64, m + jnp.log(l), o)
            ot = o.T
            src, off = (t * BLK) // rows, (t * BLK) % rows
            given[src, pl.ds(base, size), off : off + BLK] = ot[:size].astype(bf16)
            of_ref[pl.ds(base, size), t * BLK : (t + 1) * BLK] = ot[:size]
            lse_ref[pl.ds(h, 1), t * BLK : (t + 1) * BLK] = ot[size : size + 1]
        for k in range(1, n):
            mixed_copy(h, k).start()
        mixed[pl.ds(pl.multiple_of(me * group + base, 16), size), :] = given[me, pl.ds(base, size), :]

        @pl.when(h == 0)
        def _():
            advance(2, 1)

        @pl.when(h == 1)
        def _():
            for s in range(3, n):
                advance(s, 0)

        return carry

    lax.fori_loop(0, heads, head, 0)
    relays = []
    for k in range(1, experts // 2):
        sent[k].wait_recv()
        passed = relay(k, cots_hbm, relay_sems)
        passed.start()
        relays.append(passed)
    sent[0].wait_recv()
    for h in range(heads):
        for k in range(1, n):
            mixed_copy(h, k).wait()
    for copy in held_copies + sent:
        copy.wait_send()
    for copy in relays + info_copies + owns:
        copy.wait()
    for v in range(2):
        for s in range(n):
            for way in range(2):
                if v == 1 and s == n - 1:
                    continue
                if passes(way, s, v) is not None:
                    @pl.when(passes(way, s, v))
                    def _():
                        along(way, s, v).wait_send()

                if s > 0 or way == 0:
                    @pl.when(holds(way, s))
                    def _():
                        for copy in across(way, s, v):
                            copy.wait()


def front_pass(x, gain, wq, wk, wv, table, segments, routes, order, cot, win, wout):
    rows, width = x.shape
    n = lax.axis_size("ctx")
    sides = lax.axis_size("dp")
    experts = lax.axis_size("expert")
    heads = table.shape[0] // n
    group = heads * 64
    length = n * rows
    blocks = n * sides
    vmem = pl.BlockSpec(memory_space=pltpu.VMEM)
    hbm = pl.BlockSpec(memory_space=pl.ANY)
    dma = pltpu.SemaphoreType.DMA
    far = max(experts // 2 - 1, 1)
    some = max(sides - 1, 1)
    return pl.pallas_call(
        partial(front_kernel, heads, n, rows),
        out_shape=[
            jax.ShapeDtypeStruct((n, 3 * group + 16, rows), bf16),
            jax.ShapeDtypeStruct((width, rows), bf16),
            jax.ShapeDtypeStruct((group, length), f32),
            jax.ShapeDtypeStruct((heads, length), f32),
            jax.ShapeDtypeStruct((width, rows), bf16),
            jax.ShapeDtypeStruct((experts, 8, rows), jnp.int32),
            jax.ShapeDtypeStruct((experts, rows, width), bf16),
            jax.ShapeDtypeStruct((blocks,) + win.shape, bf16),
            jax.ShapeDtypeStruct((blocks,) + wout.shape, bf16),
        ],
        in_specs=[vmem] * 9 + [hbm] * 3,
        out_specs=[vmem] * 6 + [hbm] * 3,
        scratch_shapes=[
            pltpu.VMEM((4, width, rows), bf16),
            pltpu.VMEM((n, group, rows), bf16),
            pltpu.VMEM((length, 128), bf16),
            pltpu.VMEM((128, length), bf16),
            pltpu.VMEM((length, 128), bf16),
            pltpu.VMEM((BLK, 2 * BLK), f32),
            pltpu.VMEM((BLK, length), f32),
            pltpu.VMEM((table.shape[0], 2 * BLK), f32),
            dma((2, 4, n - 1)),
            dma((2, heads, n - 1)),
            dma((2,)),
            dma((2, far)),
            dma((2, far)),
            dma((2, experts - 1)),
            dma((3,)),
            dma((2, 2, 2, n)),
            dma((2, 2, 2, some, n)),
        ],
        compiler_params=pltpu.CompilerParams(
            collective_id=2, has_side_effects=True, vmem_limit_bytes=60 * 1024 * 1024
        ),
        name="front_pass",
    )(x, gain, wq, wk, wv, table, segments, routes, order, cot, win, wout)


def line_order(n):
    order = []
    for i in range((n + 1) // 2):
        order.append(n - 1 - i)
        if i != n - 1 - i:
            order.append(i)
    return order


def line_scatter(n, own, right, left, right_sems, left_sems, ready):
    me = lax.axis_index("ctx")
    items = {}
    for j in line_order(n):
        for r in range(j):
            items.setdefault(ready[j] + r, []).append((0, r, j))
        for r in range(n - 1, j, -1):
            items.setdefault(ready[j] + n - 1 - r, []).append((1, r, j))
    steps = max(items) + 1

    def pass_on(way, r, j):
        taken, sems = (right, right_sems) if way == 0 else (left, left_sems)
        first = 0 if way == 0 else n - 1
        return remote(
            own.at[j] if r == first else taken.at[j], taken.at[j], sems.at[0, j], sems.at[1, j],
            {"ctx": r + 1 if way == 0 else r - 1},
        )

    def advance(step):
        for way, r, j in items.get(step, []):
            @pl.when(me == r)
            def _():
                copy = pass_on(way, r, j)
                if r != (0 if way == 0 else n - 1):
                    taken = right if way == 0 else left
                    copy.wait_recv()
                    taken[j] = (taken[j].astype(f32) + own[j].astype(f32)).astype(bf16)
                copy.start()

    def finish(out):
        for j in range(n):
            @pl.when(me == j)
            def _():
                total = own[j].astype(f32)
                if j > 0:
                    pass_on(0, j - 1, j).wait_recv()
                    total = total + right[j].astype(f32)
                if j < n - 1:
                    pass_on(1, j + 1, j).wait_recv()
                    total = total + left[j].astype(f32)
                out[...] = total.astype(bf16)

    def drain():
        for step in range(steps):
            for way, r, j in items.get(step, []):
                @pl.when(me == r)
                def _():
                    pass_on(way, r, j).wait_send()

    return advance, finish, drain, steps


def back_kernel(
    heads, n, rows, x_ref, do_ref, table_ref, of_ref, lse_ref, base_ref, far_ref, gin_hbm, gout_hbm,
    cots_ref, diag_ref, ein_ref, own_b, out_ref,
    do_in, g_ref, qa, ka, va, da, qn, dn, bias, dq, gsum,
    own_a, side_a, side_b, right_a, left_a,
    do_sems, out_sems, own_sems, side_sems, right_sems, left_sems, lines, far_in, far_sems,
):
    size = 64
    group = heads * size
    length = n * rows
    sides = lax.axis_size("dp")
    me = lax.axis_index("ctx")
    side = lax.axis_index("dp")
    barrier, peers = greet(("ctx", "dp", "expert"))
    order = line_order(n)
    advance, finish, drain, steps = line_scatter(
        n, own_a, right_a, left_a, right_sems, left_sems, {j: i for i, j in enumerate(order)}
    )
    loads = {}
    for j in order:
        at = j * sides + side
        loads[j] = [
            pltpu.make_async_copy(gin_hbm.at[at], own_a.at[j], own_sems.at[0, j]),
            pltpu.make_async_copy(gout_hbm.at[at], own_b.at[j], own_sems.at[1, j]),
        ]
        for copy in loads[j]:
            copy.start()
    pl.semaphore_wait(barrier, peers)
    lanes, lane, core = expert_split()
    homes = [
        remote(
            far_ref.at[k - 1], far_in.at[k - 1], far_sems.at[0, k - 1], far_sems.at[1, k - 1],
            {"expert": lax.rem(lane - k + lanes, lanes) * 2 + core},
        )
        for k in range(1, lanes)
    ]
    for copy in homes:
        copy.start()
    lines[...] = bias_line(lax.broadcasted_iota(jnp.int32, (1, 2 * BLK), 1), table_ref[...])
    arriving = []
    for k in range(1, n):
        to = lax.rem(me + k, n)
        copy = remote(
            do_ref.at[pl.ds(pl.multiple_of(to * group, 16), group)], do_in.at[me], do_sems.at[0, k - 1], do_sems.at[1, k - 1], {"ctx": to}
        )
        copy.start()
        arriving.append(copy)
    beside = {}
    for v, gone, taken in ((0, gin_hbm, side_a), (1, gout_hbm, side_b)):
        for j in order:
            beside[v, j] = []
            for k in range(1, sides):
                to = lax.rem(side + k, sides)
                beside[v, j].append(
                    remote(
                        gone.at[j * sides + to], taken.at[k - 1, j],
                        side_sems.at[0, v, k - 1, j], side_sems.at[1, v, k - 1, j], {"dp": to},
                    )
                )
                beside[v, j][-1].start()

    def sum_sides(v, j):
        own, taken = ((own_a, side_a), (own_b, side_b))[v]
        loads[j][v].wait()
        total = own[j].astype(f32)
        for k in range(1, sides):
            beside[v, j][k - 1].wait_recv()
            total = total + taken[k - 1, j].astype(f32)
        own[j] = total.astype(bf16)

    do_in[me] = do_ref[pl.ds(pl.multiple_of(me * group, 16), group), :]

    sum_sides(0, order[0])
    advance(0)
    for copy in arriving:
        copy.wait_recv()

    def out_copy(h, kind, k):
        to = lax.rem(me + k, n)
        base = pl.multiple_of(h * size, size)
        return remote(
            g_ref.at[to, pl.ds(kind * group + base, size)],
            cots_ref.at[pl.ds(pl.multiple_of(kind * n * group + me * group + base, 16), size)],
            out_sems.at[0, h, kind, k - 1],
            out_sems.at[1, h, kind, k - 1],
            {"ctx": to},
        )

    def head(h, carry):
        base = pl.multiple_of(h * size, size)
        for s in range(n):
            at = slice(s * rows, (s + 1) * rows)
            q = x_ref[s, pl.ds(base, size), :] * jnp.asarray(0.125, bf16)
            k = x_ref[s, pl.ds(base + group, size), :]
            v = x_ref[s, pl.ds(base + 2 * group, size), :]
            d = do_in[s, pl.ds(base, size), :]
            seg = x_ref[s, 3 * group : 3 * group + 16, :]
            mask, hot = seg_mask_rows(seg)
            which = lax.broadcasted_iota(jnp.int32, (16, rows), 0)

            def rows3(vec):
                hi, mid, lo = split3(jnp.broadcast_to(vec, (16, rows)))
                return jnp.where(which == 0, hi, jnp.where(which == 1, mid, jnp.where(which == 2, lo, jnp.zeros((), bf16))))

            ones = jnp.where(which < 3, 1.0, 0.0).astype(bf16)
            zeros = jnp.zeros((32, rows), bf16)
            zeros48 = jnp.zeros((48, rows), bf16)
            lse = lse_ref[pl.ds(h, 1), at]
            delta = jnp.sum(of_ref[pl.ds(base, size), at] * d.astype(f32), axis=0, keepdims=True)
            qt = jnp.concatenate([q, mask, rows3(-lse), zeros], axis=0)
            qa[:, at] = qt
            qn[at, :] = qt.T
            ka[at, :] = jnp.concatenate([k, hot, ones, zeros], axis=0).T
            dt = jnp.concatenate([d, rows3(-delta), zeros48], axis=0)
            da[:, at] = dt
            dn[at, :] = dt.T
            va[at, :] = jnp.concatenate([v, ones, zeros48], axis=0).T
        line = jnp.broadcast_to(lines[pl.ds(me * heads + h, 1), :], (BLK, 2 * BLK))
        rolled = pltpu.roll(line, 0, 1, stride=1, stride_axis=0)
        r = lax.broadcasted_iota(jnp.int32, (BLK, 2 * BLK), 0)
        c = lax.broadcasted_iota(jnp.int32, (BLK, 2 * BLK), 1)
        bias[...] = jnp.where(c < r, NEG, rolled)
        gsum[...] = jnp.zeros_like(gsum)
        for j in range(length // BLK):
            a0 = j * BLK
            kj = ka[a0 : a0 + BLK, :]
            vj = va[a0 : a0 + BLK, :]
            src, off = a0 // rows, a0 % rows
            kt = x_ref[src, pl.ds(base + group, size), off : off + BLK]
            dk = dv = None
            for a in range(a0, length, 2 * BLK):
                b = min(a + 2 * BLK, length)
                s = dot(kj, qa[:, a:b])
                if a == a0:
                    s = s + bias[:, : b - a]
                p = jnp.exp(s)
                ds = p * dot(vj, da[:, a:b])
                if a == a0:
                    gsum[:, : b - a] += ds
                p_low, ds_low = p.astype(bf16), ds.astype(bf16)
                u = dot(p_low, dn[a:b, :])
                dv = u if dv is None else dv + u
                u = dot(ds_low, qn[a:b, :])
                dk = u if dk is None else dk + u
                u = dot(kt, ds_low)
                if j == 0:
                    dq[:, a:b] = u
                else:
                    dq[:, a:b] += u
            g_ref[src, pl.ds(base + group, size), off : off + BLK] = dk.T[:size].astype(bf16)
            g_ref[src, pl.ds(base + 2 * group, size), off : off + BLK] = dv.T[:size].astype(bf16)
        for s in range(n):
            g_ref[s, pl.ds(base, size), :] = (dq[:, s * rows : (s + 1) * rows] * 0.125).astype(bf16)
        for kind in range(3):
            for k in range(1, n):
                out_copy(h, kind, k).start()
            cots_ref[pl.ds(pl.multiple_of(kind * n * group + me * group + base, 16), size), :] = g_ref[
                me, pl.ds(kind * group + base, size), :
            ]
        eight = gsum[0:8, :]
        for i in range(1, BLK // 8):
            eight = eight + pltpu.roll(gsum[8 * i : 8 * i + 8, :], 2 * BLK - 8 * i, 1)
        line = eight[0:1]
        for i in range(1, 8):
            line = line + pltpu.roll(eight, 2 * BLK - i, 1)[i : i + 1]
        diag_ref[pl.ds(h, 1), :] = line
        for step in range(1, heads):
            @pl.when(h == step - 1)
            def _():
                if step < n:
                    sum_sides(0, order[step])
                advance(step)

        return carry

    lax.fori_loop(0, heads, head, 0)
    for step in range(heads, steps):
        if step < n:
            sum_sides(0, order[step])
        advance(step)
        if step >= n and step - n < n:
            sum_sides(1, order[step - n])
    for i in range(max(steps - n, 0), n):
        sum_sides(1, order[i])
    mixture = base_ref[...]
    for k in range(1, lanes):
        homes[k - 1].wait()
        mixture = mixture + far_in[k - 1].astype(f32)
    out_ref[...] = mixture.astype(bf16)
    finish(ein_ref)
    for h in range(heads):
        for kind in range(3):
            for k in range(1, n):
                out_copy(h, kind, k).wait()
    for copy in arriving:
        copy.wait_send()
    for copies in beside.values():
        for copy in copies:
            copy.wait_send()
    drain()


def back_pass(x, do, table, of, lse, base, far, gin, gout):
    n, depth, rows = x.shape
    heads = table.shape[0] // n
    group = heads * 64
    length = n * rows
    sides = lax.axis_size("dp")
    _, high_a, wide_a = gin.shape
    _, high_b, wide_b = gout.shape
    vmem = pl.BlockSpec(memory_space=pltpu.VMEM)
    hbm = pl.BlockSpec(memory_space=pl.ANY)
    dma = pltpu.SemaphoreType.DMA
    some = max(sides - 1, 1)
    return pl.pallas_call(
        partial(back_kernel, heads, n, rows),
        out_shape=[
            jax.ShapeDtypeStruct((3 * n * group, rows), bf16),
            jax.ShapeDtypeStruct((heads, 2 * BLK), f32),
            jax.ShapeDtypeStruct((high_a, wide_a), bf16),
            jax.ShapeDtypeStruct((n, high_b, wide_b), bf16),
            jax.ShapeDtypeStruct(base.shape, bf16),
        ],
        in_specs=[vmem] * 7 + [hbm] * 2,
        out_specs=[vmem] * 5,
        scratch_shapes=[
            pltpu.VMEM((n, group, rows), bf16),
            pltpu.VMEM((n, 3 * group, rows), bf16),
            pltpu.VMEM((128, length), bf16),
            pltpu.VMEM((length, 128), bf16),
            pltpu.VMEM((length, 128), bf16),
            pltpu.VMEM((128, length), bf16),
            pltpu.VMEM((length, 128), bf16),
            pltpu.VMEM((length, 128), bf16),
            pltpu.VMEM((BLK, 2 * BLK), f32),
            pltpu.VMEM((64, length), f32),
            pltpu.VMEM((BLK, 2 * BLK), f32),
            pltpu.VMEM((n, high_a, wide_a), bf16),
            pltpu.VMEM((some, n, high_a, wide_a), bf16),
            pltpu.VMEM((some, n, high_b, wide_b), bf16),
            pltpu.VMEM((n, high_a, wide_a), bf16),
            pltpu.VMEM((n, high_a, wide_a), bf16),
            dma((2, n - 1)),
            dma((2, heads, 3, n - 1)),
            dma((2, n)),
            dma((2, 2, some, n)),
            dma((2, n)),
            dma((2, n)),
            pltpu.VMEM((table.shape[0], 2 * BLK), f32),
            pltpu.VMEM(far.shape, bf16),
            dma((2, far.shape[0])),
        ],
        compiler_params=pltpu.CompilerParams(
            collective_id=3, has_side_effects=True, vmem_limit_bytes=60 * 1024 * 1024
        ),
        name="back_pass",
    )(x, do, table, of, lse, base, far, gin, gout)


def add_all(parts):
    return functools.reduce(lambda a, b: a + b, parts)


def axis_stages():
    experts = lax.axis_size("expert")
    me = lax.axis_index("expert")
    core, lane = lax.rem(me, 2), lax.div(me, 2)
    return {
        "core": (2, core, lambda j: {"expert": lane * 2 + j}),
        "lane": (experts // 2, lane, lambda j: {"expert": j * 2 + core}),
        "dp": (lax.axis_size("dp"), lax.axis_index("dp"), lambda j: {"dp": j}),
        "ctx": (lax.axis_size("ctx"), lax.axis_index("ctx"), lambda j: {"ctx": j}),
    }


ORDERS = (("core", "lane", "dp", "ctx"), ("core", "dp", "lane", "ctx"))
SLICES = 2


def sum_plan(sizes, rows):
    plans = []
    for order in ORDERS:
        length, plan = rows // 2, []
        for name in order:
            count = sizes[name]
            split = length % count == 0 and (length // count) % 16 == 0
            plan.append((name, count, length, split))
            if split:
                length = length // count
        plans.append(plan)
    return plans


def received_rows(plans):
    return [
        [(count - 1) * (length // count if split else length) for (_, count, length, split) in plan]
        for plan in plans
    ]


def sizes_of():
    return {
        "core": 2,
        "lane": lax.axis_size("expert") // 2,
        "dp": lax.axis_size("dp"),
        "ctx": lax.axis_size("ctx"),
    }


def tail_kernel(
    plans, normed_t, cots, mixed_t, wq, wk, wv, x_ref, gain_ref, hidden_cot_ref, moe_small_ref, diag_ref, sums_ref,
    grads_ref, input_grad_ref, small_out_ref, eout_ref,
    acc, whole, taken_a, taken_b, small, small_taken, send, recv, back_send, back_recv, small_send, small_recv,
    right, left, right_sems, left_sems,
):
    stages = axis_stages()
    width = wq.shape[0]
    rows = x_ref.shape[0]
    barrier = pltpu.get_barrier_semaphore()
    peers = 0
    for name, (count, me, at) in stages.items():
        for k in range(1, count):
            pl.semaphore_signal(barrier, inc=1, device_id=at(lax.rem(me + k, count)), device_id_type=pl.DeviceIdType.MESH)
            peers += 1

    def make(k):
        if k < 3:
            acc[k * width : (k + 1) * width, :] = dot(
                normed_t[...], cots[k * width : (k + 1) * width, :], NT
            ).astype(bf16)
        else:
            acc[3 * width :, :] = dot(mixed_t[...], hidden_cot_ref[...].astype(bf16)).astype(bf16)

    taken = (taken_a, taken_b)
    half = 2 * width
    piece = width // SLICES
    parts = [(h, c) for c in range(SLICES) for h in range(2)]
    spans = {}
    for part in parts:
        spans[part] = [part[0] * half]

    def columns(part):
        return pl.ds(part[1] * piece, piece)

    def rows_at(start, size):
        return pl.ds(pl.multiple_of(start, 16), size)

    flying = {}

    def send_stage(part, step):
        h, c = part
        name, count, length, split = plans[h][step]
        _, me, at = stages[name]
        start = spans[part][-1]
        size = length // count if split else length
        base = sum(received[h][:step])
        copies = []
        for k in range(1, count):
            peer = lax.rem(me + k, count)
            copies.append(
                pltpu.make_async_remote_copy(
                    src_ref=acc.at[rows_at(start + peer * size if split else start, size), columns(part)],
                    dst_ref=taken[h].at[pl.ds(base + (k - 1) * size, size), columns(part)],
                    send_sem=send.at[h * SLICES + c, step, k - 1],
                    recv_sem=recv.at[h * SLICES + c, step, k - 1],
                    device_id=at(peer),
                    device_id_type=pl.DeviceIdType.MESH,
                )
            )
        for copy in copies:
            copy.start()
        flying[part] = copies

    def add_stage(part, step):
        h, c = part
        name, count, length, split = plans[h][step]
        _, me, at = stages[name]
        size = length // count if split else length
        start = spans[part][-1] + me * size if split else spans[part][-1]
        base = sum(received[h][:step])
        for copy in flying[part]:
            copy.wait()
        total = acc[rows_at(start, size), columns(part)].astype(f32)
        for k in range(1, count):
            total = total + taken[h][base + (k - 1) * size : base + k * size, columns(part)].astype(f32)
        if step == len(plans[h]) - 1:
            whole[rows_at(start, size), columns(part)] = total.astype(bf16)
        else:
            acc[rows_at(start, size), columns(part)] = total.astype(bf16)
        spans[part].append(start)

    def give_stage(part, step):
        h, c = part
        name, count, length, split = plans[h][step]
        if not split:
            flying[part] = []
            return
        _, me, at = stages[name]
        size = length // count
        start = spans[part][step + 1]
        copies = []
        for k in range(1, count):
            peer = lax.rem(me + k, count)
            copies.append(
                pltpu.make_async_remote_copy(
                    src_ref=whole.at[rows_at(start, size), columns(part)],
                    dst_ref=whole.at[rows_at(start, size), columns(part)],
                    send_sem=back_send.at[h * SLICES + c, step, k - 1],
                    recv_sem=back_recv.at[h * SLICES + c, step, k - 1],
                    device_id=at(peer),
                    device_id_type=pl.DeviceIdType.MESH,
                )
            )
        for copy in copies:
            copy.start()
        flying[part] = copies

    n = sums_ref.shape[0]
    advance, finish, drain, line_steps = line_scatter(n, sums_ref, right, left, right_sems, left_sems, [0] * n)
    received = received_rows(plans)
    make(2)
    make(3)
    pl.semaphore_wait(barrier, peers)
    for c in range(SLICES):
        send_stage((1, c), 0)
    advance(0)
    make(0)
    make(1)
    for c in range(SLICES):
        send_stage((0, c), 0)
    parts = [(1, 0), (0, 0), (1, 1), (0, 1)]

    def make_small():
        turned = dot(wq[...], cots[:width, :]) + dot(wk[...], cots[width : 2 * width, :]) + dot(wv[...], cots[2 * width :, :])
        cot = turned.T
        x = x_ref[...].astype(f32)
        gain = gain_ref[...].reshape(1, width)
        scale = lax.rsqrt(jnp.mean(x * x, axis=1, keepdims=True) + EPSILON)
        unit = x * scale
        gained = cot * gain
        input_grad_ref[...] = hidden_cot_ref[...] + scale * (gained - unit * jnp.mean(unit * gained, axis=1, keepdims=True))
        gain_grad = jnp.sum(unit * cot, axis=0, keepdims=True)
        which = lax.broadcasted_iota(jnp.int32, (8, width), 0)
        low = jnp.where(which == 0, gain_grad, jnp.where(which == 1, moe_small_ref[0:8, :], 0.0))
        near_rows, near_lanes = 128, 256
        distance = lax.broadcasted_iota(jnp.int32, (near_rows, near_lanes), 0)
        lane = lax.broadcasted_iota(jnp.int32, (near_rows, near_lanes), 1)
        far = jnp.full(distance.shape, BUCKETS // 2, jnp.int32)
        for limit in THRESHOLDS:
            far = far + jnp.where(distance >= limit, 1, 0)
        bucket = jnp.where(distance < BUCKETS // 2, distance, far)
        own = distance < THRESHOLDS[-1]
        lane_row = lax.broadcasted_iota(jnp.int32, (1, near_lanes), 1)
        which = lax.broadcasted_iota(jnp.int32, (8, near_lanes), 0)
        sums = jnp.zeros((8, near_lanes), f32)
        heads = diag_ref.shape[0]
        for h in range(heads):
            at = lax.axis_index("ctx") * heads + h
            start = lax.div(at, 6) * 128
            hot = jnp.where(own & (bucket + start == lane), 1.0, 0.0).astype(bf16)
            three = split3(jnp.broadcast_to(diag_ref[h : h + 1, :near_rows], (16, near_rows)))
            near = (dot(three[0], hot) + dot(three[1], hot) + dot(three[2], hot))[0:1]
            near = jnp.where(lane_row == start + BUCKETS - 1, -jnp.sum(near, axis=1, keepdims=True), near)
            sums = sums + jnp.where(which == 2 + lax.rem(at, 6), near, 0.0)
        low = low + jnp.concatenate([sums, jnp.zeros((8, width - near_lanes), f32)], axis=1)
        small[0:8, :] = low
        small[8:16, :] = moe_small_ref[8:16, :]

    def send_small(step):
        name = ORDERS[0][step]
        count, me, at = stages[name]
        base = sum(stages[n][0] - 1 for n in ORDERS[0][:step])
        copies = [
            pltpu.make_async_remote_copy(
                src_ref=small,
                dst_ref=small_taken.at[base + k - 1],
                send_sem=small_send.at[base + k - 1],
                recv_sem=small_recv.at[base + k - 1],
                device_id=at(lax.rem(me + k, count)),
                device_id_type=pl.DeviceIdType.MESH,
            )
            for k in range(1, count)
        ]
        for copy in copies:
            copy.start()
        flying["small"] = copies

    def add_small(step):
        base = sum(stages[n][0] - 1 for n in ORDERS[0][:step])
        for copy in flying["small"]:
            copy.wait()
        total = small[...]
        for k in range(len(flying["small"])):
            total = total + small_taken[base + k]
        small[...] = total

    last = len(ORDERS[0])
    for step in range(last):
        for part in parts:
            add_stage(part, step)
            if step + 1 < last:
                send_stage(part, step + 1)
            else:
                give_stage(part, step)
        if step == 0:
            make_small()
        else:
            add_small(step - 1)
        send_small(step)
        if step == 1:
            advance(1)
    for step in range(2, line_steps):
        advance(step)
    for step in range(last - 1, -1, -1):
        for part in parts:
            for copy in flying[part]:
                copy.wait()
            if step > 0:
                give_stage(part, step - 1)
        if step == last - 1:
            add_small(last - 1)
            small_out_ref[...] = small[...]
    finish(eout_ref)
    drain()
    grads_ref[...] = whole[...]


def tail_pass(normed_t, cots, mixed_t, wq, wk, wv, x, gain, hidden_cot, moe_small, diag, sums):
    rows, width = x.shape
    sizes = sizes_of()
    plans = sum_plan(sizes, 4 * width)
    received = [sum(r) for r in received_rows(plans)]
    most = max(sizes.values()) - 1
    few = sum(n - 1 for n in sizes.values())
    small = jax.ShapeDtypeStruct((16, width), f32)
    return pl.pallas_call(
        partial(tail_kernel, plans),
        out_shape=[
            jax.ShapeDtypeStruct((4 * width, width), bf16),
            jax.ShapeDtypeStruct((rows, width), f32),
            jax.ShapeDtypeStruct(small.shape, f32),
            jax.ShapeDtypeStruct(sums.shape[1:], bf16),
        ],
        in_specs=[pl.BlockSpec(memory_space=pltpu.VMEM)] * 12,
        out_specs=[pl.BlockSpec(memory_space=pltpu.VMEM)] * 4,
        scratch_shapes=[
            pltpu.VMEM((4 * width, width), bf16),
            pltpu.VMEM((4 * width, width), bf16),
            pltpu.VMEM((received[0], width), bf16),
            pltpu.VMEM((received[1], width), bf16),
            pltpu.VMEM(small.shape, f32),
            pltpu.VMEM((few,) + small.shape, f32),
            pltpu.SemaphoreType.DMA((2 * SLICES, 4, most)),
            pltpu.SemaphoreType.DMA((2 * SLICES, 4, most)),
            pltpu.SemaphoreType.DMA((2 * SLICES, 4, most)),
            pltpu.SemaphoreType.DMA((2 * SLICES, 4, most)),
            pltpu.SemaphoreType.DMA((few,)),
            pltpu.SemaphoreType.DMA((few,)),
            pltpu.VMEM(sums.shape, bf16),
            pltpu.VMEM(sums.shape, bf16),
            pltpu.SemaphoreType.DMA((2, sums.shape[0])),
            pltpu.SemaphoreType.DMA((2, sums.shape[0])),
        ],
        compiler_params=pltpu.CompilerParams(
            collective_id=0, has_side_effects=True, vmem_limit_bytes=56 * 1024 * 1024
        ),
        name="tail_pass",
    )(normed_t, cots, mixed_t, wq, wk, wv, x, gain, hidden_cot, moe_small, diag, sums)


def finish_kernel(heads, width, large_ref, small_ref, *refs):
    extra = (len(refs) - 7) // 2
    ins, outs, others = refs[:extra], refs[extra : extra + 7], refs[extra + 7 :]
    for k in range(4):
        outs[k][...] = large_ref[k].astype(f32)
    for source, out in zip(ins, others):
        out[...] = source[...].astype(f32)

    @pl.when(pl.program_id(0) == 0)
    def _():
        outs[4][...] = small_ref[0:1, :].reshape(width)
        outs[5][...] = small_ref[1:2, :].reshape(width)
        for a in range(0, heads, 6):
            outs[6][a : a + 6, :] = small_ref[2:8, a // 6 * 128 : a // 6 * 128 + BUCKETS]


def finish_pass(large, small, heads, extra):
    _, width, _ = large.shape
    steps = 6
    tall = width // steps
    whole = pl.BlockSpec(small.shape, lambda i: (0, 0))

    def cut(array):
        return pl.BlockSpec((array.shape[0] // steps, array.shape[1]), lambda i: (i, 0))

    flat = pl.BlockSpec((width,), lambda i: (0,))
    return pl.pallas_call(
        partial(finish_kernel, heads, width),
        grid=(steps,),
        out_shape=[jax.ShapeDtypeStruct((width, width), f32)] * 4
        + [jax.ShapeDtypeStruct((width,), f32)] * 2
        + [jax.ShapeDtypeStruct((heads, BUCKETS), f32)]
        + [jax.ShapeDtypeStruct(array.shape, f32) for array in extra],
        in_specs=[pl.BlockSpec((4, tall, width), lambda i: (0, i, 0)), whole] + [cut(array) for array in extra],
        out_specs=[pl.BlockSpec((tall, width), lambda i: (i, 0))] * 4
        + [flat] * 2
        + [pl.BlockSpec((heads, BUCKETS), lambda i: (0, 0))]
        + [cut(array) for array in extra],
        compiler_params=pltpu.CompilerParams(vmem_limit_bytes=32 * 1024 * 1024),
        name="finish_pass",
    )(large, small, *extra)


def local(
    layer_input,
    cotangent,
    norm_gain_one,
    w_query,
    w_key,
    w_value,
    w_output,
    rel_table,
    norm_gain_two,
    w_router,
    w_expert_in,
    w_expert_out,
    segment_ids,
    routes,
    priority,
):
    rows, width = layer_input.shape[1:]
    heads = rel_table.shape[0]
    shards = lax.axis_size("ctx")
    experts = lax.axis_size("expert")
    capacity = min(rows, 5 * rows // (2 * experts))
    blocks = shards * lax.axis_size("dp")

    def padded(array):
        return jnp.pad(array, ((0, 0), (0, -array.shape[1] % 16), (0, 0)))

    held, mixed_t, attended_whole, lse, normed_t, info_all, cots_all, inner_weight, outer_weight = front_pass(
        layer_input[0], norm_gain_one, w_query, w_key, w_value, rel_table, segment_ids, routes[0].T, priority[0],
        cotangent[0], padded(w_expert_in)[0], padded(w_expert_out)[0],
    )
    inner_weight = inner_weight[:, : w_expert_in.shape[1]].reshape(width, -1)
    outer_weight = outer_weight[:, : w_expert_out.shape[1]].reshape(-1, width)
    router_t = jnp.pad(w_router.T, ((0, 16 - experts), (0, 0)))
    base, far, hidden_cot, mixed_cot, moe_small, inner_grad, outer_grad = moe_pass(
        capacity, mixed_t, w_output, layer_input[0], cotangent[0], norm_gain_two, router_t, info_all, cots_all, inner_weight, outer_weight
    )

    def cut(array):
        return padded(array.reshape(blocks, array.shape[0] // blocks, array.shape[1]))

    cots, diagonals, expert_in_grad, expert_out_sums, layer_output = back_pass(
        held, mixed_cot, rel_table, attended_whole, lse, base, far, cut(inner_grad), cut(outer_grad)
    )
    large, input_grad, small, expert_out_grad = tail_pass(
        normed_t, cots, mixed_t, w_query, w_key, w_value, layer_input[0], norm_gain_one, hidden_cot, moe_small, diagonals, expert_out_sums
    )
    extra = [expert_in_grad, expert_out_grad]
    fits = [array.shape[0] % 96 == 0 for array in extra]
    finished = finish_pass(
        large.reshape(4, width, width), small, heads, [array for array, fit in zip(extra, fits) if fit]
    )
    converted = list(finished[7:])
    extra = [converted.pop(0) if fit else array.astype(f32) for array, fit in zip(extra, fits)]
    return (
        layer_output[None],
        input_grad[None],
        finished[4],
        finished[0],
        finished[1],
        finished[2],
        finished[3],
        finished[6],
        finished[5],
        small[8 : 8 + experts].T,
        extra[0][None, : w_expert_in.shape[1]],
        extra[1][None, : w_expert_out.shape[1]],
    )


def solution(mesh):
    placed = (
        P(("expert", "dp"), "ctx", None),
        P(("expert", "dp"), "ctx", None),
        P(),
        P(),
        P(),
        P(),
        P(),
        P(),
        P(),
        P(),
        P("expert", ("ctx", "dp"), None),
        P("expert", ("ctx", "dp"), None),
        P(("expert", "dp"), "ctx"),
        P(("expert", "dp"), "ctx", None),
        P(("expert", "dp"), "ctx", None),
    )
    return jax.shard_map(
        local,
        mesh=mesh,
        in_specs=placed,
        out_specs=(
            P(("expert", "dp"), "ctx", None),
            P(("expert", "dp"), "ctx", None),
            P(),
            P(),
            P(),
            P(),
            P(),
            P(),
            P(),
            P(),
            P("expert", ("ctx", "dp"), None),
            P("expert", ("ctx", "dp"), None),
        ),
        check_vma=False,
    )
```

```python
import functools
from functools import partial

import jax
import jax.numpy as jnp
from jax import lax
from jax.experimental import pallas as pl
from jax.experimental.pallas import tpu as pltpu
from jax.sharding import PartitionSpec as P

bf16 = jnp.bfloat16
f32 = jnp.float32
HIGH_PRECISION = lax.Precision.HIGHEST
EPSILON = 1e-06
THRESHOLDS = (19, 21, 24, 27, 31, 35, 40, 46, 52, 59, 67, 77, 87, 99, 113)
BUCKETS=32
NEG=-1e30
BLK=256
NT=(((1,),(1,)),((),()))
TN=(((0,),(0,)),((),()))

def dot(a,b,dims=(((1,),(0,)),((),()))):
    return lax.dot_general(a,b,dims,preferred_element_type=f32)

def seg_mask_rows(seg):
    which = lax.broadcasted_iota(jnp.int32, seg.shape, 0).astype(f32)
    same = seg.astype(f32) == which
    return jnp.where(same, 0.0, NEG).astype(bf16), jnp.where(same, 1.0, 0.0).astype(bf16)

def split3(v):
    hi = v.astype(bf16); rest = v - hi.astype(f32)
    mid = rest.astype(bf16); rest = rest - mid.astype(f32)
    return hi, mid, rest.astype(bf16)

ROOT = 0.7978845608028654


def remote(src, dst, send_sem, recv_sem, where):
    return pltpu.make_async_remote_copy(
        src_ref=src,
        dst_ref=dst,
        send_sem=send_sem,
        recv_sem=recv_sem,
        device_id=where,
        device_id_type=pl.DeviceIdType.MESH,
    )


def expert_split():
    experts = lax.axis_size("expert")
    me = lax.axis_index("expert")
    return experts // 2, lax.div(me, 2), lax.rem(me, 2)


def gather_start(piece, whole, near_sems, far_sems, rows=None):
    lanes, lane, core = expert_split()
    me = lane * 2 + core
    view = whole.at[me] if rows is None else whole.at[me, rows]
    copies = [remote(piece, view, near_sems.at[0], near_sems.at[1], {"expert": lane * 2 + 1 - core})]
    for k in range(1, lanes):
        copies.append(
            remote(piece, view, far_sems.at[0, k - 1], far_sems.at[1, k - 1], {"expert": lax.rem(lane + k, lanes) * 2 + core})
        )
    for copy in copies:
        copy.start()
    return copies


def relay(k, whole, sems):
    lanes, lane, core = expert_split()
    source = lax.rem(lane - k + lanes, lanes) * 2 + core
    return remote(whole.at[source], whole.at[source], sems.at[0, k - 1], sems.at[1, k - 1], {"expert": lane * 2 + 1 - core})


def greet(names):
    barrier = pltpu.get_barrier_semaphore()
    total = 0
    for name in names:
        count, at = lax.axis_size(name), lax.axis_index(name)
        for k in range(1, count):
            pl.semaphore_signal(
                barrier, inc=1, device_id={name: lax.rem(at + k, count)}, device_id_type=pl.DeviceIdType.MESH
            )
        total += count - 1
    return barrier, total


def moe_kernel(
    capacity, mixed_t, w_output, x_ref, cot_ref, gain_ref, router_ref, info_ref, cots_hbm, inner_hbm, outer_hbm,
    base_ref, far_ref, hidden_cot_ref, mixed_cot_ref, small_ref, gin_hbm, gout_hbm,
    nt, cots, inner, outer, act_all, pre_all, rows_all, cots_all, made, back, part, pair_in, total,
    core_in, far_in, gate_out, gate_in,
    load_sems, cot_sems, near_sems, far_sems, relay_sems, pair_sems, core_sems, back_sems, gate_sems, stage_sems, free_sem, late_sems, router_rows,
):
    experts = lax.axis_size("expert")
    lanes, lane, core = expert_split()
    me = lane * 2 + core
    other = lane * 2 + 1 - core
    rows, width = cot_ref.shape
    hidden = hidden_cot_ref
    pieces = 2
    step_rows = rows // pieces
    hidden_size = inner.shape[1]
    n = lax.axis_size("ctx")
    place_z = lax.axis_index("ctx")
    wide = hidden_size // n

    first = pltpu.make_async_copy(inner_hbm, inner, load_sems.at[n])
    first.start()

    def chunk_rows(j):
        return pl.ds(pl.multiple_of(j * wide, wide), wide)

    def chunk_at(f):
        return jnp.where(place_z == n - 1, n - 1 - f, f)

    def has(f):
        return (f < n - 1) | ((place_z > 0) & (place_z < n - 1))

    def load(f):
        at = chunk_rows(chunk_at(f))
        return pltpu.make_async_copy(outer_hbm.at[at], outer.at[at], load_sems.at[f])

    for f in range(n):
        @pl.when(has(f))
        def _():
            load(f).start()

    def late(up):
        at = chunk_rows(0 if up else n - 1)
        return remote(
            outer_hbm.at[at], outer.at[at], late_sems.at[0, int(up)], late_sems.at[1, int(up)],
            {"ctx": n - 1 if up else 0},
        )

    barrier, peers = greet(("expert", "ctx"))
    pl.semaphore_wait(barrier, peers)

    @pl.when(place_z == n - 2)
    def _():
        late(True).start()

    @pl.when(place_z == 1)
    def _():
        late(False).start()

    sent = []
    for p in range(pieces):
        at = slice(p * step_rows, (p + 1) * step_rows)
        now = x_ref[at, :].astype(f32) + dot(mixed_t[:, at], w_output[...], TN)
        hidden[at, :] = now
        scale = lax.rsqrt(jnp.mean(now * now, axis=1, keepdims=True) + EPSILON)
        nt[me, at, :] = (now * scale * gain_ref[...].reshape(1, width)).astype(bf16)
        sent.append(gather_start(nt.at[me, at], nt, near_sems.at[p], far_sems.at[p], at))

    router_rows[...] = jnp.zeros_like(router_rows)
    router_rows[0:experts, :] = router_ref[...].astype(f32)
    router = router_rows[...].astype(bf16)

    def gate_rows(source):
        logits = dot(router, nt[source], NT)
        which = lax.broadcasted_iota(jnp.int32, logits.shape, 0)
        info = info_ref[source]
        chosen = (which == info[0:1]) | (which == info[1:2])
        top = jnp.max(jnp.where(chosen, logits, NEG), axis=0, keepdims=True)
        power = jnp.where(chosen, jnp.exp(jnp.minimum(logits - top, 0.0)), 0.0)
        return power / jnp.sum(power, axis=0, keepdims=True)

    def pair_of(k):
        return [lax.rem(lane - k + lanes, lanes) * 2 + sc for sc in range(2)]

    order = pair_of(1) + [me, other]
    for k in range(2, lanes):
        order += pair_of(k)
    first_group = 4

    def fetch(i):
        return pltpu.make_async_copy(cots_hbm.at[order[i]], cots.at[i % first_group], cot_sems.at[i % first_group])

    for i in range(first_group):
        fetch(i).start()

    def place_of(i):
        info = info_ref[order[i]]
        place = jnp.where(info[0:1] == me, info[2:3], jnp.where(info[1:2] == me, info[3:4], -1))
        slot = lax.broadcasted_iota(jnp.int32, (capacity, rows), 0)
        pick = jnp.where(slot == place, 1.0, 0.0)
        gates = gate_rows(order[i])
        which = lax.broadcasted_iota(jnp.int32, gates.shape, 0)
        own_gate = jnp.sum(jnp.where(which == me, gates, 0.0), axis=0, keepdims=True)
        return place, pick, jnp.sum(pick * own_gate, axis=1, keepdims=True)

    def dispatch(i):
        fetch(i).wait()
        _, pick, slot_gate = place_of(i)
        block = slice(i * capacity, (i + 1) * capacity)
        rows_all[block, :] = dot(pick.astype(bf16), nt[order[i]]).astype(bf16)
        cots_all[block, :] = (slot_gate * dot(pick.astype(bf16), cots[i % first_group])).astype(bf16)
        made[i % first_group] = jnp.zeros((capacity, width), f32)
        back[i % first_group] = jnp.zeros((capacity, width), f32)

    def part_of(i, f):
        block = pl.ds(i * capacity if isinstance(i, int) else pl.multiple_of(i * capacity, 16), capacity)
        at = chunk_rows(chunk_at(f))
        turn = i % first_group if isinstance(i, int) else i
        pre = dot(rows_all[block, :], inner[:, at])
        cot = dot(cots_all[block, :], outer[at, :], NT)
        square = pre * pre
        t = jnp.tanh(pre * (ROOT + (ROOT * 0.044715) * square))
        half = 0.5 + 0.5 * t
        act = (pre * half).astype(bf16)
        slope = half + (0.5 * pre) * (1.0 - t * t) * (ROOT + (ROOT * 3 * 0.044715) * square)
        back_pre = (cot * slope).astype(bf16)
        act_all[block, at] = act
        pre_all[block, at] = back_pre
        made[turn] += dot(act, outer[at, :])
        back[turn] += dot(back_pre, inner[:, at], NT)

    def finish_source(i, target):
        place, pick, slot_gate = place_of(i)
        outcome = made[i % first_group].astype(bf16).astype(f32)
        slot_cot = jnp.sum(dot(pick.astype(bf16), cots[i % first_group]) * outcome, axis=1, keepdims=True)
        gate_out[order[i]] = jnp.broadcast_to(jnp.sum(pick * slot_cot, axis=0, keepdims=True), (8, rows))
        column = jnp.broadcast_to(place.astype(f32), (128, rows)).T[:, 0:1]
        lane_at = lax.broadcasted_iota(jnp.int32, (rows, capacity), 1).astype(f32)
        put = jnp.where(lane_at == column, 1.0, 0.0).astype(bf16)
        target[0] = dot(put, back[i % first_group].astype(bf16)).astype(bf16)
        target[1] = dot(put, (slot_gate * outcome).astype(bf16)).astype(bf16)
        if i + first_group < len(order):
            fetch(i + first_group).start()

    def process(i, target):
        dispatch(i)

        def step(f, carry):
            part_of(i, f)
            return carry

        lax.fori_loop(0, n, step, 0)
        finish_source(i, target)

    def pair_copies(k, sc):
        return [
            remote(part.at[sc, v], pair_in.at[v], pair_sems.at[0, v, k - 1], pair_sems.at[1, v, k - 1], {"expert": other})
            for v in range(2)
        ]

    def home_copy(k, sc):
        to = lax.rem(lane - k + lanes, lanes) * 2 + sc
        return remote(part.at[sc, 0], far_in.at[k - 1], back_sems.at[0, k - 1], back_sems.at[1, k - 1], {"expert": to})

    def begin_pair(k, sc):
        @pl.when(core != sc)
        def _():
            if k > 1:
                pl.semaphore_wait(free_sem, 1)
            for copy in pair_copies(k, sc):
                copy.start()

    def end_pair(k, sc):
        @pl.when(core == sc)
        def _():
            pair = pair_copies(k, sc)
            pair[0].wait_recv()
            part[sc, 0] = (part[sc, 0].astype(f32) + pair_in[0].astype(f32)).astype(bf16)
            home_copy(k, sc).start()
            pair[1].wait_recv()
            far_ref[k - 1] = (part[sc, 1].astype(f32) + pair_in[1].astype(f32)).astype(bf16)
            if k + 1 < lanes:
                pl.semaphore_signal(
                    free_sem, inc=1, device_id={"expert": other}, device_id_type=pl.DeviceIdType.MESH
                )

    def pair_sent(k):
        for sc in range(2):
            @pl.when(core != sc)
            def _():
                for copy in pair_copies(k, sc):
                    copy.wait_send()

    def home_sent(k):
        for sc in range(2):
            @pl.when(core == sc)
            def _():
                home_copy(k, sc).wait_send()

    dispatch(2)
    for p in range(pieces):
        sent[p][0].wait_recv()
    dispatch(3)
    first.wait()
    for f in range(n - 1):
        load(f).wait()

    def steps_of(start):
        def step(at, carry):
            part_of(start + lax.rem(at, 2), lax.div(at, 2))
            return carry

        return step

    lax.fori_loop(0, 2 * (n - 1), steps_of(2), 0)
    passed_on = []
    for k in range(1, lanes):
        for p in range(pieces):
            sent[p][k].wait_recv()
        passed = relay(k, nt, relay_sems)
        passed.start()
        passed_on.append(passed)

    def relayed(k, sc):
        @pl.when(core != sc)
        def _():
            passed_on[k - 1].wait_recv()

    for sc in range(2):
        relayed(1, sc)
        dispatch(sc)
    lax.fori_loop(0, 2 * (n - 1), steps_of(0), 0)

    @pl.when(has(n - 1))
    def _():
        load(n - 1).wait()

    @pl.when(place_z == n - 1)
    def _():
        late(True).wait_recv()

    @pl.when(place_z == 0)
    def _():
        late(False).wait_recv()

    lax.fori_loop(2 * (n - 1), 2 * n, steps_of(0), 0)
    finish_source(0, part.at[0])
    begin_pair(1, 0)
    finish_source(1, part.at[1])
    begin_pair(1, 1)
    end_pair(1, 0)
    lax.fori_loop(2 * (n - 1), 2 * n, steps_of(2), 0)
    end_pair(1, 1)
    pair_sent(1)
    finish_source(3, part.at[1 - core])
    core_copies = [
        remote(part.at[1 - core, v], core_in.at[v], core_sems.at[0, v], core_sems.at[1, v], {"expert": other}) for v in range(2)
    ]
    for copy in core_copies:
        copy.start()
    finish_source(2, total)

    def gate_copy(k):
        to = lax.rem(me + k, experts)
        return remote(gate_out.at[to], gate_in.at[me], gate_sems.at[0, k - 1], gate_sems.at[1, k - 1], {"expert": to})

    for k in range(2, lanes):
        if k == 2:
            for copy in core_copies:
                copy.wait_send()
        home_sent(k - 1)
        for sc in range(2):
            relayed(k, sc)
            process(2 * k + sc, part.at[sc])
            begin_pair(k, sc)
        for sc in range(2):
            end_pair(k, sc)
        pair_sent(k)
    gate_copies = [gate_copy(k) for k in range(1, experts)]
    for copy in gate_copies:
        copy.start()
    count = rows_all.shape[0]
    for b in range(count // 128):
        at = slice(b * 128, (b + 1) * 128)
        inner[:, at] = rows_all[at, :].T
        inner[:, slice(count + b * 128, count + (b + 1) * 128)] = cots_all[at, :].T
    wide = width
    steps = hidden_size // wide

    def store(f, v):
        at = pl.ds(pl.multiple_of(f * wide, wide), wide)
        return pltpu.make_async_copy(outer.at[v * width : (v + 1) * width], gin_hbm.at[:, at] if v == 0 else gout_hbm.at[at, :], stage_sems.at[v])

    def grads(f, carry):
        at = pl.ds(pl.multiple_of(f * wide, wide), wide)

        @pl.when(f > 0)
        def _():
            store(f - 1, 0).wait()

        outer[:width, :] = dot(inner[:, :count], pre_all[:, at]).astype(bf16)
        store(f, 0).start()

        @pl.when(f > 0)
        def _():
            store(f - 1, 1).wait()

        outer[width : 2 * width, :] = dot(inner[:, count : 2 * count], act_all[:, at]).astype(bf16).T
        store(f, 1).start()
        return carry

    lax.fori_loop(0, steps, grads, 0)
    for copy in gate_copies:
        copy.wait()
    gates = gate_rows(me)
    pad = gates.shape[0]
    which = lax.broadcasted_iota(jnp.int32, gates.shape, 0)
    gate_cot = jnp.where(which == me, gate_out[me][0:1], 0.0)
    for k in range(1, experts):
        source = lax.rem(me + k, experts)
        gate_cot = gate_cot + jnp.where(which == source, gate_in[source][0:1], 0.0)
    logit_cot = gates * (gate_cot - jnp.sum(gates * gate_cot, axis=0, keepdims=True))
    three = jnp.concatenate(split3(logit_cot), axis=0)
    router_three = jnp.concatenate([router] * 3, axis=0)
    router_grad = dot(three, nt[me])
    small_ref[8:, :] = router_grad[:pad] + router_grad[pad : 2 * pad] + router_grad[2 * pad :]
    for copy in core_copies:
        copy.wait_recv()
    for k in range(1, lanes):
        remote(part.at[0, 0], far_in.at[k - 1], back_sems.at[0, k - 1], back_sems.at[1, k - 1], {"expert": other}).wait_recv()
    gain = gain_ref[...].reshape(1, width)
    gain_grad = jnp.zeros((1, width), f32)
    for start in range(0, rows, 128):
        at = slice(start, start + 128)
        normed_cot = total[0, at, :].astype(f32) + core_in[0, at, :].astype(f32)
        for k in range(1, lanes):
            normed_cot = normed_cot + far_in[k - 1, at, :].astype(f32)
        normed_cot = normed_cot + dot(three[:, at], router_three, TN)
        now = hidden[at, :]
        scale = lax.rsqrt(jnp.mean(now * now, axis=1, keepdims=True) + EPSILON)
        unit = now * scale
        gained = normed_cot * gain
        hidden_cot = cot_ref[at, :].astype(f32) + scale * (gained - unit * jnp.mean(unit * gained, axis=1, keepdims=True))
        hidden_cot_ref[at, :] = hidden_cot
        mixed_cot_ref[:, at] = dot(w_output[...], hidden_cot.astype(bf16), NT).astype(bf16)
        gain_grad = gain_grad + jnp.sum(unit * normed_cot, axis=0, keepdims=True)
        base_ref[at, :] = now + (total[1, at, :].astype(f32) + core_in[1, at, :].astype(f32))
    small_ref[0:8, :] = jnp.broadcast_to(gain_grad, (8, width))
    store(steps - 1, 0).wait()
    store(steps - 1, 1).wait()
    home_sent(lanes - 1)
    if lanes == 2:
        for copy in core_copies:
            copy.wait_send()
    for copy in passed_on:
        copy.wait_send()
    for p in range(pieces):
        for copy in sent[p]:
            copy.wait_send()

    @pl.when(place_z == n - 2)
    def _():
        late(True).wait_send()

    @pl.when(place_z == 1)
    def _():
        late(False).wait_send()


def moe_pass(capacity, mixed_t, w_output, x, cot, gain, router, info, cots, inner, outer):
    rows, width = cot.shape
    experts = cots.shape[0]
    lanes = experts // 2
    hidden_size = inner.shape[1]
    total = experts * capacity
    vmem = pl.BlockSpec(memory_space=pltpu.VMEM)
    hbm = pl.BlockSpec(memory_space=pl.ANY)
    dma = pltpu.SemaphoreType.DMA
    far = max(lanes - 1, 1)
    return pl.pallas_call(
        partial(moe_kernel, capacity),
        out_shape=[
            jax.ShapeDtypeStruct((rows, width), f32),
            jax.ShapeDtypeStruct((far, rows, width), bf16),
            jax.ShapeDtypeStruct((rows, width), f32),
            jax.ShapeDtypeStruct((width, rows), bf16),
            jax.ShapeDtypeStruct((24, width), f32),
            jax.ShapeDtypeStruct((width, hidden_size), bf16),
            jax.ShapeDtypeStruct((hidden_size, width), bf16),
        ],
        in_specs=[vmem] * 7 + [hbm] * 3,
        out_specs=[vmem] * 5 + [hbm] * 2,
        scratch_shapes=[
            pltpu.VMEM((experts, rows, width), bf16),
            pltpu.VMEM((4, rows, width), bf16),
            pltpu.VMEM((width, hidden_size), bf16),
            pltpu.VMEM((hidden_size, width), bf16),
            pltpu.VMEM((total, hidden_size), bf16),
            pltpu.VMEM((total, hidden_size), bf16),
            pltpu.VMEM((total, width), bf16),
            pltpu.VMEM((total, width), bf16),
            pltpu.VMEM((4, capacity, width), f32),
            pltpu.VMEM((4, capacity, width), f32),
            pltpu.VMEM((2, 2, rows, width), bf16),
            pltpu.VMEM((2, rows, width), bf16),
            pltpu.VMEM((2, rows, width), bf16),
            pltpu.VMEM((2, rows, width), bf16),
            pltpu.VMEM((far, rows, width), bf16),
            pltpu.VMEM((experts, 8, rows), f32),
            pltpu.VMEM((experts, 8, rows), f32),
            dma((lax.axis_size("ctx") + 1,)),
            dma((4,)),
            dma((2, 2)),
            dma((2, 2, far)),
            dma((2, far)),
            dma((2, 2, far)),
            dma((2, 2)),
            dma((2, far)),
            dma((2, experts - 1)),
            dma((2,)),
            pltpu.SemaphoreType.REGULAR,
            dma((2, 2)),
            pltpu.VMEM((16, width), f32),
        ],
        compiler_params=pltpu.CompilerParams(
            collective_id=1, has_side_effects=True, vmem_limit_bytes=65000 * 1024
        ),
        name="moe_pass",
    )(mixed_t, w_output, x, cot, gain, router, info, cots, inner, outer)


def bias_line(distance, table):
    far = jnp.full(distance.shape, BUCKETS // 2, jnp.int32)
    for limit in THRESHOLDS:
        far = far + jnp.where(distance >= limit, 1, 0)
    bucket = jnp.where(distance < BUCKETS // 2, distance, far)
    own = (distance >= 0) & (distance < THRESHOLDS[-1])
    which = lax.broadcasted_iota(jnp.int32, (BUCKETS, distance.shape[1]), 0)
    hot = jnp.where(own & (which == bucket), 1.0, 0.0).astype(bf16)
    last = table[:, BUCKETS - 1 :].astype(f32)
    return dot(table, hot) - jnp.where(own, last, 0.0)


def column_of(row):
    return jnp.broadcast_to(row, (128, row.shape[1])).T


def front_kernel(
    heads, n, rows, x_ref, gain_ref, wq, wk, wv, table_ref, segment_ref, routes_ref, order_ref, cot_hbm, win_hbm, wout_hbm,
    held, mixed, of_ref, lse_ref, normed_t, infos, cots_hbm, win_all, wout_all,
    made, given, qa, ka, vn, bias, s_ref, lines,
    held_sems, mixed_sems, near_sems, far_sems, relay_sems, info_sems, own_sems, line_sems, side_sems,
):
    size = 64
    group = heads * size
    width = n * group
    length = n * rows
    sides = lax.axis_size("dp")
    me = lax.axis_index("ctx")
    side = lax.axis_index("dp")
    experts = lax.axis_size("expert")
    expert = lax.axis_index("expert")
    barrier = pltpu.get_barrier_semaphore()
    for name, count, at in (("ctx", n, me), ("dp", sides, side), ("expert", experts, expert)):
        for k in range(1, count):
            pl.semaphore_signal(
                barrier, inc=1, device_id={name: lax.rem(at + k, count)}, device_id_type=pl.DeviceIdType.MESH
            )
    owns = [
        pltpu.make_async_copy(cot_hbm, cots_hbm.at[expert], own_sems.at[0]),
        pltpu.make_async_copy(win_hbm, win_all.at[me * sides + side], own_sems.at[1]),
        pltpu.make_async_copy(wout_hbm, wout_all.at[me * sides + side], own_sems.at[2]),
    ]
    for copy in owns:
        copy.start()
    pl.semaphore_wait(barrier, n + sides + experts - 3)
    shard = (win_hbm, wout_hbm)
    whole = (win_all, wout_all)

    def along(way, s, v):
        j = me - s if way == 0 else me + s
        to = me + 1 if way == 0 else me - 1
        at = j * sides + side
        source = shard[v] if s == 0 else whole[v].at[at]
        return remote(source, whole[v].at[at], line_sems.at[0, way, v, s], line_sems.at[1, way, v, s], {"ctx": to})

    def across(way, s, v):
        j = me - s if way == 0 else me + s
        at = j * sides + side
        source = shard[v] if s == 0 else whole[v].at[at]
        return [
            remote(
                source, whole[v].at[at], side_sems.at[0, way, v, k - 1, s], side_sems.at[1, way, v, k - 1, s],
                {"dp": lax.rem(side + k, sides)},
            )
            for k in range(1, sides)
        ]

    def holds(way, s):
        return me - s >= 0 if way == 0 else me + s < n

    def passes(way, s, v):
        if v == 1 and s == n - 2:
            return None
        return (me - s >= 0) & (me < n - 1) if way == 0 else (me + s < n) & (me > 0)

    def advance(s, v):
        for way in range(2):
            if s > 0:
                @pl.when(holds(way, s))
                def _():
                    along(way, s - 1, v).wait_recv()

            if passes(way, s, v) is not None:
                @pl.when(passes(way, s, v))
                def _():
                    along(way, s, v).start()

            if s > 0:
                @pl.when(holds(way, s))
                def _():
                    for copy in across(way, s, v):
                        copy.start()

    for v in range(2):
        for copy in across(0, 0, v):
            copy.start()
        advance(0, v)
    sent = gather_start(cot_hbm, cots_hbm, near_sems, far_sems)

    x = x_ref[...].astype(f32)
    normed = x * lax.rsqrt(jnp.mean(x * x, axis=1, keepdims=True) + EPSILON) * gain_ref[...].reshape(1, width)
    normed = normed.astype(bf16)
    held_copies = []
    here = pl.ds(pl.multiple_of(me * group, 16), group)
    seg = jnp.broadcast_to(segment_ref[...].astype(f32), (16, rows)).astype(bf16)
    made[3, 0:16, :] = seg
    held[me, 3 * group : 3 * group + 16, :] = seg
    for kind, weight in enumerate((wq, wk, wv)):
        made[kind] = dot(normed, weight[...]).astype(bf16).T
        for k in range(1, n):
            to = lax.rem(me + k, n)
            copy = remote(
                made.at[kind, pl.ds(pl.multiple_of(to * group, 16), group)],
                held.at[me, kind * group : (kind + 1) * group],
                held_sems.at[0, kind, k - 1], held_sems.at[1, kind, k - 1], {"ctx": to},
            )
            copy.start()
            held_copies.append(copy)
        held[me, kind * group : (kind + 1) * group, :] = made[kind, here, :]
    for k in range(1, n):
        copy = remote(
            made.at[3, 0:16], held.at[me, 3 * group : 3 * group + 16], held_sems.at[0, 3, k - 1], held_sems.at[1, 3, k - 1],
            {"ctx": lax.rem(me + k, n)},
        )
        copy.start()
        held_copies.append(copy)
    normed_t[...] = normed.T

    order_row = order_ref[...].astype(f32)
    before = jnp.where(column_of(order_row)[:, 0:1] < order_row, 1.0, 0.0).astype(bf16)
    kinds = 16
    which = lax.broadcasted_iota(jnp.int32, (kinds, rows), 0)
    chosen = [routes_ref[c : c + 1, :] for c in range(2)]
    hot = [jnp.where(which == c, 1.0, 0.0) for c in chosen]
    ahead = [dot(h.astype(bf16), before) for h in hot]
    firsts = jnp.sum(hot[0], axis=1, keepdims=True)
    slots = [jnp.sum(hot[0] * ahead[0], axis=0, keepdims=True), jnp.sum(hot[1] * (ahead[1] + firsts), axis=0, keepdims=True)]
    infos[expert] = jnp.concatenate(chosen + [s.astype(jnp.int32) for s in slots] + [jnp.zeros((4, rows), jnp.int32)], axis=0)
    info_copies = [
        remote(infos.at[expert], infos.at[expert], info_sems.at[0, k - 1], info_sems.at[1, k - 1], {"expert": lax.rem(expert + k, experts)})
        for k in range(1, experts)
    ]
    for copy in info_copies:
        copy.start()
    lines[...] = bias_line(BLK - lax.broadcasted_iota(jnp.int32, (1, 2 * BLK), 1), table_ref[...])

    advance(1, 0)
    advance(1, 1)
    advance(2, 0)
    for copy in held_copies:
        copy.wait_recv()

    def mixed_copy(h, k):
        to = lax.rem(me + k, n)
        base = pl.multiple_of(h * size, size)
        return remote(
            given.at[to, pl.ds(base, size)], mixed.at[pl.ds(pl.multiple_of(me * group + base, 16), size)],
            mixed_sems.at[0, h, k - 1], mixed_sems.at[1, h, k - 1], {"ctx": to},
        )

    def head(h, carry):
        base = pl.multiple_of(h * size, size)
        for s in range(n):
            at = slice(s * rows, (s + 1) * rows)
            q = held[s, pl.ds(base, size), :]
            k = held[s, pl.ds(base + group, size), :]
            v = held[s, pl.ds(base + 2 * group, size), :]
            mask, hot = seg_mask_rows(held[s, 3 * group : 3 * group + 16, :])
            zeros = jnp.zeros((48, rows), bf16)
            qa[at, :] = jnp.concatenate([q * jnp.asarray(0.125, bf16), mask, zeros], axis=0).T
            ka[:, at] = jnp.concatenate([k, hot, zeros], axis=0)
            vn[at, :] = jnp.concatenate([v, jnp.zeros((64, rows), bf16)], axis=0).T
        line = jnp.broadcast_to(lines[pl.ds(me * heads + h, 1), :], (BLK, 2 * BLK))
        rolled = pltpu.roll(line, 0, 1, stride=1, stride_axis=0)
        r = lax.broadcasted_iota(jnp.int32, (BLK, 2 * BLK), 0)
        c = lax.broadcasted_iota(jnp.int32, (BLK, 2 * BLK), 1)
        bias[...] = jnp.where(c - r > BLK, NEG, rolled)
        for t in range(length // BLK):
            qt = qa[t * BLK : (t + 1) * BLK, :]
            near0 = max(t - 1, 0) * BLK
            end = (t + 1) * BLK
            chunks = [(near0, end)] + [(a, min(a + 2 * BLK, near0)) for a in range(0, near0, 2 * BLK)]
            top = None
            for a, b in chunks:
                s = dot(qt, ka[:, a:b])
                if a == near0:
                    s = s + bias[:, 2 * BLK - (b - a) :]
                s_ref[:, a:b] = s
                part = s[:, :128]
                for i in range(1, (b - a) // 128):
                    part = jnp.maximum(part, s[:, i * 128 : (i + 1) * 128])
                top = part if top is None else jnp.maximum(top, part)
            m = jnp.max(top, axis=1, keepdims=True)
            total = None
            o = None
            for a, b in chunks:
                p = jnp.exp(s_ref[:, a:b] - m)
                part = p[:, :128]
                for i in range(1, (b - a) // 128):
                    part = part + p[:, i * 128 : (i + 1) * 128]
                total = part if total is None else total + part
                u = dot(p.astype(bf16), vn[a:b, :])
                o = u if o is None else o + u
            l = jnp.sum(total, axis=1, keepdims=True)
            o = o / l
            lane = lax.broadcasted_iota(jnp.int32, (BLK, 128), 1)
            o = jnp.where(lane == 64, m + jnp.log(l), o)
            ot = o.T
            src, off = (t * BLK) // rows, (t * BLK) % rows
            given[src, pl.ds(base, size), off : off + BLK] = ot[:size].astype(bf16)
            of_ref[pl.ds(base, size), t * BLK : (t + 1) * BLK] = ot[:size]
            lse_ref[pl.ds(h, 1), t * BLK : (t + 1) * BLK] = ot[size : size + 1]
        for k in range(1, n):
            mixed_copy(h, k).start()
        mixed[pl.ds(pl.multiple_of(me * group + base, 16), size), :] = given[me, pl.ds(base, size), :]

        @pl.when(h == 0)
        def _():
            advance(2, 1)

        @pl.when(h == 1)
        def _():
            for s in range(3, n):
                advance(s, 0)

        return carry

    lax.fori_loop(0, heads, head, 0)
    relays = []
    for k in range(1, experts // 2):
        sent[k].wait_recv()
        passed = relay(k, cots_hbm, relay_sems)
        passed.start()
        relays.append(passed)
    sent[0].wait_recv()
    for h in range(heads):
        for k in range(1, n):
            mixed_copy(h, k).wait()
    for copy in held_copies + sent:
        copy.wait_send()
    for copy in relays + info_copies + owns:
        copy.wait()
    for v in range(2):
        for s in range(n):
            for way in range(2):
                if v == 1 and s == n - 1:
                    continue
                if passes(way, s, v) is not None:
                    @pl.when(passes(way, s, v))
                    def _():
                        along(way, s, v).wait_send()

                if s > 0 or way == 0:
                    @pl.when(holds(way, s))
                    def _():
                        for copy in across(way, s, v):
                            copy.wait()


def front_pass(x, gain, wq, wk, wv, table, segments, routes, order, cot, win, wout):
    rows, width = x.shape
    n = lax.axis_size("ctx")
    sides = lax.axis_size("dp")
    experts = lax.axis_size("expert")
    heads = table.shape[0] // n
    group = heads * 64
    length = n * rows
    blocks = n * sides
    vmem = pl.BlockSpec(memory_space=pltpu.VMEM)
    hbm = pl.BlockSpec(memory_space=pl.ANY)
    dma = pltpu.SemaphoreType.DMA
    far = max(experts // 2 - 1, 1)
    some = max(sides - 1, 1)
    return pl.pallas_call(
        partial(front_kernel, heads, n, rows),
        out_shape=[
            jax.ShapeDtypeStruct((n, 3 * group + 16, rows), bf16),
            jax.ShapeDtypeStruct((width, rows), bf16),
            jax.ShapeDtypeStruct((group, length), f32),
            jax.ShapeDtypeStruct((heads, length), f32),
            jax.ShapeDtypeStruct((width, rows), bf16),
            jax.ShapeDtypeStruct((experts, 8, rows), jnp.int32),
            jax.ShapeDtypeStruct((experts, rows, width), bf16),
            jax.ShapeDtypeStruct((blocks,) + win.shape, bf16),
            jax.ShapeDtypeStruct((blocks,) + wout.shape, bf16),
        ],
        in_specs=[vmem] * 9 + [hbm] * 3,
        out_specs=[vmem] * 6 + [hbm] * 3,
        scratch_shapes=[
            pltpu.VMEM((4, width, rows), bf16),
            pltpu.VMEM((n, group, rows), bf16),
            pltpu.VMEM((length, 128), bf16),
            pltpu.VMEM((128, length), bf16),
            pltpu.VMEM((length, 128), bf16),
            pltpu.VMEM((BLK, 2 * BLK), f32),
            pltpu.VMEM((BLK, length), f32),
            pltpu.VMEM((table.shape[0], 2 * BLK), f32),
            dma((2, 4, n - 1)),
            dma((2, heads, n - 1)),
            dma((2,)),
            dma((2, far)),
            dma((2, far)),
            dma((2, experts - 1)),
            dma((3,)),
            dma((2, 2, 2, n)),
            dma((2, 2, 2, some, n)),
        ],
        compiler_params=pltpu.CompilerParams(
            collective_id=2, has_side_effects=True, vmem_limit_bytes=60 * 1024 * 1024
        ),
        name="front_pass",
    )(x, gain, wq, wk, wv, table, segments, routes, order, cot, win, wout)


def line_order(n):
    order = []
    for i in range((n + 1) // 2):
        order.append(n - 1 - i)
        if i != n - 1 - i:
            order.append(i)
    return order


def line_scatter(n, own, right, left, right_sems, left_sems, ready):
    me = lax.axis_index("ctx")
    items = {}
    for j in line_order(n):
        for r in range(j):
            items.setdefault(ready[j] + r, []).append((0, r, j))
        for r in range(n - 1, j, -1):
            items.setdefault(ready[j] + n - 1 - r, []).append((1, r, j))
    steps = max(items) + 1

    def pass_on(way, r, j):
        taken, sems = (right, right_sems) if way == 0 else (left, left_sems)
        first = 0 if way == 0 else n - 1
        return remote(
            own.at[j] if r == first else taken.at[j], taken.at[j], sems.at[0, j], sems.at[1, j],
            {"ctx": r + 1 if way == 0 else r - 1},
        )

    def advance(step):
        for way, r, j in items.get(step, []):
            @pl.when(me == r)
            def _():
                copy = pass_on(way, r, j)
                if r != (0 if way == 0 else n - 1):
                    taken = right if way == 0 else left
                    copy.wait_recv()
                    taken[j] = (taken[j].astype(f32) + own[j].astype(f32)).astype(bf16)
                copy.start()

    def finish(out):
        for j in range(n):
            @pl.when(me == j)
            def _():
                total = own[j].astype(f32)
                if j > 0:
                    pass_on(0, j - 1, j).wait_recv()
                    total = total + right[j].astype(f32)
                if j < n - 1:
                    pass_on(1, j + 1, j).wait_recv()
                    total = total + left[j].astype(f32)
                out[...] = total.astype(bf16)

    def drain():
        for step in range(steps):
            for way, r, j in items.get(step, []):
                @pl.when(me == r)
                def _():
                    pass_on(way, r, j).wait_send()

    return advance, finish, drain, steps


def back_kernel(
    heads, n, rows, x_ref, do_ref, table_ref, of_ref, lse_ref, base_ref, far_ref, gin_hbm, gout_hbm,
    cots_ref, diag_ref, ein_ref, own_b, out_ref,
    do_in, g_ref, qa, ka, va, da, qn, dn, bias, dq, gsum,
    own_a, side_a, side_b, right_a, left_a,
    do_sems, out_sems, own_sems, side_sems, right_sems, left_sems, lines, far_in, far_sems,
):
    size = 64
    group = heads * size
    length = n * rows
    sides = lax.axis_size("dp")
    me = lax.axis_index("ctx")
    side = lax.axis_index("dp")
    barrier, peers = greet(("ctx", "dp", "expert"))
    order = line_order(n)
    advance, finish, drain, steps = line_scatter(
        n, own_a, right_a, left_a, right_sems, left_sems, {j: i for i, j in enumerate(order)}
    )
    loads = {}
    for j in order:
        at = j * sides + side
        loads[j] = [
            pltpu.make_async_copy(gin_hbm.at[at], own_a.at[j], own_sems.at[0, j]),
            pltpu.make_async_copy(gout_hbm.at[at], own_b.at[j], own_sems.at[1, j]),
        ]
        for copy in loads[j]:
            copy.start()
    pl.semaphore_wait(barrier, peers)
    lanes, lane, core = expert_split()
    homes = [
        remote(
            far_ref.at[k - 1], far_in.at[k - 1], far_sems.at[0, k - 1], far_sems.at[1, k - 1],
            {"expert": lax.rem(lane - k + lanes, lanes) * 2 + core},
        )
        for k in range(1, lanes)
    ]
    for copy in homes:
        copy.start()
    lines[...] = bias_line(lax.broadcasted_iota(jnp.int32, (1, 2 * BLK), 1), table_ref[...])
    arriving = []
    for k in range(1, n):
        to = lax.rem(me + k, n)
        copy = remote(
            do_ref.at[pl.ds(pl.multiple_of(to * group, 16), group)], do_in.at[me], do_sems.at[0, k - 1], do_sems.at[1, k - 1], {"ctx": to}
        )
        copy.start()
        arriving.append(copy)
    beside = {}
    for v, gone, taken in ((0, gin_hbm, side_a), (1, gout_hbm, side_b)):
        for j in order:
            beside[v, j] = []
            for k in range(1, sides):
                to = lax.rem(side + k, sides)
                beside[v, j].append(
                    remote(
                        gone.at[j * sides + to], taken.at[k - 1, j],
                        side_sems.at[0, v, k - 1, j], side_sems.at[1, v, k - 1, j], {"dp": to},
                    )
                )
                beside[v, j][-1].start()

    def sum_sides(v, j):
        own, taken = ((own_a, side_a), (own_b, side_b))[v]
        loads[j][v].wait()
        total = own[j].astype(f32)
        for k in range(1, sides):
            beside[v, j][k - 1].wait_recv()
            total = total + taken[k - 1, j].astype(f32)
        own[j] = total.astype(bf16)

    do_in[me] = do_ref[pl.ds(pl.multiple_of(me * group, 16), group), :]

    sum_sides(0, order[0])
    advance(0)
    for copy in arriving:
        copy.wait_recv()

    def out_copy(h, kind, k):
        to = lax.rem(me + k, n)
        base = pl.multiple_of(h * size, size)
        return remote(
            g_ref.at[to, pl.ds(kind * group + base, size)],
            cots_ref.at[pl.ds(pl.multiple_of(kind * n * group + me * group + base, 16), size)],
            out_sems.at[0, h, kind, k - 1],
            out_sems.at[1, h, kind, k - 1],
            {"ctx": to},
        )

    def head(h, carry):
        base = pl.multiple_of(h * size, size)
        for s in range(n):
            at = slice(s * rows, (s + 1) * rows)
            q = x_ref[s, pl.ds(base, size), :] * jnp.asarray(0.125, bf16)
            k = x_ref[s, pl.ds(base + group, size), :]
            v = x_ref[s, pl.ds(base + 2 * group, size), :]
            d = do_in[s, pl.ds(base, size), :]
            seg = x_ref[s, 3 * group : 3 * group + 16, :]
            mask, hot = seg_mask_rows(seg)
            which = lax.broadcasted_iota(jnp.int32, (16, rows), 0)

            def rows3(vec):
                hi, mid, lo = split3(jnp.broadcast_to(vec, (16, rows)))
                return jnp.where(which == 0, hi, jnp.where(which == 1, mid, jnp.where(which == 2, lo, jnp.zeros((), bf16))))

            ones = jnp.where(which < 3, 1.0, 0.0).astype(bf16)
            zeros = jnp.zeros((32, rows), bf16)
            zeros48 = jnp.zeros((48, rows), bf16)
            lse = lse_ref[pl.ds(h, 1), at]
            delta = jnp.sum(of_ref[pl.ds(base, size), at] * d.astype(f32), axis=0, keepdims=True)
            qt = jnp.concatenate([q, mask, rows3(-lse), zeros], axis=0)
            qa[:, at] = qt
            qn[at, :] = qt.T
            ka[at, :] = jnp.concatenate([k, hot, ones, zeros], axis=0).T
            dt = jnp.concatenate([d, rows3(-delta), zeros48], axis=0)
            da[:, at] = dt
            dn[at, :] = dt.T
            va[at, :] = jnp.concatenate([v, ones, zeros48], axis=0).T
        line = jnp.broadcast_to(lines[pl.ds(me * heads + h, 1), :], (BLK, 2 * BLK))
        rolled = pltpu.roll(line, 0, 1, stride=1, stride_axis=0)
        r = lax.broadcasted_iota(jnp.int32, (BLK, 2 * BLK), 0)
        c = lax.broadcasted_iota(jnp.int32, (BLK, 2 * BLK), 1)
        bias[...] = jnp.where(c < r, NEG, rolled)
        gsum[...] = jnp.zeros_like(gsum)
        for j in range(length // BLK):
            a0 = j * BLK
            kj = ka[a0 : a0 + BLK, :]
            vj = va[a0 : a0 + BLK, :]
            src, off = a0 // rows, a0 % rows
            kt = x_ref[src, pl.ds(base + group, size), off : off + BLK]
            dk = dv = None
            for a in range(a0, length, 2 * BLK):
                b = min(a + 2 * BLK, length)
                s = dot(kj, qa[:, a:b])
                if a == a0:
                    s = s + bias[:, : b - a]
                p = jnp.exp(s)
                ds = p * dot(vj, da[:, a:b])
                if a == a0:
                    gsum[:, : b - a] += ds
                p_low, ds_low = p.astype(bf16), ds.astype(bf16)
                u = dot(p_low, dn[a:b, :])
                dv = u if dv is None else dv + u
                u = dot(ds_low, qn[a:b, :])
                dk = u if dk is None else dk + u
                u = dot(kt, ds_low)
                if j == 0:
                    dq[:, a:b] = u
                else:
                    dq[:, a:b] += u
            g_ref[src, pl.ds(base + group, size), off : off + BLK] = dk.T[:size].astype(bf16)
            g_ref[src, pl.ds(base + 2 * group, size), off : off + BLK] = dv.T[:size].astype(bf16)
        for s in range(n):
            g_ref[s, pl.ds(base, size), :] = (dq[:, s * rows : (s + 1) * rows] * 0.125).astype(bf16)
        for kind in range(3):
            for k in range(1, n):
                out_copy(h, kind, k).start()
            cots_ref[pl.ds(pl.multiple_of(kind * n * group + me * group + base, 16), size), :] = g_ref[
                me, pl.ds(kind * group + base, size), :
            ]
        eight = gsum[0:8, :]
        for i in range(1, BLK // 8):
            eight = eight + pltpu.roll(gsum[8 * i : 8 * i + 8, :], 2 * BLK - 8 * i, 1)
        line = eight[0:1]
        for i in range(1, 8):
            line = line + pltpu.roll(eight, 2 * BLK - i, 1)[i : i + 1]
        diag_ref[pl.ds(h, 1), :] = line
        for step in range(1, heads):
            @pl.when(h == step - 1)
            def _():
                if step < n:
                    sum_sides(0, order[step])
                advance(step)

        return carry

    lax.fori_loop(0, heads, head, 0)
    for step in range(heads, steps):
        if step < n:
            sum_sides(0, order[step])
        advance(step)
        if step >= n and step - n < n:
            sum_sides(1, order[step - n])
    for i in range(max(steps - n, 0), n):
        sum_sides(1, order[i])
    mixture = base_ref[...]
    for k in range(1, lanes):
        homes[k - 1].wait()
        mixture = mixture + far_in[k - 1].astype(f32)
    out_ref[...] = mixture.astype(bf16)
    finish(ein_ref)
    for h in range(heads):
        for kind in range(3):
            for k in range(1, n):
                out_copy(h, kind, k).wait()
    for copy in arriving:
        copy.wait_send()
    for copies in beside.values():
        for copy in copies:
            copy.wait_send()
    drain()


def back_pass(x, do, table, of, lse, base, far, gin, gout):
    n, depth, rows = x.shape
    heads = table.shape[0] // n
    group = heads * 64
    length = n * rows
    sides = lax.axis_size("dp")
    _, high_a, wide_a = gin.shape
    _, high_b, wide_b = gout.shape
    vmem = pl.BlockSpec(memory_space=pltpu.VMEM)
    hbm = pl.BlockSpec(memory_space=pl.ANY)
    dma = pltpu.SemaphoreType.DMA
    some = max(sides - 1, 1)
    return pl.pallas_call(
        partial(back_kernel, heads, n, rows),
        out_shape=[
            jax.ShapeDtypeStruct((3 * n * group, rows), bf16),
            jax.ShapeDtypeStruct((heads, 2 * BLK), f32),
            jax.ShapeDtypeStruct((high_a, wide_a), bf16),
            jax.ShapeDtypeStruct((n, high_b, wide_b), bf16),
            jax.ShapeDtypeStruct(base.shape, bf16),
        ],
        in_specs=[vmem] * 7 + [hbm] * 2,
        out_specs=[vmem] * 5,
        scratch_shapes=[
            pltpu.VMEM((n, group, rows), bf16),
            pltpu.VMEM((n, 3 * group, rows), bf16),
            pltpu.VMEM((128, length), bf16),
            pltpu.VMEM((length, 128), bf16),
            pltpu.VMEM((length, 128), bf16),
            pltpu.VMEM((128, length), bf16),
            pltpu.VMEM((length, 128), bf16),
            pltpu.VMEM((length, 128), bf16),
            pltpu.VMEM((BLK, 2 * BLK), f32),
            pltpu.VMEM((64, length), f32),
            pltpu.VMEM((BLK, 2 * BLK), f32),
            pltpu.VMEM((n, high_a, wide_a), bf16),
            pltpu.VMEM((some, n, high_a, wide_a), bf16),
            pltpu.VMEM((some, n, high_b, wide_b), bf16),
            pltpu.VMEM((n, high_a, wide_a), bf16),
            pltpu.VMEM((n, high_a, wide_a), bf16),
            dma((2, n - 1)),
            dma((2, heads, 3, n - 1)),
            dma((2, n)),
            dma((2, 2, some, n)),
            dma((2, n)),
            dma((2, n)),
            pltpu.VMEM((table.shape[0], 2 * BLK), f32),
            pltpu.VMEM(far.shape, bf16),
            dma((2, far.shape[0])),
        ],
        compiler_params=pltpu.CompilerParams(
            collective_id=3, has_side_effects=True, vmem_limit_bytes=60 * 1024 * 1024
        ),
        name="back_pass",
    )(x, do, table, of, lse, base, far, gin, gout)


def add_all(parts):
    return functools.reduce(lambda a, b: a + b, parts)


def axis_stages():
    experts = lax.axis_size("expert")
    me = lax.axis_index("expert")
    core, lane = lax.rem(me, 2), lax.div(me, 2)
    return {
        "core": (2, core, lambda j: {"expert": lane * 2 + j}),
        "lane": (experts // 2, lane, lambda j: {"expert": j * 2 + core}),
        "dp": (lax.axis_size("dp"), lax.axis_index("dp"), lambda j: {"dp": j}),
        "ctx": (lax.axis_size("ctx"), lax.axis_index("ctx"), lambda j: {"ctx": j}),
    }


ORDERS = (("core", "lane", "dp", "ctx"), ("core", "dp", "lane", "ctx"))
SLICES = 2


def sum_plan(sizes, rows):
    plans = []
    for order in ORDERS:
        length, plan = rows // 2, []
        for name in order:
            count = sizes[name]
            split = length % count == 0 and (length // count) % 16 == 0
            plan.append((name, count, length, split))
            if split:
                length = length // count
        plans.append(plan)
    return plans


def received_rows(plans):
    return [
        [(count - 1) * (length // count if split else length) for (_, count, length, split) in plan]
        for plan in plans
    ]


def sizes_of():
    return {
        "core": 2,
        "lane": lax.axis_size("expert") // 2,
        "dp": lax.axis_size("dp"),
        "ctx": lax.axis_size("ctx"),
    }


def tail_kernel(
    plans, normed_t, cots, mixed_t, wq, wk, wv, x_ref, gain_ref, hidden_cot_ref, moe_small_ref, diag_ref, sums_ref,
    grads_ref, input_grad_ref, small_out_ref, eout_ref,
    acc, whole, taken_a, taken_b, small, small_taken, send, recv, back_send, back_recv, small_send, small_recv,
    right, left, right_sems, left_sems,
):
    stages = axis_stages()
    width = wq.shape[0]
    rows = x_ref.shape[0]
    barrier = pltpu.get_barrier_semaphore()
    peers = 0
    for name, (count, me, at) in stages.items():
        for k in range(1, count):
            pl.semaphore_signal(barrier, inc=1, device_id=at(lax.rem(me + k, count)), device_id_type=pl.DeviceIdType.MESH)
            peers += 1

    def make(k):
        if k < 3:
            acc[k * width : (k + 1) * width, :] = dot(
                normed_t[...], cots[k * width : (k + 1) * width, :], NT
            ).astype(bf16)
        else:
            acc[3 * width :, :] = dot(mixed_t[...], hidden_cot_ref[...].astype(bf16)).astype(bf16)

    taken = (taken_a, taken_b)
    half = 2 * width
    piece = width // SLICES
    parts = [(h, c) for c in range(SLICES) for h in range(2)]
    spans = {}
    for part in parts:
        spans[part] = [part[0] * half]

    def columns(part):
        return pl.ds(part[1] * piece, piece)

    def rows_at(start, size):
        return pl.ds(pl.multiple_of(start, 16), size)

    flying = {}

    def send_stage(part, step):
        h, c = part
        name, count, length, split = plans[h][step]
        _, me, at = stages[name]
        start = spans[part][-1]
        size = length // count if split else length
        base = sum(received[h][:step])
        copies = []
        for k in range(1, count):
            peer = lax.rem(me + k, count)
            copies.append(
                pltpu.make_async_remote_copy(
                    src_ref=acc.at[rows_at(start + peer * size if split else start, size), columns(part)],
                    dst_ref=taken[h].at[pl.ds(base + (k - 1) * size, size), columns(part)],
                    send_sem=send.at[h * SLICES + c, step, k - 1],
                    recv_sem=recv.at[h * SLICES + c, step, k - 1],
                    device_id=at(peer),
                    device_id_type=pl.DeviceIdType.MESH,
                )
            )
        for copy in copies:
            copy.start()
        flying[part] = copies

    def add_stage(part, step):
        h, c = part
        name, count, length, split = plans[h][step]
        _, me, at = stages[name]
        size = length // count if split else length
        start = spans[part][-1] + me * size if split else spans[part][-1]
        base = sum(received[h][:step])
        for copy in flying[part]:
            copy.wait()
        total = acc[rows_at(start, size), columns(part)].astype(f32)
        for k in range(1, count):
            total = total + taken[h][base + (k - 1) * size : base + k * size, columns(part)].astype(f32)
        if step == len(plans[h]) - 1:
            whole[rows_at(start, size), columns(part)] = total.astype(bf16)
        else:
            acc[rows_at(start, size), columns(part)] = total.astype(bf16)
        spans[part].append(start)

    def give_stage(part, step):
        h, c = part
        name, count, length, split = plans[h][step]
        if not split:
            flying[part] = []
            return
        _, me, at = stages[name]
        size = length // count
        start = spans[part][step + 1]
        copies = []
        for k in range(1, count):
            peer = lax.rem(me + k, count)
            copies.append(
                pltpu.make_async_remote_copy(
                    src_ref=whole.at[rows_at(start, size), columns(part)],
                    dst_ref=whole.at[rows_at(start, size), columns(part)],
                    send_sem=back_send.at[h * SLICES + c, step, k - 1],
                    recv_sem=back_recv.at[h * SLICES + c, step, k - 1],
                    device_id=at(peer),
                    device_id_type=pl.DeviceIdType.MESH,
                )
            )
        for copy in copies:
            copy.start()
        flying[part] = copies

    n = sums_ref.shape[0]
    advance, finish, drain, line_steps = line_scatter(n, sums_ref, right, left, right_sems, left_sems, [0] * n)
    received = received_rows(plans)
    make(2)
    make(3)
    pl.semaphore_wait(barrier, peers)
    for c in range(SLICES):
        send_stage((1, c), 0)
    advance(0)
    make(0)
    make(1)
    for c in range(SLICES):
        send_stage((0, c), 0)
    parts = [(1, 0), (0, 0), (1, 1), (0, 1)]

    def make_small():
        turned = dot(wq[...], cots[:width, :]) + dot(wk[...], cots[width : 2 * width, :]) + dot(wv[...], cots[2 * width :, :])
        cot = turned.T
        x = x_ref[...].astype(f32)
        gain = gain_ref[...].reshape(1, width)
        scale = lax.rsqrt(jnp.mean(x * x, axis=1, keepdims=True) + EPSILON)
        unit = x * scale
        gained = cot * gain
        input_grad_ref[...] = hidden_cot_ref[...] + scale * (gained - unit * jnp.mean(unit * gained, axis=1, keepdims=True))
        gain_grad = jnp.sum(unit * cot, axis=0, keepdims=True)
        which = lax.broadcasted_iota(jnp.int32, (8, width), 0)
        low = jnp.where(which == 0, gain_grad, jnp.where(which == 1, moe_small_ref[0:8, :], 0.0))
        near_rows, near_lanes = 128, 256
        distance = lax.broadcasted_iota(jnp.int32, (near_rows, near_lanes), 0)
        lane = lax.broadcasted_iota(jnp.int32, (near_rows, near_lanes), 1)
        far = jnp.full(distance.shape, BUCKETS // 2, jnp.int32)
        for limit in THRESHOLDS:
            far = far + jnp.where(distance >= limit, 1, 0)
        bucket = jnp.where(distance < BUCKETS // 2, distance, far)
        own = distance < THRESHOLDS[-1]
        lane_row = lax.broadcasted_iota(jnp.int32, (1, near_lanes), 1)
        which = lax.broadcasted_iota(jnp.int32, (8, near_lanes), 0)
        sums = jnp.zeros((8, near_lanes), f32)
        heads = diag_ref.shape[0]
        for h in range(heads):
            at = lax.axis_index("ctx") * heads + h
            start = lax.div(at, 6) * 128
            hot = jnp.where(own & (bucket + start == lane), 1.0, 0.0).astype(bf16)
            three = split3(jnp.broadcast_to(diag_ref[h : h + 1, :near_rows], (16, near_rows)))
            near = (dot(three[0], hot) + dot(three[1], hot) + dot(three[2], hot))[0:1]
            near = jnp.where(lane_row == start + BUCKETS - 1, -jnp.sum(near, axis=1, keepdims=True), near)
            sums = sums + jnp.where(which == 2 + lax.rem(at, 6), near, 0.0)
        low = low + jnp.concatenate([sums, jnp.zeros((8, width - near_lanes), f32)], axis=1)
        small[0:8, :] = low
        small[8:16, :] = moe_small_ref[8:16, :]

    def send_small(step):
        name = ORDERS[0][step]
        count, me, at = stages[name]
        base = sum(stages[n][0] - 1 for n in ORDERS[0][:step])
        copies = [
            pltpu.make_async_remote_copy(
                src_ref=small,
                dst_ref=small_taken.at[base + k - 1],
                send_sem=small_send.at[base + k - 1],
                recv_sem=small_recv.at[base + k - 1],
                device_id=at(lax.rem(me + k, count)),
                device_id_type=pl.DeviceIdType.MESH,
            )
            for k in range(1, count)
        ]
        for copy in copies:
            copy.start()
        flying["small"] = copies

    def add_small(step):
        base = sum(stages[n][0] - 1 for n in ORDERS[0][:step])
        for copy in flying["small"]:
            copy.wait()
        total = small[...]
        for k in range(len(flying["small"])):
            total = total + small_taken[base + k]
        small[...] = total

    last = len(ORDERS[0])
    for step in range(last):
        for part in parts:
            add_stage(part, step)
            if step + 1 < last:
                send_stage(part, step + 1)
            else:
                give_stage(part, step)
        if step == 0:
            make_small()
        else:
            add_small(step - 1)
        send_small(step)
        if step == 1:
            advance(1)
    for step in range(2, line_steps):
        advance(step)
    for step in range(last - 1, -1, -1):
        for part in parts:
            for copy in flying[part]:
                copy.wait()
            if step > 0:
                give_stage(part, step - 1)
        if step == last - 1:
            add_small(last - 1)
            small_out_ref[...] = small[...]
    finish(eout_ref)
    drain()
    grads_ref[...] = whole[...]


def tail_pass(normed_t, cots, mixed_t, wq, wk, wv, x, gain, hidden_cot, moe_small, diag, sums):
    rows, width = x.shape
    sizes = sizes_of()
    plans = sum_plan(sizes, 4 * width)
    received = [sum(r) for r in received_rows(plans)]
    most = max(sizes.values()) - 1
    few = sum(n - 1 for n in sizes.values())
    small = jax.ShapeDtypeStruct((16, width), f32)
    return pl.pallas_call(
        partial(tail_kernel, plans),
        out_shape=[
            jax.ShapeDtypeStruct((4 * width, width), bf16),
            jax.ShapeDtypeStruct((rows, width), f32),
            jax.ShapeDtypeStruct(small.shape, f32),
            jax.ShapeDtypeStruct(sums.shape[1:], bf16),
        ],
        in_specs=[pl.BlockSpec(memory_space=pltpu.VMEM)] * 12,
        out_specs=[pl.BlockSpec(memory_space=pltpu.VMEM)] * 4,
        scratch_shapes=[
            pltpu.VMEM((4 * width, width), bf16),
            pltpu.VMEM((4 * width, width), bf16),
            pltpu.VMEM((received[0], width), bf16),
            pltpu.VMEM((received[1], width), bf16),
            pltpu.VMEM(small.shape, f32),
            pltpu.VMEM((few,) + small.shape, f32),
            pltpu.SemaphoreType.DMA((2 * SLICES, 4, most)),
            pltpu.SemaphoreType.DMA((2 * SLICES, 4, most)),
            pltpu.SemaphoreType.DMA((2 * SLICES, 4, most)),
            pltpu.SemaphoreType.DMA((2 * SLICES, 4, most)),
            pltpu.SemaphoreType.DMA((few,)),
            pltpu.SemaphoreType.DMA((few,)),
            pltpu.VMEM(sums.shape, bf16),
            pltpu.VMEM(sums.shape, bf16),
            pltpu.SemaphoreType.DMA((2, sums.shape[0])),
            pltpu.SemaphoreType.DMA((2, sums.shape[0])),
        ],
        compiler_params=pltpu.CompilerParams(
            collective_id=0, has_side_effects=True, vmem_limit_bytes=56 * 1024 * 1024
        ),
        name="tail_pass",
    )(normed_t, cots, mixed_t, wq, wk, wv, x, gain, hidden_cot, moe_small, diag, sums)


def finish_kernel(heads, width, large_ref, small_ref, *refs):
    extra = (len(refs) - 7) // 2
    ins, outs, others = refs[:extra], refs[extra : extra + 7], refs[extra + 7 :]
    for k in range(4):
        outs[k][...] = large_ref[k].astype(f32)
    for source, out in zip(ins, others):
        out[...] = source[...].astype(f32)

    @pl.when(pl.program_id(0) == 0)
    def _():
        outs[4][...] = small_ref[0:1, :].reshape(width)
        outs[5][...] = small_ref[1:2, :].reshape(width)
        for a in range(0, heads, 6):
            outs[6][a : a + 6, :] = small_ref[2:8, a // 6 * 128 : a // 6 * 128 + BUCKETS]


def finish_pass(large, small, heads, extra):
    _, width, _ = large.shape
    steps = 6
    tall = width // steps
    whole = pl.BlockSpec(small.shape, lambda i: (0, 0))

    def cut(array):
        return pl.BlockSpec((array.shape[0] // steps, array.shape[1]), lambda i: (i, 0))

    flat = pl.BlockSpec((width,), lambda i: (0,))
    return pl.pallas_call(
        partial(finish_kernel, heads, width),
        grid=(steps,),
        out_shape=[jax.ShapeDtypeStruct((width, width), f32)] * 4
        + [jax.ShapeDtypeStruct((width,), f32)] * 2
        + [jax.ShapeDtypeStruct((heads, BUCKETS), f32)]
        + [jax.ShapeDtypeStruct(array.shape, f32) for array in extra],
        in_specs=[pl.BlockSpec((4, tall, width), lambda i: (0, i, 0)), whole] + [cut(array) for array in extra],
        out_specs=[pl.BlockSpec((tall, width), lambda i: (i, 0))] * 4
        + [flat] * 2
        + [pl.BlockSpec((heads, BUCKETS), lambda i: (0, 0))]
        + [cut(array) for array in extra],
        compiler_params=pltpu.CompilerParams(vmem_limit_bytes=60 * 1024 * 1024),
        name="finish_pass",
    )(large, small, *extra)


def local(
    layer_input,
    cotangent,
    norm_gain_one,
    w_query,
    w_key,
    w_value,
    w_output,
    rel_table,
    norm_gain_two,
    w_router,
    w_expert_in,
    w_expert_out,
    segment_ids,
    routes,
    priority,
):
    rows, width = layer_input.shape[1:]
    heads = rel_table.shape[0]
    shards = lax.axis_size("ctx")
    experts = lax.axis_size("expert")
    capacity = min(rows, 5 * rows // (2 * experts))
    blocks = shards * lax.axis_size("dp")

    def padded(array):
        return jnp.pad(array, ((0, 0), (0, -array.shape[1] % 16), (0, 0)))

    held, mixed_t, attended_whole, lse, normed_t, info_all, cots_all, inner_weight, outer_weight = front_pass(
        layer_input[0], norm_gain_one, w_query, w_key, w_value, rel_table, segment_ids, routes[0].T, priority[0],
        cotangent[0], padded(w_expert_in)[0], padded(w_expert_out)[0],
    )
    inner_weight = inner_weight[:, : w_expert_in.shape[1]].reshape(width, -1)
    outer_weight = outer_weight[:, : w_expert_out.shape[1]].reshape(-1, width)
    router_t = w_router.T
    base, far, hidden_cot, mixed_cot, moe_small, inner_grad, outer_grad = moe_pass(
        capacity, mixed_t, w_output, layer_input[0], cotangent[0], norm_gain_two, router_t, info_all, cots_all, inner_weight, outer_weight
    )

    def cut(array):
        return padded(array.reshape(blocks, array.shape[0] // blocks, array.shape[1]))

    cots, diagonals, expert_in_grad, expert_out_sums, layer_output = back_pass(
        held, mixed_cot, rel_table, attended_whole, lse, base, far, cut(inner_grad), cut(outer_grad)
    )
    large, input_grad, small, expert_out_grad = tail_pass(
        normed_t, cots, mixed_t, w_query, w_key, w_value, layer_input[0], norm_gain_one, hidden_cot, moe_small, diagonals, expert_out_sums
    )
    extra = [expert_in_grad, expert_out_grad]
    fits = [array.shape[0] % 96 == 0 for array in extra]
    finished = finish_pass(
        large.reshape(4, width, width), small, heads, [array for array, fit in zip(extra, fits) if fit]
    )
    converted = list(finished[7:])
    extra = [converted.pop(0) if fit else array.astype(f32) for array, fit in zip(extra, fits)]
    return (
        layer_output[None],
        input_grad[None],
        finished[4],
        finished[0],
        finished[1],
        finished[2],
        finished[3],
        finished[6],
        finished[5],
        small[8 : 8 + experts].T,
        extra[0][None, : w_expert_in.shape[1]],
        extra[1][None, : w_expert_out.shape[1]],
    )


def solution(mesh):
    placed = (
        P(("expert", "dp"), "ctx", None),
        P(("expert", "dp"), "ctx", None),
        P(),
        P(),
        P(),
        P(),
        P(),
        P(),
        P(),
        P(),
        P("expert", ("ctx", "dp"), None),
        P("expert", ("ctx", "dp"), None),
        P(("expert", "dp"), "ctx"),
        P(("expert", "dp"), "ctx", None),
        P(("expert", "dp"), "ctx", None),
    )
    return jax.shard_map(
        local,
        mesh=mesh,
        in_specs=placed,
        out_specs=(
            P(("expert", "dp"), "ctx", None),
            P(("expert", "dp"), "ctx", None),
            P(),
            P(),
            P(),
            P(),
            P(),
            P(),
            P(),
            P(),
            P("expert", ("ctx", "dp"), None),
            P("expert", ("ctx", "dp"), None),
        ),
        check_vma=False,
    )
```

```python
import functools
from functools import partial

import jax
import jax.numpy as jnp
from jax import lax
from jax.experimental import pallas as pl
from jax.experimental.pallas import tpu as pltpu
from jax.sharding import PartitionSpec as P

bf16 = jnp.bfloat16
f32 = jnp.float32
HIGH_PRECISION = lax.Precision.HIGHEST
EPSILON = 1e-06
THRESHOLDS = (19, 21, 24, 27, 31, 35, 40, 46, 52, 59, 67, 77, 87, 99, 113)
BUCKETS=32
NEG=-1e30
BLK=256
NT=(((1,),(1,)),((),()))
TN=(((0,),(0,)),((),()))

def dot(a,b,dims=(((1,),(0,)),((),()))):
    return lax.dot_general(a,b,dims,preferred_element_type=f32)

def seg_mask_rows(seg):
    which = lax.broadcasted_iota(jnp.int32, seg.shape, 0).astype(f32)
    same = seg.astype(f32) == which
    return jnp.where(same, 0.0, NEG).astype(bf16), jnp.where(same, 1.0, 0.0).astype(bf16)

def split3(v):
    hi = v.astype(bf16); rest = v - hi.astype(f32)
    mid = rest.astype(bf16); rest = rest - mid.astype(f32)
    return hi, mid, rest.astype(bf16)

ROOT = 0.7978845608028654


def remote(src, dst, send_sem, recv_sem, where):
    return pltpu.make_async_remote_copy(
        src_ref=src,
        dst_ref=dst,
        send_sem=send_sem,
        recv_sem=recv_sem,
        device_id=where,
        device_id_type=pl.DeviceIdType.MESH,
    )


def expert_split():
    experts = lax.axis_size("expert")
    me = lax.axis_index("expert")
    return experts // 2, lax.div(me, 2), lax.rem(me, 2)


def gather_start(piece, whole, near_sems, far_sems, rows=None):
    lanes, lane, core = expert_split()
    me = lane * 2 + core
    view = whole.at[me] if rows is None else whole.at[me, rows]
    copies = [remote(piece, view, near_sems.at[0], near_sems.at[1], {"expert": lane * 2 + 1 - core})]
    for k in range(1, lanes):
        copies.append(
            remote(piece, view, far_sems.at[0, k - 1], far_sems.at[1, k - 1], {"expert": lax.rem(lane + k, lanes) * 2 + core})
        )
    for copy in copies:
        copy.start()
    return copies


def relay(k, whole, sems):
    lanes, lane, core = expert_split()
    source = lax.rem(lane - k + lanes, lanes) * 2 + core
    return remote(whole.at[source], whole.at[source], sems.at[0, k - 1], sems.at[1, k - 1], {"expert": lane * 2 + 1 - core})


def greet(names):
    barrier = pltpu.get_barrier_semaphore()
    total = 0
    for name in names:
        count, at = lax.axis_size(name), lax.axis_index(name)
        for k in range(1, count):
            pl.semaphore_signal(
                barrier, inc=1, device_id={name: lax.rem(at + k, count)}, device_id_type=pl.DeviceIdType.MESH
            )
        total += count - 1
    return barrier, total


def moe_kernel(
    capacity, mixed_t, w_output, x_ref, cot_ref, gain_ref, router_ref, info_ref, cots_hbm, inner_hbm, outer_hbm,
    base_ref, far_ref, hidden_cot_ref, mixed_cot_ref, small_ref, gin_hbm, gout_hbm,
    nt, cots, inner, outer, act_all, pre_all, rows_all, cots_all, made, back, part, pair_in, total,
    core_in, far_in, gate_out, gate_in,
    load_sems, cot_sems, near_sems, far_sems, relay_sems, pair_sems, core_sems, back_sems, gate_sems, stage_sems, free_sem, late_sems, router_rows,
):
    experts = lax.axis_size("expert")
    lanes, lane, core = expert_split()
    me = lane * 2 + core
    other = lane * 2 + 1 - core
    rows, width = cot_ref.shape
    hidden = hidden_cot_ref
    pieces = 2
    step_rows = rows // pieces
    hidden_size = inner.shape[1]
    n = lax.axis_size("ctx")
    place_z = lax.axis_index("ctx")
    wide = hidden_size // n

    first = pltpu.make_async_copy(inner_hbm, inner, load_sems.at[n])
    first.start()

    def chunk_rows(j):
        return pl.ds(pl.multiple_of(j * wide, wide), wide)

    def chunk_at(f):
        return jnp.where(place_z == n - 1, n - 1 - f, f)

    def has(f):
        return (f < n - 1) | ((place_z > 0) & (place_z < n - 1))

    def load(f):
        at = chunk_rows(chunk_at(f))
        return pltpu.make_async_copy(outer_hbm.at[at], outer.at[at], load_sems.at[f])

    for f in range(n):
        @pl.when(has(f))
        def _():
            load(f).start()

    def late(up):
        at = chunk_rows(0 if up else n - 1)
        return remote(
            outer_hbm.at[at], outer.at[at], late_sems.at[0, int(up)], late_sems.at[1, int(up)],
            {"ctx": n - 1 if up else 0},
        )

    barrier, peers = greet(("expert", "ctx"))
    pl.semaphore_wait(barrier, peers)

    @pl.when(place_z == n - 2)
    def _():
        late(True).start()

    @pl.when(place_z == 1)
    def _():
        late(False).start()

    sent = []
    for p in range(pieces):
        at = slice(p * step_rows, (p + 1) * step_rows)
        now = x_ref[at, :].astype(f32) + dot(mixed_t[:, at], w_output[...], TN)
        hidden[at, :] = now
        scale = lax.rsqrt(jnp.mean(now * now, axis=1, keepdims=True) + EPSILON)
        nt[me, at, :] = (now * scale * gain_ref[...].reshape(1, width)).astype(bf16)
        sent.append(gather_start(nt.at[me, at], nt, near_sems.at[p], far_sems.at[p], at))

    router_rows[...] = jnp.zeros_like(router_rows)
    router_rows[0:experts, :] = router_ref[...].astype(f32)
    router = router_rows[...].astype(bf16)

    def gate_rows(source):
        logits = dot(router, nt[source], NT)
        which = lax.broadcasted_iota(jnp.int32, logits.shape, 0)
        info = info_ref[source]
        chosen = (which == info[0:1]) | (which == info[1:2])
        top = jnp.max(jnp.where(chosen, logits, NEG), axis=0, keepdims=True)
        power = jnp.where(chosen, jnp.exp(jnp.minimum(logits - top, 0.0)), 0.0)
        return power / jnp.sum(power, axis=0, keepdims=True)

    def pair_of(k):
        return [lax.rem(lane - k + lanes, lanes) * 2 + sc for sc in range(2)]

    order = pair_of(1) + [me, other]
    for k in range(2, lanes):
        order += pair_of(k)
    first_group = 4

    def fetch(i):
        return pltpu.make_async_copy(cots_hbm.at[order[i]], cots.at[i % first_group], cot_sems.at[i % first_group])

    for i in range(first_group):
        fetch(i).start()

    def place_of(i):
        info = info_ref[order[i]]
        place = jnp.where(info[0:1] == me, info[2:3], jnp.where(info[1:2] == me, info[3:4], -1))
        slot = lax.broadcasted_iota(jnp.int32, (capacity, rows), 0)
        pick = jnp.where(slot == place, 1.0, 0.0)
        gates = gate_rows(order[i])
        which = lax.broadcasted_iota(jnp.int32, gates.shape, 0)
        own_gate = jnp.sum(jnp.where(which == me, gates, 0.0), axis=0, keepdims=True)
        return place, pick, jnp.sum(pick * own_gate, axis=1, keepdims=True)

    def dispatch(i):
        fetch(i).wait()
        _, pick, slot_gate = place_of(i)
        block = slice(i * capacity, (i + 1) * capacity)
        rows_all[block, :] = dot(pick.astype(bf16), nt[order[i]]).astype(bf16)
        cots_all[block, :] = (slot_gate * dot(pick.astype(bf16), cots[i % first_group])).astype(bf16)
        made[i % first_group] = jnp.zeros((capacity, width), f32)
        back[i % first_group] = jnp.zeros((capacity, width), f32)

    def part_of(i, f):
        block = pl.ds(i * capacity if isinstance(i, int) else pl.multiple_of(i * capacity, 16), capacity)
        at = chunk_rows(chunk_at(f))
        turn = i % first_group if isinstance(i, int) else i
        pre = dot(rows_all[block, :], inner[:, at])
        cot = dot(cots_all[block, :], outer[at, :], NT)
        square = pre * pre
        t = jnp.tanh(pre * (ROOT + (ROOT * 0.044715) * square))
        half = 0.5 + 0.5 * t
        act = (pre * half).astype(bf16)
        slope = half + (0.5 * pre) * (1.0 - t * t) * (ROOT + (ROOT * 3 * 0.044715) * square)
        back_pre = (cot * slope).astype(bf16)
        act_all[block, at] = act
        pre_all[block, at] = back_pre
        made[turn] += dot(act, outer[at, :])
        back[turn] += dot(back_pre, inner[:, at], NT)

    def finish_source(i, target):
        place, pick, slot_gate = place_of(i)
        outcome = made[i % first_group].astype(bf16).astype(f32)
        slot_cot = jnp.sum(dot(pick.astype(bf16), cots[i % first_group]) * outcome, axis=1, keepdims=True)
        gate_out[order[i]] = jnp.broadcast_to(jnp.sum(pick * slot_cot, axis=0, keepdims=True), (8, rows))
        column = jnp.broadcast_to(place.astype(f32), (128, rows)).T[:, 0:1]
        lane_at = lax.broadcasted_iota(jnp.int32, (rows, capacity), 1).astype(f32)
        put = jnp.where(lane_at == column, 1.0, 0.0).astype(bf16)
        target[0] = dot(put, back[i % first_group].astype(bf16)).astype(bf16)
        target[1] = dot(put, (slot_gate * outcome).astype(bf16)).astype(bf16)
        if i + first_group < len(order):
            fetch(i + first_group).start()

    def process(i, target):
        dispatch(i)

        def step(f, carry):
            part_of(i, f)
            return carry

        lax.fori_loop(0, n, step, 0)
        finish_source(i, target)

    def pair_copies(k, sc):
        return [
            remote(part.at[sc, v], pair_in.at[v], pair_sems.at[0, v, k - 1], pair_sems.at[1, v, k - 1], {"expert": other})
            for v in range(2)
        ]

    def home_copy(k, sc):
        to = lax.rem(lane - k + lanes, lanes) * 2 + sc
        return remote(part.at[sc, 0], far_in.at[k - 1], back_sems.at[0, k - 1], back_sems.at[1, k - 1], {"expert": to})

    def begin_pair(k, sc):
        @pl.when(core != sc)
        def _():
            if k > 1:
                pl.semaphore_wait(free_sem, 1)
            for copy in pair_copies(k, sc):
                copy.start()

    def end_pair(k, sc):
        @pl.when(core == sc)
        def _():
            pair = pair_copies(k, sc)
            pair[0].wait_recv()
            part[sc, 0] = (part[sc, 0].astype(f32) + pair_in[0].astype(f32)).astype(bf16)
            home_copy(k, sc).start()
            pair[1].wait_recv()
            far_ref[k - 1] = (part[sc, 1].astype(f32) + pair_in[1].astype(f32)).astype(bf16)
            if k + 1 < lanes:
                pl.semaphore_signal(
                    free_sem, inc=1, device_id={"expert": other}, device_id_type=pl.DeviceIdType.MESH
                )

    def pair_sent(k):
        for sc in range(2):
            @pl.when(core != sc)
            def _():
                for copy in pair_copies(k, sc):
                    copy.wait_send()

    def home_sent(k):
        for sc in range(2):
            @pl.when(core == sc)
            def _():
                home_copy(k, sc).wait_send()

    dispatch(2)
    for p in range(pieces):
        sent[p][0].wait_recv()
    dispatch(3)
    first.wait()
    for f in range(n - 1):
        load(f).wait()

    def steps_of(start):
        def step(at, carry):
            part_of(start + lax.rem(at, 2), lax.div(at, 2))
            return carry

        return step

    lax.fori_loop(0, 2 * (n - 1), steps_of(2), 0)
    passed_on = []
    for k in range(1, lanes):
        for p in range(pieces):
            sent[p][k].wait_recv()
        passed = relay(k, nt, relay_sems)
        passed.start()
        passed_on.append(passed)

    def relayed(k, sc):
        @pl.when(core != sc)
        def _():
            passed_on[k - 1].wait_recv()

    for sc in range(2):
        relayed(1, sc)
        dispatch(sc)
    lax.fori_loop(0, 2 * (n - 1), steps_of(0), 0)

    @pl.when(has(n - 1))
    def _():
        load(n - 1).wait()

    @pl.when(place_z == n - 1)
    def _():
        late(True).wait_recv()

    @pl.when(place_z == 0)
    def _():
        late(False).wait_recv()

    lax.fori_loop(2 * (n - 1), 2 * n, steps_of(0), 0)
    finish_source(0, part.at[0])
    begin_pair(1, 0)
    finish_source(1, part.at[1])
    begin_pair(1, 1)
    end_pair(1, 0)
    lax.fori_loop(2 * (n - 1), 2 * n, steps_of(2), 0)
    end_pair(1, 1)
    pair_sent(1)
    finish_source(3, part.at[1 - core])
    core_copies = [
        remote(part.at[1 - core, v], core_in.at[v], core_sems.at[0, v], core_sems.at[1, v], {"expert": other}) for v in range(2)
    ]
    for copy in core_copies:
        copy.start()
    finish_source(2, total)

    def gate_copy(k):
        to = lax.rem(me + k, experts)
        return remote(gate_out.at[to], gate_in.at[me], gate_sems.at[0, k - 1], gate_sems.at[1, k - 1], {"expert": to})

    for k in range(2, lanes):
        if k == 2:
            for copy in core_copies:
                copy.wait_send()
        home_sent(k - 1)
        for sc in range(2):
            relayed(k, sc)
            process(2 * k + sc, part.at[sc])
            begin_pair(k, sc)
        for sc in range(2):
            end_pair(k, sc)
        pair_sent(k)
    gate_copies = [gate_copy(k) for k in range(1, experts)]
    for copy in gate_copies:
        copy.start()
    count = rows_all.shape[0]
    for b in range(count // 128):
        at = slice(b * 128, (b + 1) * 128)
        inner[:, at] = rows_all[at, :].T
        inner[:, slice(count + b * 128, count + (b + 1) * 128)] = cots_all[at, :].T
    wide = width
    steps = hidden_size // wide

    def store(f, v):
        at = pl.ds(pl.multiple_of(f * wide, wide), wide)
        return pltpu.make_async_copy(outer.at[v * width : (v + 1) * width], gin_hbm.at[:, at] if v == 0 else gout_hbm.at[at, :], stage_sems.at[v])

    def grads(f, carry):
        at = pl.ds(pl.multiple_of(f * wide, wide), wide)

        @pl.when(f > 0)
        def _():
            store(f - 1, 0).wait()

        outer[:width, :] = dot(inner[:, :count], pre_all[:, at]).astype(bf16)
        store(f, 0).start()

        @pl.when(f > 0)
        def _():
            store(f - 1, 1).wait()

        outer[width : 2 * width, :] = dot(inner[:, count : 2 * count], act_all[:, at]).astype(bf16).T
        store(f, 1).start()
        return carry

    lax.fori_loop(0, steps, grads, 0)
    for copy in gate_copies:
        copy.wait()
    gates = gate_rows(me)
    pad = gates.shape[0]
    which = lax.broadcasted_iota(jnp.int32, gates.shape, 0)
    gate_cot = jnp.where(which == me, gate_out[me][0:1], 0.0)
    for k in range(1, experts):
        source = lax.rem(me + k, experts)
        gate_cot = gate_cot + jnp.where(which == source, gate_in[source][0:1], 0.0)
    logit_cot = gates * (gate_cot - jnp.sum(gates * gate_cot, axis=0, keepdims=True))
    three = jnp.concatenate(split3(logit_cot), axis=0)
    router_three = jnp.concatenate([router] * 3, axis=0)
    router_grad = dot(three, nt[me])
    small_ref[8:, :] = router_grad[:pad] + router_grad[pad : 2 * pad] + router_grad[2 * pad :]
    for copy in core_copies:
        copy.wait_recv()
    for k in range(1, lanes):
        remote(part.at[0, 0], far_in.at[k - 1], back_sems.at[0, k - 1], back_sems.at[1, k - 1], {"expert": other}).wait_recv()
    gain = gain_ref[...].reshape(1, width)
    gain_grad = jnp.zeros((1, width), f32)
    for start in range(0, rows, 128):
        at = slice(start, start + 128)
        normed_cot = total[0, at, :].astype(f32) + core_in[0, at, :].astype(f32)
        for k in range(1, lanes):
            normed_cot = normed_cot + far_in[k - 1, at, :].astype(f32)
        normed_cot = normed_cot + dot(three[:, at], router_three, TN)
        now = hidden[at, :]
        scale = lax.rsqrt(jnp.mean(now * now, axis=1, keepdims=True) + EPSILON)
        unit = now * scale
        gained = normed_cot * gain
        hidden_cot = cot_ref[at, :].astype(f32) + scale * (gained - unit * jnp.mean(unit * gained, axis=1, keepdims=True))
        hidden_cot_ref[at, :] = hidden_cot
        mixed_cot_ref[:, at] = dot(w_output[...], hidden_cot.astype(bf16), NT).astype(bf16)
        gain_grad = gain_grad + jnp.sum(unit * normed_cot, axis=0, keepdims=True)
        base_ref[at, :] = now + (total[1, at, :].astype(f32) + core_in[1, at, :].astype(f32))
    small_ref[0:8, :] = jnp.broadcast_to(gain_grad, (8, width))
    store(steps - 1, 0).wait()
    store(steps - 1, 1).wait()
    home_sent(lanes - 1)
    if lanes == 2:
        for copy in core_copies:
            copy.wait_send()
    for copy in passed_on:
        copy.wait_send()
    for p in range(pieces):
        for copy in sent[p]:
            copy.wait_send()

    @pl.when(place_z == n - 2)
    def _():
        late(True).wait_send()

    @pl.when(place_z == 1)
    def _():
        late(False).wait_send()


def moe_pass(capacity, mixed_t, w_output, x, cot, gain, router, info, cots, inner, outer):
    rows, width = cot.shape
    experts = cots.shape[0]
    lanes = experts // 2
    hidden_size = inner.shape[1]
    total = experts * capacity
    vmem = pl.BlockSpec(memory_space=pltpu.VMEM)
    hbm = pl.BlockSpec(memory_space=pl.ANY)
    dma = pltpu.SemaphoreType.DMA
    far = max(lanes - 1, 1)
    return pl.pallas_call(
        partial(moe_kernel, capacity),
        out_shape=[
            jax.ShapeDtypeStruct((rows, width), f32),
            jax.ShapeDtypeStruct((far, rows, width), bf16),
            jax.ShapeDtypeStruct((rows, width), f32),
            jax.ShapeDtypeStruct((width, rows), bf16),
            jax.ShapeDtypeStruct((24, width), f32),
            jax.ShapeDtypeStruct((width, hidden_size), bf16),
            jax.ShapeDtypeStruct((hidden_size, width), bf16),
        ],
        in_specs=[vmem] * 7 + [hbm] * 3,
        out_specs=[vmem] * 5 + [hbm] * 2,
        scratch_shapes=[
            pltpu.VMEM((experts, rows, width), bf16),
            pltpu.VMEM((4, rows, width), bf16),
            pltpu.VMEM((width, hidden_size), bf16),
            pltpu.VMEM((hidden_size, width), bf16),
            pltpu.VMEM((total, hidden_size), bf16),
            pltpu.VMEM((total, hidden_size), bf16),
            pltpu.VMEM((total, width), bf16),
            pltpu.VMEM((total, width), bf16),
            pltpu.VMEM((4, capacity, width), f32),
            pltpu.VMEM((4, capacity, width), f32),
            pltpu.VMEM((2, 2, rows, width), bf16),
            pltpu.VMEM((2, rows, width), bf16),
            pltpu.VMEM((2, rows, width), bf16),
            pltpu.VMEM((2, rows, width), bf16),
            pltpu.VMEM((far, rows, width), bf16),
            pltpu.VMEM((experts, 8, rows), f32),
            pltpu.VMEM((experts, 8, rows), f32),
            dma((lax.axis_size("ctx") + 1,)),
            dma((4,)),
            dma((2, 2)),
            dma((2, 2, far)),
            dma((2, far)),
            dma((2, 2, far)),
            dma((2, 2)),
            dma((2, far)),
            dma((2, experts - 1)),
            dma((2,)),
            pltpu.SemaphoreType.REGULAR,
            dma((2, 2)),
            pltpu.VMEM((16, width), f32),
        ],
        compiler_params=pltpu.CompilerParams(
            collective_id=1, has_side_effects=True, vmem_limit_bytes=65000 * 1024
        ),
        name="moe_pass",
    )(mixed_t, w_output, x, cot, gain, router, info, cots, inner, outer)


def bias_line(distance, table):
    far = jnp.full(distance.shape, BUCKETS // 2, jnp.int32)
    for limit in THRESHOLDS:
        far = far + jnp.where(distance >= limit, 1, 0)
    bucket = jnp.where(distance < BUCKETS // 2, distance, far)
    own = (distance >= 0) & (distance < THRESHOLDS[-1])
    which = lax.broadcasted_iota(jnp.int32, (BUCKETS, distance.shape[1]), 0)
    hot = jnp.where(own & (which == bucket), 1.0, 0.0).astype(bf16)
    last = table[:, BUCKETS - 1 :].astype(f32)
    return dot(table, hot) - jnp.where(own, last, 0.0)


def column_of(row):
    return jnp.broadcast_to(row, (128, row.shape[1])).T


def front_kernel(
    heads, n, rows, x_ref, gain_ref, wq, wk, wv, table_ref, segment_ref, routes_ref, order_ref, cot_hbm, win_hbm, wout_hbm,
    held, mixed, of_ref, lse_ref, normed_t, infos, cots_hbm, win_all, wout_all,
    made, given, qa, ka, vn, bias, s_ref, lines,
    held_sems, mixed_sems, near_sems, far_sems, relay_sems, info_sems, own_sems, line_sems, side_sems,
):
    size = 64
    group = heads * size
    width = n * group
    length = n * rows
    sides = lax.axis_size("dp")
    me = lax.axis_index("ctx")
    side = lax.axis_index("dp")
    experts = lax.axis_size("expert")
    expert = lax.axis_index("expert")
    barrier = pltpu.get_barrier_semaphore()
    for name, count, at in (("ctx", n, me), ("dp", sides, side), ("expert", experts, expert)):
        for k in range(1, count):
            pl.semaphore_signal(
                barrier, inc=1, device_id={name: lax.rem(at + k, count)}, device_id_type=pl.DeviceIdType.MESH
            )
    owns = [
        pltpu.make_async_copy(cot_hbm, cots_hbm.at[expert], own_sems.at[0]),
        pltpu.make_async_copy(win_hbm, win_all.at[me * sides + side], own_sems.at[1]),
        pltpu.make_async_copy(wout_hbm, wout_all.at[me * sides + side], own_sems.at[2]),
    ]
    for copy in owns:
        copy.start()
    pl.semaphore_wait(barrier, n + sides + experts - 3)
    shard = (win_hbm, wout_hbm)
    whole = (win_all, wout_all)

    def along(way, s, v):
        j = me - s if way == 0 else me + s
        to = me + 1 if way == 0 else me - 1
        at = j * sides + side
        source = shard[v] if s == 0 else whole[v].at[at]
        return remote(source, whole[v].at[at], line_sems.at[0, way, v, s], line_sems.at[1, way, v, s], {"ctx": to})

    def across(way, s, v):
        j = me - s if way == 0 else me + s
        at = j * sides + side
        source = shard[v] if s == 0 else whole[v].at[at]
        return [
            remote(
                source, whole[v].at[at], side_sems.at[0, way, v, k - 1, s], side_sems.at[1, way, v, k - 1, s],
                {"dp": lax.rem(side + k, sides)},
            )
            for k in range(1, sides)
        ]

    def holds(way, s):
        return me - s >= 0 if way == 0 else me + s < n

    def passes(way, s, v):
        if v == 1 and s == n - 2:
            return None
        return (me - s >= 0) & (me < n - 1) if way == 0 else (me + s < n) & (me > 0)

    def advance(s, v):
        for way in range(2):
            if s > 0:
                @pl.when(holds(way, s))
                def _():
                    along(way, s - 1, v).wait_recv()

            if passes(way, s, v) is not None:
                @pl.when(passes(way, s, v))
                def _():
                    along(way, s, v).start()

            if s > 0:
                @pl.when(holds(way, s))
                def _():
                    for copy in across(way, s, v):
                        copy.start()

    for v in range(2):
        for copy in across(0, 0, v):
            copy.start()
        advance(0, v)
    sent = gather_start(cot_hbm, cots_hbm, near_sems, far_sems)

    x = x_ref[...].astype(f32)
    normed = x * lax.rsqrt(jnp.mean(x * x, axis=1, keepdims=True) + EPSILON) * gain_ref[...].reshape(1, width)
    normed = normed.astype(bf16)
    held_copies = []
    here = pl.ds(pl.multiple_of(me * group, 16), group)
    seg = jnp.broadcast_to(segment_ref[...].astype(f32), (16, rows)).astype(bf16)
    made[3, 0:16, :] = seg
    held[me, 3 * group : 3 * group + 16, :] = seg
    for kind, weight in enumerate((wq, wk, wv)):
        made[kind] = dot(normed, weight[...]).astype(bf16).T
        for k in range(1, n):
            to = lax.rem(me + k, n)
            copy = remote(
                made.at[kind, pl.ds(pl.multiple_of(to * group, 16), group)],
                held.at[me, kind * group : (kind + 1) * group],
                held_sems.at[0, kind, k - 1], held_sems.at[1, kind, k - 1], {"ctx": to},
            )
            copy.start()
            held_copies.append(copy)
        held[me, kind * group : (kind + 1) * group, :] = made[kind, here, :]
    for k in range(1, n):
        copy = remote(
            made.at[3, 0:16], held.at[me, 3 * group : 3 * group + 16], held_sems.at[0, 3, k - 1], held_sems.at[1, 3, k - 1],
            {"ctx": lax.rem(me + k, n)},
        )
        copy.start()
        held_copies.append(copy)
    normed_t[...] = normed.T

    order_row = order_ref[...].astype(f32)
    before = jnp.where(column_of(order_row)[:, 0:1] < order_row, 1.0, 0.0).astype(bf16)
    kinds = 16
    which = lax.broadcasted_iota(jnp.int32, (kinds, rows), 0)
    chosen = [routes_ref[c : c + 1, :] for c in range(2)]
    hot = [jnp.where(which == c, 1.0, 0.0) for c in chosen]
    ahead = [dot(h.astype(bf16), before) for h in hot]
    firsts = jnp.sum(hot[0], axis=1, keepdims=True)
    slots = [jnp.sum(hot[0] * ahead[0], axis=0, keepdims=True), jnp.sum(hot[1] * (ahead[1] + firsts), axis=0, keepdims=True)]
    infos[expert] = jnp.concatenate(chosen + [s.astype(jnp.int32) for s in slots] + [jnp.zeros((4, rows), jnp.int32)], axis=0)
    info_copies = [
        remote(infos.at[expert], infos.at[expert], info_sems.at[0, k - 1], info_sems.at[1, k - 1], {"expert": lax.rem(expert + k, experts)})
        for k in range(1, experts)
    ]
    for copy in info_copies:
        copy.start()
    lines[...] = bias_line(BLK - lax.broadcasted_iota(jnp.int32, (1, 2 * BLK), 1), table_ref[...])

    advance(1, 0)
    advance(1, 1)
    advance(2, 0)
    for copy in held_copies:
        copy.wait_recv()

    def mixed_copy(h, k):
        to = lax.rem(me + k, n)
        base = pl.multiple_of(h * size, size)
        return remote(
            given.at[to, pl.ds(base, size)], mixed.at[pl.ds(pl.multiple_of(me * group + base, 16), size)],
            mixed_sems.at[0, h, k - 1], mixed_sems.at[1, h, k - 1], {"ctx": to},
        )

    def head(h, carry):
        base = pl.multiple_of(h * size, size)
        for s in range(n):
            at = slice(s * rows, (s + 1) * rows)
            q = held[s, pl.ds(base, size), :]
            k = held[s, pl.ds(base + group, size), :]
            v = held[s, pl.ds(base + 2 * group, size), :]
            mask, hot = seg_mask_rows(held[s, 3 * group : 3 * group + 16, :])
            zeros = jnp.zeros((48, rows), bf16)
            qa[at, :] = jnp.concatenate([q * jnp.asarray(0.125, bf16), mask, zeros], axis=0).T
            ka[:, at] = jnp.concatenate([k, hot, zeros], axis=0)
            vn[at, :] = jnp.concatenate([v, jnp.zeros((64, rows), bf16)], axis=0).T
        line = jnp.broadcast_to(lines[pl.ds(me * heads + h, 1), :], (BLK, 2 * BLK))
        rolled = pltpu.roll(line, 0, 1, stride=1, stride_axis=0)
        r = lax.broadcasted_iota(jnp.int32, (BLK, 2 * BLK), 0)
        c = lax.broadcasted_iota(jnp.int32, (BLK, 2 * BLK), 1)
        bias[...] = jnp.where(c - r > BLK, NEG, rolled)
        for t in range(length // BLK):
            qt = qa[t * BLK : (t + 1) * BLK, :]
            near0 = max(t - 1, 0) * BLK
            end = (t + 1) * BLK
            chunks = [(near0, end)] + [(a, min(a + 2 * BLK, near0)) for a in range(0, near0, 2 * BLK)]
            top = None
            for a, b in chunks:
                s = dot(qt, ka[:, a:b])
                if a == near0:
                    s = s + bias[:, 2 * BLK - (b - a) :]
                s_ref[:, a:b] = s
                part = s[:, :128]
                for i in range(1, (b - a) // 128):
                    part = jnp.maximum(part, s[:, i * 128 : (i + 1) * 128])
                top = part if top is None else jnp.maximum(top, part)
            m = jnp.max(top, axis=1, keepdims=True)
            total = None
            o = None
            for a, b in chunks:
                p = jnp.exp(s_ref[:, a:b] - m)
                part = p[:, :128]
                for i in range(1, (b - a) // 128):
                    part = part + p[:, i * 128 : (i + 1) * 128]
                total = part if total is None else total + part
                u = dot(p.astype(bf16), vn[a:b, :])
                o = u if o is None else o + u
            l = jnp.sum(total, axis=1, keepdims=True)
            o = o / l
            lane = lax.broadcasted_iota(jnp.int32, (BLK, 128), 1)
            o = jnp.where(lane == 64, m + jnp.log(l), o)
            ot = o.T
            src, off = (t * BLK) // rows, (t * BLK) % rows
            given[src, pl.ds(base, size), off : off + BLK] = ot[:size].astype(bf16)
            of_ref[pl.ds(base, size), t * BLK : (t + 1) * BLK] = ot[:size]
            lse_ref[pl.ds(h, 1), t * BLK : (t + 1) * BLK] = ot[size : size + 1]
        for k in range(1, n):
            mixed_copy(h, k).start()
        mixed[pl.ds(pl.multiple_of(me * group + base, 16), size), :] = given[me, pl.ds(base, size), :]

        @pl.when(h == 0)
        def _():
            advance(2, 1)

        @pl.when(h == 1)
        def _():
            for s in range(3, n):
                advance(s, 0)

        return carry

    lax.fori_loop(0, heads, head, 0)
    relays = []
    for k in range(1, experts // 2):
        sent[k].wait_recv()
        passed = relay(k, cots_hbm, relay_sems)
        passed.start()
        relays.append(passed)
    sent[0].wait_recv()
    for h in range(heads):
        for k in range(1, n):
            mixed_copy(h, k).wait()
    for copy in held_copies + sent:
        copy.wait_send()
    for copy in relays + info_copies + owns:
        copy.wait()
    for v in range(2):
        for s in range(n):
            for way in range(2):
                if v == 1 and s == n - 1:
                    continue
                if passes(way, s, v) is not None:
                    @pl.when(passes(way, s, v))
                    def _():
                        along(way, s, v).wait_send()

                if s > 0 or way == 0:
                    @pl.when(holds(way, s))
                    def _():
                        for copy in across(way, s, v):
                            copy.wait()


def front_pass(x, gain, wq, wk, wv, table, segments, routes, order, cot, win, wout):
    rows, width = x.shape
    n = lax.axis_size("ctx")
    sides = lax.axis_size("dp")
    experts = lax.axis_size("expert")
    heads = table.shape[0] // n
    group = heads * 64
    length = n * rows
    blocks = n * sides
    vmem = pl.BlockSpec(memory_space=pltpu.VMEM)
    hbm = pl.BlockSpec(memory_space=pl.ANY)
    dma = pltpu.SemaphoreType.DMA
    far = max(experts // 2 - 1, 1)
    some = max(sides - 1, 1)
    return pl.pallas_call(
        partial(front_kernel, heads, n, rows),
        out_shape=[
            jax.ShapeDtypeStruct((n, 3 * group + 16, rows), bf16),
            jax.ShapeDtypeStruct((width, rows), bf16),
            jax.ShapeDtypeStruct((group, length), f32),
            jax.ShapeDtypeStruct((heads, length), f32),
            jax.ShapeDtypeStruct((width, rows), bf16),
            jax.ShapeDtypeStruct((experts, 8, rows), jnp.int32),
            jax.ShapeDtypeStruct((experts, rows, width), bf16),
            jax.ShapeDtypeStruct((blocks,) + win.shape, bf16),
            jax.ShapeDtypeStruct((blocks,) + wout.shape, bf16),
        ],
        in_specs=[vmem] * 9 + [hbm] * 3,
        out_specs=[vmem] * 6 + [hbm] * 3,
        scratch_shapes=[
            pltpu.VMEM((4, width, rows), bf16),
            pltpu.VMEM((n, group, rows), bf16),
            pltpu.VMEM((length, 128), bf16),
            pltpu.VMEM((128, length), bf16),
            pltpu.VMEM((length, 128), bf16),
            pltpu.VMEM((BLK, 2 * BLK), f32),
            pltpu.VMEM((BLK, length), f32),
            pltpu.VMEM((table.shape[0], 2 * BLK), f32),
            dma((2, 4, n - 1)),
            dma((2, heads, n - 1)),
            dma((2,)),
            dma((2, far)),
            dma((2, far)),
            dma((2, experts - 1)),
            dma((3,)),
            dma((2, 2, 2, n)),
            dma((2, 2, 2, some, n)),
        ],
        compiler_params=pltpu.CompilerParams(
            collective_id=2, has_side_effects=True, vmem_limit_bytes=60 * 1024 * 1024
        ),
        name="front_pass",
    )(x, gain, wq, wk, wv, table, segments, routes, order, cot, win, wout)


def line_order(n):
    order = []
    for i in range((n + 1) // 2):
        order.append(n - 1 - i)
        if i != n - 1 - i:
            order.append(i)
    return order


def line_scatter(n, own, right, left, right_sems, left_sems, ready):
    me = lax.axis_index("ctx")
    items = {}
    for j in line_order(n):
        for r in range(j):
            items.setdefault(ready[j] + r, []).append((0, r, j))
        for r in range(n - 1, j, -1):
            items.setdefault(ready[j] + n - 1 - r, []).append((1, r, j))
    steps = max(items) + 1

    def pass_on(way, r, j):
        taken, sems = (right, right_sems) if way == 0 else (left, left_sems)
        first = 0 if way == 0 else n - 1
        return remote(
            own.at[j] if r == first else taken.at[j], taken.at[j], sems.at[0, j], sems.at[1, j],
            {"ctx": r + 1 if way == 0 else r - 1},
        )

    def advance(step):
        for way, r, j in items.get(step, []):
            @pl.when(me == r)
            def _():
                copy = pass_on(way, r, j)
                if r != (0 if way == 0 else n - 1):
                    taken = right if way == 0 else left
                    copy.wait_recv()
                    taken[j] = (taken[j].astype(f32) + own[j].astype(f32)).astype(bf16)
                copy.start()

    def finish(out):
        for j in range(n):
            @pl.when(me == j)
            def _():
                total = own[j].astype(f32)
                if j > 0:
                    pass_on(0, j - 1, j).wait_recv()
                    total = total + right[j].astype(f32)
                if j < n - 1:
                    pass_on(1, j + 1, j).wait_recv()
                    total = total + left[j].astype(f32)
                out[...] = total.astype(bf16)

    def drain():
        for step in range(steps):
            for way, r, j in items.get(step, []):
                @pl.when(me == r)
                def _():
                    pass_on(way, r, j).wait_send()

    return advance, finish, drain, steps


def back_kernel(
    heads, n, rows, x_ref, do_ref, table_ref, of_ref, lse_ref, base_ref, far_ref, gin_hbm, gout_hbm,
    cots_ref, diag_ref, ein_ref, own_b, out_ref,
    do_in, g_ref, qa, ka, va, da, qn, dn, bias, dq, gsum,
    own_a, side_a, side_b, right_a, left_a,
    do_sems, out_sems, own_sems, side_sems, right_sems, left_sems, lines, far_in, far_sems,
):
    size = 64
    group = heads * size
    length = n * rows
    sides = lax.axis_size("dp")
    me = lax.axis_index("ctx")
    side = lax.axis_index("dp")
    barrier, peers = greet(("ctx", "dp", "expert"))
    order = line_order(n)
    advance, finish, drain, steps = line_scatter(
        n, own_a, right_a, left_a, right_sems, left_sems, {j: i for i, j in enumerate(order)}
    )
    loads = {}
    for j in order:
        at = j * sides + side
        loads[j] = [
            pltpu.make_async_copy(gin_hbm.at[at], own_a.at[j], own_sems.at[0, j]),
            pltpu.make_async_copy(gout_hbm.at[at], own_b.at[j], own_sems.at[1, j]),
        ]
        for copy in loads[j]:
            copy.start()
    pl.semaphore_wait(barrier, peers)
    lanes, lane, core = expert_split()
    homes = [
        remote(
            far_ref.at[k - 1], far_in.at[k - 1], far_sems.at[0, k - 1], far_sems.at[1, k - 1],
            {"expert": lax.rem(lane - k + lanes, lanes) * 2 + core},
        )
        for k in range(1, lanes)
    ]
    for copy in homes:
        copy.start()
    lines[...] = bias_line(lax.broadcasted_iota(jnp.int32, (1, 2 * BLK), 1), table_ref[...])
    arriving = []
    for k in range(1, n):
        to = lax.rem(me + k, n)
        copy = remote(
            do_ref.at[pl.ds(pl.multiple_of(to * group, 16), group)], do_in.at[me], do_sems.at[0, k - 1], do_sems.at[1, k - 1], {"ctx": to}
        )
        copy.start()
        arriving.append(copy)
    beside = {}
    for v, gone, taken in ((0, gin_hbm, side_a), (1, gout_hbm, side_b)):
        for j in order:
            beside[v, j] = []
            for k in range(1, sides):
                to = lax.rem(side + k, sides)
                beside[v, j].append(
                    remote(
                        gone.at[j * sides + to], taken.at[k - 1, j],
                        side_sems.at[0, v, k - 1, j], side_sems.at[1, v, k - 1, j], {"dp": to},
                    )
                )
                beside[v, j][-1].start()

    def sum_sides(v, j):
        own, taken = ((own_a, side_a), (own_b, side_b))[v]
        loads[j][v].wait()
        total = own[j].astype(f32)
        for k in range(1, sides):
            beside[v, j][k - 1].wait_recv()
            total = total + taken[k - 1, j].astype(f32)
        own[j] = total.astype(bf16)

    do_in[me] = do_ref[pl.ds(pl.multiple_of(me * group, 16), group), :]

    sum_sides(0, order[0])
    advance(0)
    for copy in arriving:
        copy.wait_recv()

    def out_copy(h, kind, k):
        to = lax.rem(me + k, n)
        base = pl.multiple_of(h * size, size)
        return remote(
            g_ref.at[to, pl.ds(kind * group + base, size)],
            cots_ref.at[pl.ds(pl.multiple_of(kind * n * group + me * group + base, 16), size)],
            out_sems.at[0, h, kind, k - 1],
            out_sems.at[1, h, kind, k - 1],
            {"ctx": to},
        )

    def head(h, carry):
        base = pl.multiple_of(h * size, size)
        for s in range(n):
            at = slice(s * rows, (s + 1) * rows)
            q = x_ref[s, pl.ds(base, size), :] * jnp.asarray(0.125, bf16)
            k = x_ref[s, pl.ds(base + group, size), :]
            v = x_ref[s, pl.ds(base + 2 * group, size), :]
            d = do_in[s, pl.ds(base, size), :]
            seg = x_ref[s, 3 * group : 3 * group + 16, :]
            mask, hot = seg_mask_rows(seg)
            which = lax.broadcasted_iota(jnp.int32, (16, rows), 0)

            def rows3(vec):
                hi, mid, lo = split3(jnp.broadcast_to(vec, (16, rows)))
                return jnp.where(which == 0, hi, jnp.where(which == 1, mid, jnp.where(which == 2, lo, jnp.zeros((), bf16))))

            ones = jnp.where(which < 3, 1.0, 0.0).astype(bf16)
            zeros = jnp.zeros((32, rows), bf16)
            zeros48 = jnp.zeros((48, rows), bf16)
            lse = lse_ref[pl.ds(h, 1), at]
            delta = jnp.sum(of_ref[pl.ds(base, size), at] * d.astype(f32), axis=0, keepdims=True)
            qt = jnp.concatenate([q, mask, rows3(-lse), zeros], axis=0)
            qa[:, at] = qt
            qn[at, :] = qt.T
            ka[at, :] = jnp.concatenate([k, hot, ones, zeros], axis=0).T
            dt = jnp.concatenate([d, rows3(-delta), zeros48], axis=0)
            da[:, at] = dt
            dn[at, :] = dt.T
            va[at, :] = jnp.concatenate([v, ones, zeros48], axis=0).T
        line = jnp.broadcast_to(lines[pl.ds(me * heads + h, 1), :], (BLK, 2 * BLK))
        rolled = pltpu.roll(line, 0, 1, stride=1, stride_axis=0)
        r = lax.broadcasted_iota(jnp.int32, (BLK, 2 * BLK), 0)
        c = lax.broadcasted_iota(jnp.int32, (BLK, 2 * BLK), 1)
        bias[...] = jnp.where(c < r, NEG, rolled)
        gsum[...] = jnp.zeros_like(gsum)
        for j in range(length // BLK):
            a0 = j * BLK
            kj = ka[a0 : a0 + BLK, :]
            vj = va[a0 : a0 + BLK, :]
            src, off = a0 // rows, a0 % rows
            kt = x_ref[src, pl.ds(base + group, size), off : off + BLK]
            dk = dv = None
            for a in range(a0, length, 2 * BLK):
                b = min(a + 2 * BLK, length)
                s = dot(kj, qa[:, a:b])
                if a == a0:
                    s = s + bias[:, : b - a]
                p = jnp.exp(s)
                ds = p * dot(vj, da[:, a:b])
                if a == a0:
                    gsum[:, : b - a] += ds
                p_low, ds_low = p.astype(bf16), ds.astype(bf16)
                u = dot(p_low, dn[a:b, :])
                dv = u if dv is None else dv + u
                u = dot(ds_low, qn[a:b, :])
                dk = u if dk is None else dk + u
                u = dot(kt, ds_low)
                if j == 0:
                    dq[:, a:b] = u
                else:
                    dq[:, a:b] += u
            g_ref[src, pl.ds(base + group, size), off : off + BLK] = dk.T[:size].astype(bf16)
            g_ref[src, pl.ds(base + 2 * group, size), off : off + BLK] = dv.T[:size].astype(bf16)
        for s in range(n):
            g_ref[s, pl.ds(base, size), :] = (dq[:, s * rows : (s + 1) * rows] * 0.125).astype(bf16)
        for kind in range(3):
            for k in range(1, n):
                out_copy(h, kind, k).start()
            cots_ref[pl.ds(pl.multiple_of(kind * n * group + me * group + base, 16), size), :] = g_ref[
                me, pl.ds(kind * group + base, size), :
            ]
        eight = gsum[0:8, :]
        for i in range(1, BLK // 8):
            eight = eight + pltpu.roll(gsum[8 * i : 8 * i + 8, :], 2 * BLK - 8 * i, 1)
        line = eight[0:1]
        for i in range(1, 8):
            line = line + pltpu.roll(eight, 2 * BLK - i, 1)[i : i + 1]
        diag_ref[pl.ds(h, 1), :] = line
        for step in range(1, heads):
            @pl.when(h == step - 1)
            def _():
                if step < n:
                    sum_sides(0, order[step])
                advance(step)

        return carry

    lax.fori_loop(0, heads, head, 0)
    for step in range(heads, steps):
        if step < n:
            sum_sides(0, order[step])
        advance(step)
        if step >= n and step - n < n:
            sum_sides(1, order[step - n])
    for i in range(max(steps - n, 0), n):
        sum_sides(1, order[i])
    mixture = base_ref[...]
    for k in range(1, lanes):
        homes[k - 1].wait()
        mixture = mixture + far_in[k - 1].astype(f32)
    out_ref[...] = mixture.astype(bf16)
    finish(ein_ref)
    for h in range(heads):
        for kind in range(3):
            for k in range(1, n):
                out_copy(h, kind, k).wait()
    for copy in arriving:
        copy.wait_send()
    for copies in beside.values():
        for copy in copies:
            copy.wait_send()
    drain()


def back_pass(x, do, table, of, lse, base, far, gin, gout):
    n, depth, rows = x.shape
    heads = table.shape[0] // n
    group = heads * 64
    length = n * rows
    sides = lax.axis_size("dp")
    _, high_a, wide_a = gin.shape
    _, high_b, wide_b = gout.shape
    vmem = pl.BlockSpec(memory_space=pltpu.VMEM)
    hbm = pl.BlockSpec(memory_space=pl.ANY)
    dma = pltpu.SemaphoreType.DMA
    some = max(sides - 1, 1)
    return pl.pallas_call(
        partial(back_kernel, heads, n, rows),
        out_shape=[
            jax.ShapeDtypeStruct((3 * n * group, rows), bf16),
            jax.ShapeDtypeStruct((heads, 2 * BLK), f32),
            jax.ShapeDtypeStruct((high_a, wide_a), bf16),
            jax.ShapeDtypeStruct((n, high_b, wide_b), bf16),
            jax.ShapeDtypeStruct(base.shape, bf16),
        ],
        in_specs=[vmem] * 7 + [hbm] * 2,
        out_specs=[vmem] * 5,
        scratch_shapes=[
            pltpu.VMEM((n, group, rows), bf16),
            pltpu.VMEM((n, 3 * group, rows), bf16),
            pltpu.VMEM((128, length), bf16),
            pltpu.VMEM((length, 128), bf16),
            pltpu.VMEM((length, 128), bf16),
            pltpu.VMEM((128, length), bf16),
            pltpu.VMEM((length, 128), bf16),
            pltpu.VMEM((length, 128), bf16),
            pltpu.VMEM((BLK, 2 * BLK), f32),
            pltpu.VMEM((64, length), f32),
            pltpu.VMEM((BLK, 2 * BLK), f32),
            pltpu.VMEM((n, high_a, wide_a), bf16),
            pltpu.VMEM((some, n, high_a, wide_a), bf16),
            pltpu.VMEM((some, n, high_b, wide_b), bf16),
            pltpu.VMEM((n, high_a, wide_a), bf16),
            pltpu.VMEM((n, high_a, wide_a), bf16),
            dma((2, n - 1)),
            dma((2, heads, 3, n - 1)),
            dma((2, n)),
            dma((2, 2, some, n)),
            dma((2, n)),
            dma((2, n)),
            pltpu.VMEM((table.shape[0], 2 * BLK), f32),
            pltpu.VMEM(far.shape, bf16),
            dma((2, far.shape[0])),
        ],
        compiler_params=pltpu.CompilerParams(
            collective_id=3, has_side_effects=True, vmem_limit_bytes=60 * 1024 * 1024
        ),
        name="back_pass",
    )(x, do, table, of, lse, base, far, gin, gout)


def add_all(parts):
    return functools.reduce(lambda a, b: a + b, parts)


def axis_stages():
    experts = lax.axis_size("expert")
    me = lax.axis_index("expert")
    core, lane = lax.rem(me, 2), lax.div(me, 2)
    return {
        "core": (2, core, lambda j: {"expert": lane * 2 + j}),
        "lane": (experts // 2, lane, lambda j: {"expert": j * 2 + core}),
        "dp": (lax.axis_size("dp"), lax.axis_index("dp"), lambda j: {"dp": j}),
        "ctx": (lax.axis_size("ctx"), lax.axis_index("ctx"), lambda j: {"ctx": j}),
    }


ORDERS = (("core", "lane", "dp", "ctx"), ("core", "dp", "lane", "ctx"))
SLICES = 2


def sum_plan(sizes, rows):
    plans = []
    for order in ORDERS:
        length, plan = rows // 2, []
        for name in order:
            count = sizes[name]
            split = length % count == 0 and (length // count) % 16 == 0
            plan.append((name, count, length, split))
            if split:
                length = length // count
        plans.append(plan)
    return plans


def received_rows(plans):
    return [
        [(count - 1) * (length // count if split else length) for (_, count, length, split) in plan]
        for plan in plans
    ]


def sizes_of():
    return {
        "core": 2,
        "lane": lax.axis_size("expert") // 2,
        "dp": lax.axis_size("dp"),
        "ctx": lax.axis_size("ctx"),
    }


def tail_kernel(
    plans, normed_t, cots, mixed_t, wq, wk, wv, x_ref, gain_ref, hidden_cot_ref, moe_small_ref, diag_ref, sums_ref,
    grads_ref, input_grad_ref, small_out_ref, eout_ref,
    acc, whole, taken_a, taken_b, small, small_taken, send, recv, back_send, back_recv, small_send, small_recv,
    right, left, right_sems, left_sems,
):
    stages = axis_stages()
    width = wq.shape[0]
    rows = x_ref.shape[0]
    barrier = pltpu.get_barrier_semaphore()
    peers = 0
    for name, (count, me, at) in stages.items():
        for k in range(1, count):
            pl.semaphore_signal(barrier, inc=1, device_id=at(lax.rem(me + k, count)), device_id_type=pl.DeviceIdType.MESH)
            peers += 1

    def make(k):
        if k < 3:
            acc[k * width : (k + 1) * width, :] = dot(
                normed_t[...], cots[k * width : (k + 1) * width, :], NT
            ).astype(bf16)
        else:
            acc[3 * width :, :] = dot(mixed_t[...], hidden_cot_ref[...].astype(bf16)).astype(bf16)

    taken = (taken_a, taken_b)
    half = 2 * width
    piece = width // SLICES
    parts = [(h, c) for c in range(SLICES) for h in range(2)]
    spans = {}
    for part in parts:
        spans[part] = [part[0] * half]

    def columns(part):
        return pl.ds(part[1] * piece, piece)

    def rows_at(start, size):
        return pl.ds(pl.multiple_of(start, 16), size)

    flying = {}

    def send_stage(part, step):
        h, c = part
        name, count, length, split = plans[h][step]
        _, me, at = stages[name]
        start = spans[part][-1]
        size = length // count if split else length
        base = sum(received[h][:step])
        copies = []
        for k in range(1, count):
            peer = lax.rem(me + k, count)
            copies.append(
                pltpu.make_async_remote_copy(
                    src_ref=acc.at[rows_at(start + peer * size if split else start, size), columns(part)],
                    dst_ref=taken[h].at[pl.ds(base + (k - 1) * size, size), columns(part)],
                    send_sem=send.at[h * SLICES + c, step, k - 1],
                    recv_sem=recv.at[h * SLICES + c, step, k - 1],
                    device_id=at(peer),
                    device_id_type=pl.DeviceIdType.MESH,
                )
            )
        for copy in copies:
            copy.start()
        flying[part] = copies

    def add_stage(part, step):
        h, c = part
        name, count, length, split = plans[h][step]
        _, me, at = stages[name]
        size = length // count if split else length
        start = spans[part][-1] + me * size if split else spans[part][-1]
        base = sum(received[h][:step])
        for copy in flying[part]:
            copy.wait()
        total = acc[rows_at(start, size), columns(part)].astype(f32)
        for k in range(1, count):
            total = total + taken[h][base + (k - 1) * size : base + k * size, columns(part)].astype(f32)
        if step == len(plans[h]) - 1:
            whole[rows_at(start, size), columns(part)] = total.astype(bf16)
        else:
            acc[rows_at(start, size), columns(part)] = total.astype(bf16)
        spans[part].append(start)

    def give_stage(part, step):
        h, c = part
        name, count, length, split = plans[h][step]
        if not split:
            flying[part] = []
            return
        _, me, at = stages[name]
        size = length // count
        start = spans[part][step + 1]
        copies = []
        for k in range(1, count):
            peer = lax.rem(me + k, count)
            copies.append(
                pltpu.make_async_remote_copy(
                    src_ref=whole.at[rows_at(start, size), columns(part)],
                    dst_ref=whole.at[rows_at(start, size), columns(part)],
                    send_sem=back_send.at[h * SLICES + c, step, k - 1],
                    recv_sem=back_recv.at[h * SLICES + c, step, k - 1],
                    device_id=at(peer),
                    device_id_type=pl.DeviceIdType.MESH,
                )
            )
        for copy in copies:
            copy.start()
        flying[part] = copies

    n = sums_ref.shape[0]
    advance, finish, drain, line_steps = line_scatter(n, sums_ref, right, left, right_sems, left_sems, [0] * n)
    received = received_rows(plans)
    make(2)
    make(3)
    pl.semaphore_wait(barrier, peers)
    for c in range(SLICES):
        send_stage((1, c), 0)
    advance(0)
    make(0)
    make(1)
    for c in range(SLICES):
        send_stage((0, c), 0)
    parts = [(1, 0), (0, 0), (1, 1), (0, 1)]

    def make_small():
        turned = dot(wq[...], cots[:width, :]) + dot(wk[...], cots[width : 2 * width, :]) + dot(wv[...], cots[2 * width :, :])
        cot = turned.T
        x = x_ref[...].astype(f32)
        gain = gain_ref[...].reshape(1, width)
        scale = lax.rsqrt(jnp.mean(x * x, axis=1, keepdims=True) + EPSILON)
        unit = x * scale
        gained = cot * gain
        input_grad_ref[...] = hidden_cot_ref[...] + scale * (gained - unit * jnp.mean(unit * gained, axis=1, keepdims=True))
        gain_grad = jnp.sum(unit * cot, axis=0, keepdims=True)
        which = lax.broadcasted_iota(jnp.int32, (8, width), 0)
        low = jnp.where(which == 0, gain_grad, jnp.where(which == 1, moe_small_ref[0:8, :], 0.0))
        near_rows, near_lanes = 128, 256
        distance = lax.broadcasted_iota(jnp.int32, (near_rows, near_lanes), 0)
        lane = lax.broadcasted_iota(jnp.int32, (near_rows, near_lanes), 1)
        far = jnp.full(distance.shape, BUCKETS // 2, jnp.int32)
        for limit in THRESHOLDS:
            far = far + jnp.where(distance >= limit, 1, 0)
        bucket = jnp.where(distance < BUCKETS // 2, distance, far)
        own = distance < THRESHOLDS[-1]
        lane_row = lax.broadcasted_iota(jnp.int32, (1, near_lanes), 1)
        which = lax.broadcasted_iota(jnp.int32, (8, near_lanes), 0)
        sums = jnp.zeros((8, near_lanes), f32)
        heads = diag_ref.shape[0]
        for h in range(heads):
            at = lax.axis_index("ctx") * heads + h
            start = lax.div(at, 6) * 128
            hot = jnp.where(own & (bucket + start == lane), 1.0, 0.0).astype(bf16)
            three = split3(jnp.broadcast_to(diag_ref[h : h + 1, :near_rows], (16, near_rows)))
            near = (dot(three[0], hot) + dot(three[1], hot) + dot(three[2], hot))[0:1]
            near = jnp.where(lane_row == start + BUCKETS - 1, -jnp.sum(near, axis=1, keepdims=True), near)
            sums = sums + jnp.where(which == 2 + lax.rem(at, 6), near, 0.0)
        low = low + jnp.concatenate([sums, jnp.zeros((8, width - near_lanes), f32)], axis=1)
        small[0:8, :] = low
        small[8:16, :] = moe_small_ref[8:16, :]

    def send_small(step):
        name = ORDERS[0][step]
        count, me, at = stages[name]
        base = sum(stages[n][0] - 1 for n in ORDERS[0][:step])
        copies = [
            pltpu.make_async_remote_copy(
                src_ref=small,
                dst_ref=small_taken.at[base + k - 1],
                send_sem=small_send.at[base + k - 1],
                recv_sem=small_recv.at[base + k - 1],
                device_id=at(lax.rem(me + k, count)),
                device_id_type=pl.DeviceIdType.MESH,
            )
            for k in range(1, count)
        ]
        for copy in copies:
            copy.start()
        flying["small"] = copies

    def add_small(step):
        base = sum(stages[n][0] - 1 for n in ORDERS[0][:step])
        for copy in flying["small"]:
            copy.wait()
        total = small[...]
        for k in range(len(flying["small"])):
            total = total + small_taken[base + k]
        small[...] = total

    last = len(ORDERS[0])
    for step in range(last):
        for part in parts:
            add_stage(part, step)
            if step + 1 < last:
                send_stage(part, step + 1)
            else:
                give_stage(part, step)
        if step == 0:
            make_small()
        else:
            add_small(step - 1)
        send_small(step)
        if step == 1:
            advance(1)
    for step in range(last - 1, -1, -1):
        for part in parts:
            for copy in flying[part]:
                copy.wait()
            if step > 0:
                give_stage(part, step - 1)
        if step == last - 1:
            add_small(last - 1)
            small_out_ref[...] = small[...]
            for slot in range(2, line_steps):
                advance(slot)
    finish(eout_ref)
    drain()
    grads_ref[...] = whole[...]


def tail_pass(normed_t, cots, mixed_t, wq, wk, wv, x, gain, hidden_cot, moe_small, diag, sums):
    rows, width = x.shape
    sizes = sizes_of()
    plans = sum_plan(sizes, 4 * width)
    received = [sum(r) for r in received_rows(plans)]
    most = max(sizes.values()) - 1
    few = sum(n - 1 for n in sizes.values())
    small = jax.ShapeDtypeStruct((16, width), f32)
    return pl.pallas_call(
        partial(tail_kernel, plans),
        out_shape=[
            jax.ShapeDtypeStruct((4 * width, width), bf16),
            jax.ShapeDtypeStruct((rows, width), f32),
            jax.ShapeDtypeStruct(small.shape, f32),
            jax.ShapeDtypeStruct(sums.shape[1:], bf16),
        ],
        in_specs=[pl.BlockSpec(memory_space=pltpu.VMEM)] * 12,
        out_specs=[pl.BlockSpec(memory_space=pltpu.VMEM)] * 4,
        scratch_shapes=[
            pltpu.VMEM((4 * width, width), bf16),
            pltpu.VMEM((4 * width, width), bf16),
            pltpu.VMEM((received[0], width), bf16),
            pltpu.VMEM((received[1], width), bf16),
            pltpu.VMEM(small.shape, f32),
            pltpu.VMEM((few,) + small.shape, f32),
            pltpu.SemaphoreType.DMA((2 * SLICES, 4, most)),
            pltpu.SemaphoreType.DMA((2 * SLICES, 4, most)),
            pltpu.SemaphoreType.DMA((2 * SLICES, 4, most)),
            pltpu.SemaphoreType.DMA((2 * SLICES, 4, most)),
            pltpu.SemaphoreType.DMA((few,)),
            pltpu.SemaphoreType.DMA((few,)),
            pltpu.VMEM(sums.shape, bf16),
            pltpu.VMEM(sums.shape, bf16),
            pltpu.SemaphoreType.DMA((2, sums.shape[0])),
            pltpu.SemaphoreType.DMA((2, sums.shape[0])),
        ],
        compiler_params=pltpu.CompilerParams(
            collective_id=0, has_side_effects=True, vmem_limit_bytes=56 * 1024 * 1024
        ),
        name="tail_pass",
    )(normed_t, cots, mixed_t, wq, wk, wv, x, gain, hidden_cot, moe_small, diag, sums)


def finish_kernel(heads, width, large_ref, small_ref, *refs):
    extra = (len(refs) - 7) // 2
    ins, outs, others = refs[:extra], refs[extra : extra + 7], refs[extra + 7 :]
    for k in range(4):
        outs[k][...] = large_ref[k].astype(f32)
    for source, out in zip(ins, others):
        out[...] = source[...].astype(f32)

    @pl.when(pl.program_id(0) == 0)
    def _():
        outs[4][...] = small_ref[0:1, :].reshape(width)
        outs[5][...] = small_ref[1:2, :].reshape(width)
        for a in range(0, heads, 6):
            outs[6][a : a + 6, :] = small_ref[2:8, a // 6 * 128 : a // 6 * 128 + BUCKETS]


def finish_pass(large, small, heads, extra):
    _, width, _ = large.shape
    steps = 6
    tall = width // steps
    whole = pl.BlockSpec(small.shape, lambda i: (0, 0))

    def cut(array):
        return pl.BlockSpec((array.shape[0] // steps, array.shape[1]), lambda i: (i, 0))

    flat = pl.BlockSpec((width,), lambda i: (0,))
    return pl.pallas_call(
        partial(finish_kernel, heads, width),
        grid=(steps,),
        out_shape=[jax.ShapeDtypeStruct((width, width), f32)] * 4
        + [jax.ShapeDtypeStruct((width,), f32)] * 2
        + [jax.ShapeDtypeStruct((heads, BUCKETS), f32)]
        + [jax.ShapeDtypeStruct(array.shape, f32) for array in extra],
        in_specs=[pl.BlockSpec((4, tall, width), lambda i: (0, i, 0)), whole] + [cut(array) for array in extra],
        out_specs=[pl.BlockSpec((tall, width), lambda i: (i, 0))] * 4
        + [flat] * 2
        + [pl.BlockSpec((heads, BUCKETS), lambda i: (0, 0))]
        + [cut(array) for array in extra],
        compiler_params=pltpu.CompilerParams(vmem_limit_bytes=60 * 1024 * 1024),
        name="finish_pass",
    )(large, small, *extra)


def local(
    layer_input,
    cotangent,
    norm_gain_one,
    w_query,
    w_key,
    w_value,
    w_output,
    rel_table,
    norm_gain_two,
    w_router,
    w_expert_in,
    w_expert_out,
    segment_ids,
    routes,
    priority,
):
    rows, width = layer_input.shape[1:]
    heads = rel_table.shape[0]
    shards = lax.axis_size("ctx")
    experts = lax.axis_size("expert")
    capacity = min(rows, 5 * rows // (2 * experts))
    blocks = shards * lax.axis_size("dp")

    def padded(array):
        return jnp.pad(array, ((0, 0), (0, -array.shape[1] % 16), (0, 0)))

    held, mixed_t, attended_whole, lse, normed_t, info_all, cots_all, inner_weight, outer_weight = front_pass(
        layer_input[0], norm_gain_one, w_query, w_key, w_value, rel_table, segment_ids, routes[0].T, priority[0],
        cotangent[0], padded(w_expert_in)[0], padded(w_expert_out)[0],
    )
    inner_weight = inner_weight[:, : w_expert_in.shape[1]].reshape(width, -1)
    outer_weight = outer_weight[:, : w_expert_out.shape[1]].reshape(-1, width)
    router_t = w_router.T
    base, far, hidden_cot, mixed_cot, moe_small, inner_grad, outer_grad = moe_pass(
        capacity, mixed_t, w_output, layer_input[0], cotangent[0], norm_gain_two, router_t, info_all, cots_all, inner_weight, outer_weight
    )

    def cut(array):
        return padded(array.reshape(blocks, array.shape[0] // blocks, array.shape[1]))

    cots, diagonals, expert_in_grad, expert_out_sums, layer_output = back_pass(
        held, mixed_cot, rel_table, attended_whole, lse, base, far, cut(inner_grad), cut(outer_grad)
    )
    large, input_grad, small, expert_out_grad = tail_pass(
        normed_t, cots, mixed_t, w_query, w_key, w_value, layer_input[0], norm_gain_one, hidden_cot, moe_small, diagonals, expert_out_sums
    )
    extra = [expert_in_grad, expert_out_grad]
    fits = [array.shape[0] % 96 == 0 for array in extra]
    finished = finish_pass(
        large.reshape(4, width, width), small, heads, [array for array, fit in zip(extra, fits) if fit]
    )
    converted = list(finished[7:])
    extra = [converted.pop(0) if fit else array.astype(f32) for array, fit in zip(extra, fits)]
    return (
        layer_output[None],
        input_grad[None],
        finished[4],
        finished[0],
        finished[1],
        finished[2],
        finished[3],
        finished[6],
        finished[5],
        small[8 : 8 + experts].T,
        extra[0][None, : w_expert_in.shape[1]],
        extra[1][None, : w_expert_out.shape[1]],
    )


def solution(mesh):
    placed = (
        P(("expert", "dp"), "ctx", None),
        P(("expert", "dp"), "ctx", None),
        P(),
        P(),
        P(),
        P(),
        P(),
        P(),
        P(),
        P(),
        P("expert", ("ctx", "dp"), None),
        P("expert", ("ctx", "dp"), None),
        P(("expert", "dp"), "ctx"),
        P(("expert", "dp"), "ctx", None),
        P(("expert", "dp"), "ctx", None),
    )
    return jax.shard_map(
        local,
        mesh=mesh,
        in_specs=placed,
        out_specs=(
            P(("expert", "dp"), "ctx", None),
            P(("expert", "dp"), "ctx", None),
            P(),
            P(),
            P(),
            P(),
            P(),
            P(),
            P(),
            P(),
            P("expert", ("ctx", "dp"), None),
            P("expert", ("ctx", "dp"), None),
        ),
        check_vma=False,
    )
```
